32 devices in a mesh: pipe: 2 (over x), dp: 4 (over z), seq: 4 (over y, core).
Axes of the slice: x: 2, y: 2, z: 4, core: 2. Of those that a mesh axis runs over, the one named last changes fastest.
Arguments:
- token_ids: int32 [8, 1024], P('dp'), may hold values from 0 to 50303
- segments: int32 [8, 1024], P('dp'), may hold values from 0 to 2, as said below
- valid: int32 [8, 1024], P('dp'), may hold values from 0 to 1
- attn_qkv: float32 [2, 1024, 3, 1024], P('pipe', 'dp', None, 'seq'), may hold values from -0.1875 to 0.1875
- attn_qkv_first: float32 [2, 1024, 3, 1024], P('pipe', 'dp', None, 'seq'), may hold values from -7.1525574e-07 to 7.1525574e-07
- attn_qkv_second: float32 [2, 1024, 3, 1024], P('pipe', 'dp', None, 'seq'), may hold values from 6.766497e-14 to 2.7014532e-13
- attn_out: float32 [2, 1024, 1024], P('pipe', 'seq', 'dp'), may hold values from -0.75 to 0.75
- attn_out_first: float32 [2, 1024, 1024], P('pipe', 'seq', 'dp'), may hold values from -7.1525574e-07 to 7.1525574e-07
- attn_out_second: float32 [2, 1024, 1024], P('pipe', 'seq', 'dp'), may hold values from 6.766497e-14 to 2.7014532e-13
- mlp_in: float32 [2, 1024, 4096], P('pipe', 'dp', 'seq'), may hold values from -0.1875 to 0.1875
- mlp_in_first: float32 [2, 1024, 4096], P('pipe', 'dp', 'seq'), may hold values from -7.1525574e-07 to 7.1525574e-07
- mlp_in_second: float32 [2, 1024, 4096], P('pipe', 'dp', 'seq'), may hold values from 6.766497e-14 to 2.7014532e-13
- mlp_out: float32 [2, 4096, 1024], P('pipe', 'seq', 'dp'), may hold values from -0.09375 to 0.09375
- mlp_out_first: float32 [2, 4096, 1024], P('pipe', 'seq', 'dp'), may hold values from -7.1525574e-07 to 7.1525574e-07
- mlp_out_second: float32 [2, 4096, 1024], P('pipe', 'seq', 'dp'), may hold values from 6.766497e-14 to 2.7014532e-13
- embed_table: float32 [50304, 1024], P('seq', 'dp')
- embed_table_first: float32 [50304, 1024], P('seq', 'dp'), may hold values from -7.1525574e-07 to 7.1525574e-07
- embed_table_second: float32 [50304, 1024], P('seq', 'dp'), may hold values from 6.766497e-14 to 2.7014532e-13
- position_table: float32 [1024, 1024], P('seq', 'dp'), may hold values from -1.25 to 1.25
- position_table_first: float32 [1024, 1024], P('seq', 'dp'), may hold values from -7.1525574e-07 to 7.1525574e-07
- position_table_second: float32 [1024, 1024], P('seq', 'dp'), may hold values from 6.766497e-14 to 2.7014532e-13
- norm_params: float32 [2, 4, 1024], P(None, None, ('pipe', 'dp', 'seq'))
- norm_params_first: float32 [2, 4, 1024], P(None, None, ('pipe', 'dp', 'seq')), may hold values from -2.3841858e-06 to 2.3841858e-06
- norm_params_second: float32 [2, 4, 1024], P(None, None, ('pipe', 'dp', 'seq')), may hold values from 6.04611e-13 to 2.444172e-12
- final_norm: float32 [2, 1024], P(None, ('pipe', 'dp', 'seq'))
- final_norm_first: float32 [2, 1024], P(None, ('pipe', 'dp', 'seq')), may hold values from -2.3841858e-06 to 2.3841858e-06
- final_norm_second: float32 [2, 1024], P(None, ('pipe', 'dp', 'seq')), may hold values from 6.04611e-13 to 2.444172e-12
Outputs:
- loss_parts: float32 [2], replicated
- penalty_sum: float32 [], replicated
- grad_norm: float32 [], replicated
- attn_qkv_new: float32 [2, 1024, 3, 1024], P('pipe', 'dp', None, 'seq')
- attn_qkv_first_new: float32 [2, 1024, 3, 1024], P('pipe', 'dp', None, 'seq')
- attn_qkv_second_new: float32 [2, 1024, 3, 1024], P('pipe', 'dp', None, 'seq')
- attn_out_new: float32 [2, 1024, 1024], P('pipe', 'seq', 'dp')
- attn_out_first_new: float32 [2, 1024, 1024], P('pipe', 'seq', 'dp')
- attn_out_second_new: float32 [2, 1024, 1024], P('pipe', 'seq', 'dp')
- mlp_in_new: float32 [2, 1024, 4096], P('pipe', 'dp', 'seq')
- mlp_in_first_new: float32 [2, 1024, 4096], P('pipe', 'dp', 'seq')
- mlp_in_second_new: float32 [2, 1024, 4096], P('pipe', 'dp', 'seq')
- mlp_out_new: float32 [2, 4096, 1024], P('pipe', 'seq', 'dp')
- mlp_out_first_new: float32 [2, 4096, 1024], P('pipe', 'seq', 'dp')
- mlp_out_second_new: float32 [2, 4096, 1024], P('pipe', 'seq', 'dp')
- embed_table_new: float32 [50304, 1024], P('seq', 'dp')
- embed_table_first_new: float32 [50304, 1024], P('seq', 'dp')
- embed_table_second_new: float32 [50304, 1024], P('seq', 'dp')
- position_table_new: float32 [1024, 1024], P('seq', 'dp')
- position_table_first_new: float32 [1024, 1024], P('seq', 'dp')
- position_table_second_new: float32 [1024, 1024], P('seq', 'dp')
- norm_params_new: float32 [2, 4, 1024], P(None, None, ('pipe', 'dp', 'seq'))
- norm_params_first_new: float32 [2, 4, 1024], P(None, None, ('pipe', 'dp', 'seq'))
- norm_params_second_new: float32 [2, 4, 1024], P(None, None, ('pipe', 'dp', 'seq'))
- final_norm_new: float32 [2, 1024], P(None, ('pipe', 'dp', 'seq'))
- final_norm_first_new: float32 [2, 1024], P(None, ('pipe', 'dp', 'seq'))
- final_norm_second_new: float32 [2, 1024], P(None, ('pipe', 'dp', 'seq'))
The draws below stay inside these ranges and needn't reach their ends.
Inputs may be any that keep to these rules, and one draw needn't show every extreme that they name: `segments`: within a row document numbers never fall; every row holds documents 0, 1 and 2; document 1 begins at a position from 1 to 64 and document 2 at a position from 960 to 1023.
All inputs are finite; a program needn't handle non-finite values.
Results may differ from the reference program's by a relative error of at most 0.019.
Values may be sent and summed in bfloat16 or wider, within the bound.
No kernel may reach another device: no remote copies, remote signals or barrier semaphores. Data moves between devices by JAX's collectives and lax.ppermute only.
A program may use at most 1.25 GiB of HBM per device.

```python
import math
import jax
import jax.numpy as jnp
import numpy as np
from jax import lax

D = 1024
HEADS = 16
HEAD = 64
FF = 4096
VOCAB = 50304
LEN = 1024
STEP = 10
SEQS = 8
LAYERS = 2


def ramp_rows(noise_draw):
    position = jnp.arange(D, dtype=jnp.float32) / D
    gain_part = (0.5 + position) * (1.0 + noise_draw[..., 0, :])
    bias_part = 2.0 * noise_draw[..., 1, :]
    return jnp.stack([gain_part, bias_part], -2)


def draw_segments(key, part):
    key = jax.random.fold_in(key, 1)
    margin = max(LEN // 16, 1)
    first_key, second_key = jax.random.split(key)
    start_pos = jax.random.randint(first_key, (SEQS, 1), 1, margin + 1)
    finish = jax.random.randint(second_key, (SEQS, 1), LEN - margin, LEN)
    position = jnp.arange(LEN)[None, :]
    return (position >= start_pos).astype(jnp.int32) + (position >= finish).astype(jnp.int32)


def draw_valid(key, part):
    key = jax.random.fold_in(key, 2)
    position = jnp.arange(LEN)[None, :]
    integer_draw = jax.random.randint(key, (SEQS, LEN), 0, 4 * LEN)
    return (integer_draw < LEN + 3 * position).astype(jnp.int32)


def draw_embed_table(key, part):
    key = jax.random.fold_in(key, 3)
    position = jnp.arange(VOCAB, dtype=jnp.float32)[:, None] / VOCAB
    base_draw = jax.random.normal(key, (VOCAB, D), jnp.float32) * (1.0 + 2.0 * position)
    return base_draw / math.sqrt(D)


def draw_norm_params(key, part):
    key = jax.random.fold_in(key, 5)
    noise_draw = 0.1 * jax.random.normal(key, (LAYERS, 2, 2, D), jnp.float32)
    return ramp_rows(noise_draw).reshape(LAYERS, 4, D)


def draw_final_norm(key, part):
    key = jax.random.fold_in(key, 7)
    noise_draw = 0.1 * jax.random.normal(key, (2, D), jnp.float32)
    return ramp_rows(noise_draw)


def place_ends(result, stream_key, smallest, top_value):
    place = [jax.random.randint(jax.random.fold_in(stream_key, axis), (), 0, length) for axis, length in enumerate(result.shape)]
    widest = result.shape.index(max(result.shape))
    neighbour = place[:widest] + [(place[widest] + 1) % result.shape[widest]] + place[widest + 1:]
    return result.at[tuple(place)].set(smallest).at[tuple(neighbour)].set(top_value)


def levels(own_key, extent, shards, smallest, top_value):
    def one(dim, blocks):
        steps = jax.random.uniform(jax.random.fold_in(jax.random.fold_in(own_key, 6), dim), (blocks,), jnp.float32, smallest / len(shards), top_value / len(shards))
        return jnp.repeat(jnp.exp(steps), extent[dim] // blocks).reshape((-1,) + (1,) * (len(extent) - dim - 1))

    level = one(*shards[0])
    for cut in shards[1:]:
        level = level * one(*cut)
    return level


def rank_bounds(number_of, skew):
    loads = [(1 << 20) // math.isqrt(grade ** skew) + 1 for grade in range(1, number_of + 1)]
    width = 1 + sum(loads) // (1 << 30)
    return np.cumsum(np.array([max(1, weight // width) for weight in loads]))


def skewed_ids(own_key, extent, count, skew):
    listing = rank_bounds(count, skew)
    pick = jax.random.randint(jax.random.fold_in(own_key, 1), extent, 0, int(listing[count - 1]))
    grade = jnp.searchsorted(jnp.asarray(listing, jnp.int32), pick, side="right")
    return jax.random.permutation(jax.random.fold_in(own_key, 2), count)[grade].astype(jnp.int32)


def scatter_about(stream_key, dims, deviation, most, pieces=(), held_as=jnp.bfloat16):
    array = deviation * jax.random.normal(stream_key, dims, jnp.float32)
    if pieces:
        array = array * levels(stream_key, dims, pieces, -0.22, 0.18)
    return jnp.clip(array, -most, most).astype(held_as)


def setup_inputs(seed: int = 0) -> dict:
    key_list = jax.random.split(jax.random.key(seed), 28)
    return {
        "token_ids": place_ends(skewed_ids(key_list[0], (SEQS, LEN), VOCAB, 2), jax.random.fold_in(key_list[0], 3), 0, VOCAB - 1).astype(jnp.int32),
        "segments": draw_segments(jax.random.fold_in(key_list[27], 71), 0),
        "valid": draw_valid(jax.random.fold_in(key_list[27], 71), 0),
        "attn_qkv": scatter_about(key_list[3], (LAYERS, D, 3, D), D ** -0.5, 0.1875, ((0, 2), (1, 4), (3, 4)), jnp.float32),
        "attn_qkv_first": scatter_about(key_list[4], (LAYERS, D, 3, D), (0.111 * (0.01 / (12 * D * D * LAYERS + VOCAB * D + LEN * D + 4 * D * LAYERS + 2 * D) ** 0.5)), 7.152557373046875e-07, ((0, 2), (1, 4), (3, 4)), jnp.float32),
        "attn_qkv_second": jnp.clip(jnp.exp(math.log(2.7014531562251365e-13) - 1.3843914 * jax.random.uniform(key_list[5], (LAYERS, D, 3, D), jnp.float32) ** levels(key_list[5], (LAYERS, D, 3, D), ((0, 2), (1, 4), (3, 4)), -0.2, 0.2)), 6.766496949339382e-14, 2.7014531562251365e-13),
        "attn_out": scatter_about(key_list[6], (LAYERS, D, D), (D // 16) ** -0.5, 0.75, ((0, 2), (1, 4), (2, 4)), jnp.float32),
        "attn_out_first": scatter_about(key_list[7], (LAYERS, D, D), (0.111 * (0.01 / (12 * D * D * LAYERS + VOCAB * D + LEN * D + 4 * D * LAYERS + 2 * D) ** 0.5)), 7.152557373046875e-07, ((0, 2), (1, 4), (2, 4)), jnp.float32),
        "attn_out_second": jnp.clip(jnp.exp(math.log(2.7014531562251365e-13) - 1.3843914 * jax.random.uniform(key_list[8], (LAYERS, D, D), jnp.float32) ** levels(key_list[8], (LAYERS, D, D), ((0, 2), (1, 4), (2, 4)), -0.2, 0.2)), 6.766496949339382e-14, 2.7014531562251365e-13),
        "mlp_in": scatter_about(key_list[9], (LAYERS, D, FF), D ** -0.5, 0.1875, ((0, 2), (1, 4), (2, 4)), jnp.float32),
        "mlp_in_first": scatter_about(key_list[10], (LAYERS, D, FF), (0.111 * (0.01 / (12 * D * D * LAYERS + VOCAB * D + LEN * D + 4 * D * LAYERS + 2 * D) ** 0.5)), 7.152557373046875e-07, ((0, 2), (1, 4), (2, 4)), jnp.float32),
        "mlp_in_second": jnp.clip(jnp.exp(math.log(2.7014531562251365e-13) - 1.3843914 * jax.random.uniform(key_list[11], (LAYERS, D, FF), jnp.float32) ** levels(key_list[11], (LAYERS, D, FF), ((0, 2), (1, 4), (2, 4)), -0.2, 0.2)), 6.766496949339382e-14, 2.7014531562251365e-13),
        "mlp_out": scatter_about(key_list[12], (LAYERS, FF, D), FF ** -0.5, 0.09375, ((0, 2), (1, 4), (2, 4)), jnp.float32),
        "mlp_out_first": scatter_about(key_list[13], (LAYERS, FF, D), (0.111 * (0.01 / (12 * D * D * LAYERS + VOCAB * D + LEN * D + 4 * D * LAYERS + 2 * D) ** 0.5)), 7.152557373046875e-07, ((0, 2), (1, 4), (2, 4)), jnp.float32),
        "mlp_out_second": jnp.clip(jnp.exp(math.log(2.7014531562251365e-13) - 1.3843914 * jax.random.uniform(key_list[14], (LAYERS, FF, D), jnp.float32) ** levels(key_list[14], (LAYERS, FF, D), ((0, 2), (1, 4), (2, 4)), -0.2, 0.2)), 6.766496949339382e-14, 2.7014531562251365e-13),
        "embed_table": draw_embed_table(jax.random.fold_in(key_list[27], 71), 0),
        "embed_table_first": scatter_about(key_list[16], (VOCAB, D), (0.111 * (0.01 / (12 * D * D * LAYERS + VOCAB * D + LEN * D + 4 * D * LAYERS + 2 * D) ** 0.5)), 7.152557373046875e-07, ((0, 4), (1, 4)), jnp.float32),
        "embed_table_second": jnp.clip(jnp.exp(math.log(2.7014531562251365e-13) - 1.3843914 * jax.random.uniform(key_list[17], (VOCAB, D), jnp.float32) ** levels(key_list[17], (VOCAB, D), ((0, 4), (1, 4)), -0.2, 0.2)), 6.766496949339382e-14, 2.7014531562251365e-13),
        "position_table": scatter_about(key_list[18], (LEN, D), 0.2, 1.25, ((0, 4), (1, 4)), jnp.float32),
        "position_table_first": scatter_about(key_list[19], (LEN, D), (0.111 * (0.01 / (12 * D * D * LAYERS + VOCAB * D + LEN * D + 4 * D * LAYERS + 2 * D) ** 0.5)), 7.152557373046875e-07, ((0, 4), (1, 4)), jnp.float32),
        "position_table_second": jnp.clip(jnp.exp(math.log(2.7014531562251365e-13) - 1.3843914 * jax.random.uniform(key_list[20], (LEN, D), jnp.float32) ** levels(key_list[20], (LEN, D), ((0, 4), (1, 4)), -0.2, 0.2)), 6.766496949339382e-14, 2.7014531562251365e-13),
        "norm_params": draw_norm_params(jax.random.fold_in(key_list[27], 71), 0),
        "norm_params_first": scatter_about(key_list[22], (LAYERS, 4, D), (0.333 * (0.01 / (12 * D * D * LAYERS + VOCAB * D + LEN * D + 4 * D * LAYERS + 2 * D) ** 0.5)), 2.384185791015625e-06, ((2, 32),), jnp.float32),
        "norm_params_second": jnp.clip(jnp.exp(math.log(2.444172034904435e-12) - 1.3968765 * jax.random.uniform(key_list[23], (LAYERS, 4, D), jnp.float32) ** levels(key_list[23], (LAYERS, 4, D), ((2, 32),), -0.2, 0.2)), 6.046109793378385e-13, 2.444172034904435e-12),
        "final_norm": draw_final_norm(jax.random.fold_in(key_list[27], 71), 0),
        "final_norm_first": scatter_about(key_list[25], (2, D), (0.333 * (0.01 / (12 * D * D * LAYERS + VOCAB * D + LEN * D + 4 * D * LAYERS + 2 * D) ** 0.5)), 2.384185791015625e-06, ((1, 32),), jnp.float32),
        "final_norm_second": jnp.clip(jnp.exp(math.log(2.444172034904435e-12) - 1.3968765 * jax.random.uniform(key_list[26], (2, D), jnp.float32) ** levels(key_list[26], (2, D), ((1, 32),), -0.2, 0.2)), 6.046109793378385e-13, 2.444172034904435e-12),
    }


EPS_NORM = 1e-05
ZLOSS = 0.001
CLIP = 0.01
BETA_ONE = 0.9
BETA_TWO = 0.95
EPS_ADAM = 1e-08
RATES = (0.03, 0.1, 0.03, 0.015, 0.05, 0.15, 0.7, 0.7)
DECAYS = (0.1, 0.1, 0.1, 0.1, 0.1, 0.0, 0.0, 0.0)
HIGHEST_MODE = lax.Precision.HIGHEST

@jax.custom_vjp
def low(v):
    return lax.optimization_barrier(v.astype(jnp.bfloat16)).astype(jnp.float32)

@jax.custom_vjp
def low_back(v):
    return v

def low_keep(v):
    return (low(v), None)

def low_pass(kept, grad):
    return (grad,)

def back_keep(v):
    return (v, None)

def back_low(kept, grad):
    return (low(grad),)
low.defvjp(low_keep, low_pass)
low_back.defvjp(back_keep, back_low)

def norm_rows(values, gain, bias):
    center = values - lax.optimization_barrier(jnp.mean(values, -1, keepdims=True))
    spread_sq = lax.optimization_barrier(jnp.mean(center * center, -1, keepdims=True))
    return center * lax.rsqrt(spread_sq + EPS_NORM) * gain + bias

def attention_branch(normed, w_qkv, w_out, allowed):
    length = normed.shape[0]
    packed = low(low_back(jnp.einsum('td,dcf->tcf', normed, w_qkv, precision=HIGHEST_MODE)))
    queries = packed[:, 0].reshape(length, HEADS, HEAD)
    key_rows = packed[:, 1].reshape(length, HEADS, HEAD)
    value_rows = packed[:, 2].reshape(length, HEADS, HEAD)
    scores = low_back(jnp.einsum('qhe,khe->hqk', queries, key_rows, precision=HIGHEST_MODE) * HEAD ** (-0.5))
    scores = jnp.where(allowed[None], scores, -1e+30)
    row_top = lax.optimization_barrier(jnp.max(scores, -1, keepdims=True))
    exponent = jnp.exp(scores - row_top)
    probabilities = low(exponent / lax.optimization_barrier(jnp.sum(exponent, -1, keepdims=True)))
    mixed_rows = jnp.einsum('hqk,khe->qhe', probabilities, value_rows, precision=HIGHEST_MODE)
    mixed_rows = low(low_back(mixed_rows.reshape(length, D)))
    return low_back(jnp.dot(mixed_rows, w_out, precision=HIGHEST_MODE))

def sequence_loss(row_ids, row_segments, row_weight, tables):
    w_qkv, w_out, w_fc, w_proj, vocab_table, positions, gain_rows, final_rows = tables
    position = jnp.arange(row_ids.shape[0])
    allowed = (position[:, None] >= position[None, :]) & (row_segments[:, None] == row_segments[None, :])
    residual = low_back(jnp.take(vocab_table, row_ids, axis=0)) + positions
    for layer in range(LAYERS):
        normed = low(norm_rows(residual, gain_rows[layer, 0], gain_rows[layer, 1]))
        residual = residual + attention_branch(normed, w_qkv[layer], w_out[layer], allowed)
        normed = low(norm_rows(residual, gain_rows[layer, 2], gain_rows[layer, 3]))
        hidden = low_back(jnp.dot(normed, w_fc[layer], precision=HIGHEST_MODE))
        active = low(jax.nn.gelu(hidden, approximate=True))
        residual = residual + low_back(jnp.dot(active, w_proj[layer], precision=HIGHEST_MODE))
    final_normed = low(norm_rows(residual, final_rows[0], final_rows[1]))
    logits = low_back(jnp.dot(final_normed, vocab_table.T, precision=HIGHEST_MODE))
    row_top = lax.optimization_barrier(jnp.max(logits, -1, keepdims=True))
    log_total = row_top[:, 0] + jnp.log(lax.optimization_barrier(jnp.sum(jnp.exp(logits - row_top), -1)))
    targets = jnp.roll(row_ids, -1)
    picked = jnp.take_along_axis(logits, targets[:, None], 1)[:, 0]
    penalty = jnp.sum(row_weight * ZLOSS * log_total * log_total)
    return (jnp.sum(row_weight * (log_total - picked)) + penalty, penalty)

def adamw_update(master, first, second, gradient, rate, decay):
    first_new = BETA_ONE * first + (1.0 - BETA_ONE) * gradient
    second_new = BETA_TWO * second + (1.0 - BETA_TWO) * gradient * gradient
    ratio = first_new / (1.0 - BETA_ONE ** STEP) / (jnp.sqrt(second_new / (1.0 - BETA_TWO ** STEP)) + EPS_ADAM)
    return (master - rate * (ratio + decay * master), first_new, second_new)

def reference(token_ids, segments, valid, attn_qkv, attn_qkv_first, attn_qkv_second, attn_out, attn_out_first, attn_out_second, mlp_in, mlp_in_first, mlp_in_second, mlp_out, mlp_out_first, mlp_out_second, embed_table, embed_table_first, embed_table_second, position_table, position_table_first, position_table_second, norm_params, norm_params_first, norm_params_second, final_norm, final_norm_first, final_norm_second):
    position = jnp.arange(LEN)
    token_weight = valid.astype(jnp.float32) * (position < LEN - 1).astype(jnp.float32)[None, :]
    token_count = jnp.sum(token_weight)
    masters = (attn_qkv, attn_out, mlp_in, mlp_out, embed_table, position_table, norm_params, final_norm)
    moments = ((attn_qkv_first, attn_qkv_second), (attn_out_first, attn_out_second), (mlp_in_first, mlp_in_second), (mlp_out_first, mlp_out_second), (embed_table_first, embed_table_second), (position_table_first, position_table_second), (norm_params_first, norm_params_second), (final_norm_first, final_norm_second))

    def total(w_qkv, w_out, w_fc, w_proj, vocab_table, positions, gain_rows, final_rows):
        tables = (low(w_qkv), low(w_out), low(w_fc), low(w_proj), low(vocab_table), low(positions), gain_rows, final_rows)

        def add_sequence(carry, row_items):
            loss_part, penalty_part = sequence_loss(row_items[0], row_items[1], row_items[2], tables)
            return ((carry[0] + loss_part, carry[1] + penalty_part), None)
        zero_sum = jnp.zeros((), jnp.float32)
        sums = lax.scan(jax.checkpoint(add_sequence), (zero_sum, zero_sum), (token_ids, segments, token_weight))[0]
        return (sums[0], sums[1])
    loss_sum, pull_back, penalty_sum = jax.vjp(total, *masters, has_aux=True)
    gradients = pull_back(jnp.ones((), loss_sum.dtype))
    gradients = tuple((gradient / token_count for gradient in gradients))
    squares = jnp.zeros((), jnp.float32)
    for gradient in gradients:
        squares = squares + jnp.sum(gradient * gradient)
    grad_norm = jnp.sqrt(squares)
    clip_factor = jnp.minimum(1.0, CLIP / (grad_norm + 1e-06))
    results = []
    for index in range(8):
        results.append(adamw_update(masters[index], moments[index][0], moments[index][1], gradients[index] * clip_factor, RATES[index], DECAYS[index]))
    loss_parts = jnp.stack([loss_sum, token_count])
    return (loss_parts, penalty_sum, grad_norm, results[0][0], results[0][1], results[0][2], results[1][0], results[1][1], results[1][2], results[2][0], results[2][1], results[2][2], results[3][0], results[3][1], results[3][2], results[4][0], results[4][1], results[4][2], results[5][0], results[5][1], results[5][2], results[6][0], results[6][1], results[6][2], results[7][0], results[7][1], results[7][2])
```

```python
import jax
import jax.numpy as jnp
from jax import lax
from jax.sharding import PartitionSpec as P

HEAD = 64
STEP = 10


EPS_NORM = 1e-05
ZLOSS = 0.001
CLIP = 0.01
BETA_ONE = 0.9
BETA_TWO = 0.95
EPS_ADAM = 1e-08
RATES = (0.03, 0.1, 0.03, 0.015, 0.05, 0.15, 0.7, 0.7)
DECAYS = (0.1, 0.1, 0.1, 0.1, 0.1, 0.0, 0.0, 0.0)
F32 = jnp.float32
BF16 = jnp.bfloat16


def swap(block, axis, mask):
    route = [(i, i ^ mask) for i in range(lax.axis_size(axis))]
    return lax.ppermute(block, axis, route)


def masks_down(size):
    found = []
    mask = size // 2
    while mask >= 1:
        found.append(mask)
        mask //= 2
    return found


def reverse_bits(value, size):
    result = 0
    mask = 1
    while mask < size:
        result = result * 2 + (value & mask) // mask
        mask *= 2
    return result


def spread(block):
    for mask in masks_down(lax.axis_size("seq")):
        block = jnp.concatenate([block, swap(block, "seq", mask)], 0)
    return block


def collect(block):
    for mask in reversed(masks_down(lax.axis_size("seq"))):
        half = block.shape[0] // 2
        sent = swap(block[half:].astype(BF16), "seq", mask)
        block = block[:half].astype(F32) + sent.astype(F32)
    return block


def sum_everywhere(block, axes=("seq", "dp", "pipe")):
    for axis in axes:
        for mask in reversed(masks_down(lax.axis_size(axis))):
            block = block + swap(block, axis, mask)
    return block


def norm_rows(values, gain, bias):
    center = values - jnp.mean(values, -1, keepdims=True)
    spread_sq = jnp.mean(center * center, -1, keepdims=True)
    return center * lax.rsqrt(spread_sq + EPS_NORM) * gain + bias


def gelu_tanh(values):
    return jax.nn.gelu(values, approximate=True)


def split_heads(packed):
    length, columns = packed.shape
    third = columns // 3
    heads = third // HEAD
    return tuple(
        packed[:, k * third : (k + 1) * third].reshape(length, heads, HEAD) for k in range(3)
    )


def attend_forward(packed, allowed):
    queries, key_rows, value_rows = split_heads(packed)
    length, heads, _ = queries.shape
    scores = jnp.einsum(
        "qhe,khe->hqk", queries, key_rows, preferred_element_type=F32
    ) * HEAD ** (-0.5)
    scores = jnp.where(allowed[None], scores, -1e30)
    row_top = jnp.max(scores, -1, keepdims=True)
    exponent = jnp.exp(scores - row_top)
    probabilities = exponent / jnp.sum(exponent, -1, keepdims=True)
    mixed_rows = jnp.einsum(
        "hqk,khe->qhe", probabilities.astype(BF16), value_rows, preferred_element_type=F32
    )
    return (probabilities, mixed_rows.reshape(length, heads * HEAD).astype(BF16))


def attend_backward(packed, probabilities, grad_mixed):
    queries, key_rows, value_rows = split_heads(packed)
    length, heads, _ = queries.shape
    columns = heads * HEAD
    grad_rows = grad_mixed.reshape(length, heads, HEAD)
    grad_values = jnp.einsum(
        "hqk,qhe->khe", probabilities.astype(BF16), grad_rows, preferred_element_type=F32
    )
    grad_soft = jnp.einsum("qhe,khe->hqk", grad_rows, value_rows, preferred_element_type=F32)
    grad_scores = probabilities * (
        grad_soft - jnp.sum(probabilities * grad_soft, -1, keepdims=True)
    )
    grad_scores = grad_scores.astype(BF16)
    factor = HEAD ** (-0.5)
    grad_queries = (
        jnp.einsum("hqk,khe->qhe", grad_scores, key_rows, preferred_element_type=F32) * factor
    )
    grad_keys = (
        jnp.einsum("hqk,qhe->khe", grad_scores, queries, preferred_element_type=F32) * factor
    )
    return jnp.concatenate(
        [
            grad_queries.reshape(length, columns),
            grad_keys.reshape(length, columns),
            grad_values.reshape(length, columns),
        ],
        1,
    ).astype(BF16)


def forward_layer(residual, matrices, gain_rows, allowed):
    w_qkv, w_out, w_fc, w_proj = matrices
    normed = norm_rows(residual, gain_rows[0], gain_rows[1])
    first_full = spread(normed.astype(BF16))
    packed = jnp.dot(first_full, w_qkv, preferred_element_type=F32).astype(BF16)
    probabilities, mixed_rows = attend_forward(packed, allowed)
    branch = jnp.einsum("tc,dc->td", mixed_rows, w_out, preferred_element_type=F32)
    middle = residual + collect(branch)
    second = norm_rows(middle, gain_rows[2], gain_rows[3])
    second_full = spread(second.astype(BF16))
    hidden = jnp.dot(second_full, w_fc, preferred_element_type=F32)
    active = gelu_tanh(hidden).astype(BF16)
    branch = jnp.einsum("tf,df->td", active, w_proj, preferred_element_type=F32)
    output = middle + collect(branch)
    saved = (
        residual,
        first_full,
        packed,
        probabilities,
        mixed_rows,
        middle,
        second_full,
        hidden,
        active,
    )
    return output, saved


def backward_layer(saved, grad_out, matrices, gain_rows):
    w_qkv, w_out, w_fc, w_proj = matrices
    residual, first_full, packed, probabilities, mixed_rows, middle, second_full, hidden, active = (
        saved
    )
    grad_z = spread(grad_out.astype(BF16))
    grad_active = jnp.dot(grad_z, w_proj, preferred_element_type=F32)
    _, gelu_pull = jax.vjp(gelu_tanh, hidden)
    grad_hidden = gelu_pull(grad_active)[0].astype(BF16)
    grad_second = collect(jnp.einsum("tf,df->td", grad_hidden, w_fc, preferred_element_type=F32))
    grad_proj = jnp.einsum("td,tf->df", grad_z, active, preferred_element_type=F32).astype(BF16)
    grad_fc = jnp.einsum(
        "td,tf->df", second_full, grad_hidden, preferred_element_type=F32
    ).astype(BF16)
    _, norm_pull = jax.vjp(norm_rows, middle, gain_rows[2], gain_rows[3])
    grad_middle, grad_gain_two, grad_bias_two = norm_pull(grad_second)
    grad_middle = grad_middle + grad_out
    grad_y = spread(grad_middle.astype(BF16))
    grad_mixed = jnp.dot(grad_y, w_out, preferred_element_type=F32).astype(BF16)
    grad_packed = attend_backward(packed, probabilities, grad_mixed)
    grad_first = collect(jnp.einsum("tc,dc->td", grad_packed, w_qkv, preferred_element_type=F32))
    grad_out_w = jnp.einsum("td,tc->dc", grad_y, mixed_rows, preferred_element_type=F32)
    grad_qkv = jnp.einsum("td,tc->dc", first_full, grad_packed, preferred_element_type=F32)
    grad_attn = jnp.concatenate([grad_qkv, grad_out_w], 1).astype(BF16)
    _, norm_pull = jax.vjp(norm_rows, residual, gain_rows[0], gain_rows[1])
    grad_residual, grad_gain_one, grad_bias_one = norm_pull(grad_first)
    grad_gain_rows = jnp.stack([grad_gain_one, grad_bias_one, grad_gain_two, grad_bias_two])
    return (grad_residual + grad_middle, (grad_attn, grad_fc, grad_proj), grad_gain_rows)


def exchange_blocks(blocks, axis):
    return [blocks[0]] + [swap(blocks[m], axis, m) for m in range(1, len(blocks))]


def place_columns(blocks, index):
    width = blocks[0].shape[1]
    whole = jnp.zeros((blocks[0].shape[0], width * len(blocks)), blocks[0].dtype)
    for m, block in enumerate(blocks):
        whole = lax.dynamic_update_slice_in_dim(whole, block, (index ^ m) * width, 1)
    return whole


def take_columns(whole, index, count):
    width = whole.shape[1] // count
    return [
        lax.dynamic_slice_in_dim(whole, (index ^ m) * width, width, 1) for m in range(count)
    ]


def head_block(rows, table, bias):
    logits = jnp.einsum("td,vd->tv", rows, table, preferred_element_type=F32) + bias[None, :]
    row_top = jnp.max(logits, 1)
    exponent = jnp.exp(logits - row_top[:, None])
    row_sum = jnp.sum(exponent, 1)
    low = exponent.astype(BF16)
    mixed = jnp.dot(low, table, preferred_element_type=F32)
    return low, mixed, row_top, row_sum


def head_table_gradient(low, scale, weight, target, rows):
    columns = jnp.arange(low.shape[1])
    gradient = scale[:, None] * low.astype(F32) - jnp.where(
        columns[None, :] == target[:, None], weight[:, None], 0.0
    )
    return jnp.einsum("tv,td->vd", gradient.astype(BF16), rows, preferred_element_type=F32)


def merge_stats(stats):
    top, total = stats
    for axis, place in (("seq", 1), ("dp", 0)):
        size = lax.axis_size(axis)
        for mask in reversed(masks_down(size)):
            shift = reverse_bits(mask, size) if axis == "seq" else mask
            order = jnp.array([k ^ shift for k in range(size)])
            pair = jnp.take(swap(jnp.stack([top, total]), axis, mask), order, axis=place + 1)
            top_new = jnp.maximum(top, pair[0])
            total = total * jnp.exp(top - top_new) + pair[1] * jnp.exp(pair[0] - top_new)
            top = top_new
    return top + jnp.log(total)


def adamw_update(master, first, second, gradient, rate, decay):
    first_new = BETA_ONE * first + (1.0 - BETA_ONE) * gradient
    second_new = BETA_TWO * second + (1.0 - BETA_TWO) * gradient * gradient
    ratio = (
        first_new
        / (1.0 - BETA_ONE**STEP)
        / (jnp.sqrt(second_new / (1.0 - BETA_TWO**STEP)) + EPS_ADAM)
    )
    return (master - rate * (ratio + decay * master), first_new, second_new)


def per_device(
    token_ids,
    segments,
    valid,
    attn_qkv,
    attn_qkv_first,
    attn_qkv_second,
    attn_out,
    attn_out_first,
    attn_out_second,
    mlp_in,
    mlp_in_first,
    mlp_in_second,
    mlp_out,
    mlp_out_first,
    mlp_out_second,
    embed_table,
    embed_table_first,
    embed_table_second,
    position_table,
    position_table_first,
    position_table_second,
    norm_params,
    norm_params_first,
    norm_params_second,
    final_norm,
    final_norm_first,
    final_norm_second,
):
    section, replica, lane = lax.axis_index("pipe"), lax.axis_index("dp"), lax.axis_index("seq")
    sections, replicas, lanes = (lax.axis_size(name) for name in ("pipe", "dp", "seq"))
    length = token_ids.shape[1]
    assert sections == 2 and token_ids.shape[0] == sections and attn_qkv.shape[0] == 1
    shard_rows = length // lanes
    slice_rows, slice_columns = embed_table.shape
    width = slice_columns * replicas
    part_rows = -(-slice_rows // (replicas * 128)) * 128
    half_rows = part_rows // 2
    assert part_rows * (replicas - 1) < slice_rows
    lane_order = [reverse_bits(k, lanes) for k in range(lanes)]
    lane_blocks = lane ^ jnp.array(lane_order)

    norm_mine = jnp.concatenate([norm_params.reshape(-1, norm_params.shape[2]), final_norm], 0)
    norm_columns = norm_mine.shape[1]
    norm_all = lax.all_gather(norm_mine, ("pipe", "dp", "seq"), axis=1, tiled=True)
    gain_stack = norm_all[:-2].reshape(norm_params.shape[0], 4, width)
    final_rows = norm_all[-2:]

    own_ids = lax.dynamic_index_in_dim(token_ids, section, 0, keepdims=False)
    own_valid = lax.dynamic_index_in_dim(valid, section, 0, keepdims=False)
    row_segments = lax.dynamic_index_in_dim(segments, section, 0, keepdims=False)
    coded = own_ids * 2 + own_valid
    coded_all = jnp.stack([coded] + [swap(coded, "dp", m) for m in range(1, replicas)])
    ids_all = coded_all // 2
    position = jnp.arange(length)
    weight_all = jnp.where(position < length - 1, coded_all % 2, 0).astype(F32)
    targets_all = jnp.roll(ids_all, -1, axis=1)

    def by_lane(values):
        return jnp.take(values.reshape(-1, lanes, shard_rows), lane_blocks, axis=1)

    ids_lane, weight_lane, targets_lane = by_lane(ids_all), by_lane(weight_all), by_lane(targets_all)

    def two_layers(matrix):
        low = matrix.astype(BF16)
        half = low.shape[0] // 2
        kept = lax.dynamic_slice_in_dim(low, section * half, half, 0)
        sent = lax.dynamic_slice_in_dim(low, (1 - section) * half, half, 0)
        other = swap(sent, "pipe", 1)
        return [jnp.where(section == layer, kept, other) for layer in range(2)]

    qkv_columns = attn_qkv.shape[2] * attn_qkv.shape[3]
    attn_shard = jnp.concatenate(
        [attn_qkv[0].reshape(-1, qkv_columns), attn_out[0].T], 1
    )
    pieces = [two_layers(attn_shard), two_layers(mlp_in[0]), two_layers(mlp_out[0].T)]

    def layer_matrices(layer):
        attn, fc, proj = (
            lax.all_gather(piece[layer], ("dp", "pipe"), axis=0, tiled=True) for piece in pieces
        )
        return attn[:, :qkv_columns], attn[:, qkv_columns:], fc, proj

    matrices = [layer_matrices(0), layer_matrices(1)]

    vocab_start = lane * slice_rows
    wanted = jnp.transpose(ids_lane, (1, 0, 2)).reshape(-1) - vocab_start
    inside = (wanted >= 0) & (wanted < slice_rows)
    picked = jnp.take(embed_table, jnp.clip(wanted, 0, slice_rows - 1), axis=0)
    picked = jnp.where(inside[:, None], picked, 0.0).astype(BF16)
    picked = collect(picked).astype(BF16).reshape(replicas, shard_rows, slice_columns)
    embed_rows = place_columns(exchange_blocks(list(picked), "dp"), replica)
    position_low = position_table.astype(BF16)
    position_rows = place_columns(
        exchange_blocks([position_low] * replicas, "dp"), replica
    )
    start_rows = embed_rows.astype(F32) + position_rows.astype(F32)
    next_first = lax.ppermute(embed_rows[:1], "seq", [(k, k - 1) for k in range(1, lanes)])
    target_rows = jnp.concatenate([embed_rows[1:], next_first], 0).astype(F32)

    table_low = jnp.pad(
        embed_table.astype(BF16), ((0, part_rows * replicas - slice_rows), (0, 0))
    )
    table_parts = [
        lax.dynamic_slice_in_dim(table_low, (replica ^ m) * part_rows, part_rows, 0)
        for m in range(replicas)
    ]
    table = place_columns(exchange_blocks(table_parts, "dp"), replica)
    part_start = vocab_start + replica * part_rows
    part_count = jnp.minimum(part_rows, slice_rows - replica * part_rows)
    table_bias = jnp.where(jnp.arange(part_rows) < part_count, 0.0, -1e30).astype(F32)

    row_place = (lane_blocks[:, None] * shard_rows + jnp.arange(shard_rows)[None, :]).reshape(-1)
    row_document = jnp.take(row_segments.reshape(lanes, shard_rows), lane_blocks, axis=0).reshape(-1)
    allowed = (row_place[:, None] >= row_place[None, :]) & (
        row_document[:, None] == row_document[None, :]
    )
    rows = start_rows
    saved = []
    for layer in range(2):
        rows, kept = forward_layer(rows, matrices[layer], gain_stack[layer], allowed)
        saved.append(kept)
    final_value, final_pull = jax.vjp(norm_rows, rows, final_rows[0], final_rows[1])
    final_low = final_value.astype(BF16)

    full = [spread(block) for block in exchange_blocks([final_low] * replicas, "dp")]
    heads = [head_block(block, table, table_bias) for block in full]
    stat_shape = (replicas, lanes, shard_rows)
    row_top = jnp.stack([head[2] for head in heads]).reshape(stat_shape)
    row_sum = jnp.stack([head[3] for head in heads]).reshape(stat_shape)
    log_total = merge_stats((row_top, row_sum))
    scale = weight_lane * (1.0 + 2.0 * ZLOSS * log_total) * jnp.exp(row_top - log_total)
    own_weight, own_log = weight_lane[0, 0], log_total[0, 0]
    target_logit = jnp.sum(final_low.astype(F32) * target_rows, 1)
    own_penalty = own_weight * ZLOSS * own_log * own_log
    own_loss = own_weight * (own_log - target_logit) + own_penalty

    scale_flat = scale.reshape(replicas, length)
    head_parts = [
        collect(scale_flat[m][:, None] * heads[m][1]).astype(BF16) for m in range(replicas)
    ]
    head_parts = exchange_blocks(head_parts, "dp")
    grad_final_rows = sum(part.astype(F32) for part in head_parts)
    grad_final_rows = grad_final_rows - own_weight[:, None] * target_rows
    gradient, final_gain_part, final_bias_part = final_pull(grad_final_rows)
    grad_final = jnp.stack([final_gain_part, final_bias_part])

    target_part = targets_lane.reshape(replicas, length) - part_start
    weight_flat = weight_lane.reshape(replicas, length)
    table_gradient = sum(
        head_table_gradient(
            heads[m][0], scale_flat[m], weight_flat[m], target_part[m], full[m]
        )
        for m in range(replicas)
    ).astype(BF16)
    half_kept = lax.dynamic_slice_in_dim(table_gradient, section * half_rows, half_rows, 0)
    half_sent = lax.dynamic_slice_in_dim(table_gradient, (1 - section) * half_rows, half_rows, 0)
    half_sum = (
        half_kept.astype(F32) + swap(half_sent, "pipe", 1).astype(F32)
    ).astype(BF16)
    half_back = jnp.stack(
        exchange_blocks(take_columns(half_sum, replica, replicas), "dp")
    )
    half_other = swap(half_back, "pipe", 1)
    grad_table = jnp.zeros((replicas, 2, half_rows, slice_columns), BF16)
    for m in range(replicas):
        for half, block in ((section, half_back[m]), (1 - section, half_other[m])):
            grad_table = lax.dynamic_update_slice(
                grad_table, block[None, None], (replica ^ m, half, 0, 0)
            )
    grad_table = grad_table.reshape(-1, slice_columns)[:slice_rows].astype(F32)

    scattered = [None, None]
    grad_gains = [None, None]
    for layer in (1, 0):
        gradient, mat_parts, grad_gains[layer] = backward_layer(
            saved[layer], gradient, matrices[layer], gain_stack[layer]
        )
        scattered[layer] = jnp.concatenate(
            [
                lax.psum_scatter(part, ("dp", "pipe"), scatter_dimension=0, tiled=True)
                for part in mat_parts
            ],
            1,
        )
    matrix_kept = jnp.where(section == 0, scattered[0], scattered[1])
    matrix_sent = jnp.where(section == 0, scattered[1], scattered[0])
    matrix_other = swap(matrix_sent, "pipe", 1)
    matrix_grad = jnp.where(
        section == 0,
        jnp.concatenate([matrix_kept, matrix_other], 0),
        jnp.concatenate([matrix_other, matrix_kept], 0),
    ).astype(F32)
    attn_columns = attn_shard.shape[1]
    fc_columns = mlp_in.shape[2]
    qkv_grad = matrix_grad[:, :qkv_columns].reshape(attn_qkv.shape)
    out_grad = matrix_grad[:, qkv_columns:attn_columns].T[None]
    fc_grad = matrix_grad[:, attn_columns : attn_columns + fc_columns][None]
    proj_grad = matrix_grad[:, attn_columns + fc_columns :].T[None]

    back = exchange_blocks(take_columns(gradient.astype(BF16), replica, replicas), "dp")
    back = jnp.concatenate(back, 0)
    back_other = swap(back, "pipe", 1)
    back_both = jnp.where(
        section == 0,
        jnp.concatenate([back, back_other], 0),
        jnp.concatenate([back_other, back], 0),
    )
    position_grad = jnp.sum(
        back_both.astype(F32).reshape(-1, shard_rows, slice_columns), 0
    )
    back_rows = spread(back_both)
    coded_other = swap(coded_all, "pipe", 1)
    ids_both = jnp.where(
        section == 0,
        jnp.concatenate([ids_all, coded_other // 2], 0),
        jnp.concatenate([coded_other // 2, ids_all], 0),
    )
    back_wanted = jnp.transpose(by_lane(ids_both), (1, 0, 2)).reshape(-1) - vocab_start
    back_inside = (back_wanted >= 0) & (back_wanted < slice_rows)
    table_grad = grad_table.at[jnp.clip(back_wanted, 0, slice_rows - 1)].add(
        jnp.where(back_inside[:, None], back_rows.astype(F32), 0.0)
    )

    norm_grad_all = jnp.concatenate([grad_gains[0], grad_gains[1], grad_final], 0)
    norm_grad_all = sum_everywhere(norm_grad_all)
    norm_place = ((section * replicas + replica) * lanes + lane) * norm_columns
    norm_grad_mine = lax.dynamic_slice_in_dim(norm_grad_all, norm_place, norm_columns, 1)
    norm_grad = norm_grad_mine[:-2].reshape(norm_params.shape)
    final_grad = norm_grad_mine[-2:]

    gradients = (
        qkv_grad,
        out_grad,
        fc_grad,
        proj_grad,
        table_grad,
        position_grad,
        norm_grad,
        final_grad,
    )
    squares = jnp.zeros((), F32)
    for index in range(8):
        part_square = jnp.sum(gradients[index] * gradients[index])
        if index == 4 or index == 5:
            part_square = part_square / sections
        squares = squares + part_square
    sums = jnp.stack([squares, jnp.sum(own_loss), jnp.sum(own_penalty), jnp.sum(own_weight)])
    sums = sum_everywhere(sums)
    loss_sum, penalty_sum, token_count = sums[1], sums[2], sums[3]
    grad_norm = jnp.sqrt(sums[0]) / token_count
    clip_factor = jnp.minimum(1.0, CLIP / (grad_norm + 1e-06))
    step_scale = clip_factor / token_count
    masters = (
        attn_qkv,
        attn_out,
        mlp_in,
        mlp_out,
        embed_table,
        position_table,
        norm_params,
        final_norm,
    )
    moments = (
        (attn_qkv_first, attn_qkv_second),
        (attn_out_first, attn_out_second),
        (mlp_in_first, mlp_in_second),
        (mlp_out_first, mlp_out_second),
        (embed_table_first, embed_table_second),
        (position_table_first, position_table_second),
        (norm_params_first, norm_params_second),
        (final_norm_first, final_norm_second),
    )
    results = []
    for index in range(8):
        results.extend(
            adamw_update(
                masters[index],
                moments[index][0],
                moments[index][1],
                gradients[index] * step_scale,
                RATES[index],
                DECAYS[index],
            )
        )
    loss_parts = jnp.stack([loss_sum, token_count])
    return (loss_parts, penalty_sum, grad_norm, *results)


def solution(mesh):
    row_spec = P("dp", None)
    qkv_spec = P("pipe", "dp", None, "seq")
    into_spec = P("pipe", "dp", "seq")
    out_spec = P("pipe", "seq", "dp")
    table_spec = P("seq", "dp")
    norm_spec = P(None, None, ("pipe", "dp", "seq"))
    final_spec = P(None, ("pipe", "dp", "seq"))
    kinds = (
        qkv_spec,
        out_spec,
        into_spec,
        out_spec,
        table_spec,
        table_spec,
        norm_spec,
        final_spec,
    )
    triples = tuple(spec for spec in kinds for _ in range(3))
    return jax.shard_map(
        per_device,
        mesh=mesh,
        in_specs=(row_spec, row_spec, row_spec) + triples,
        out_specs=(P(), P(), P()) + triples,
        check_vma=False,
    )
```

```python
import jax
import jax.numpy as jnp
from jax import lax
from jax.experimental import pallas as pl
from jax.experimental.layout import Layout, with_layout_constraint
from jax.experimental.pallas import tpu as pltpu
from jax.sharding import PartitionSpec as P

HEAD = 64
STEP = 10


EPS_NORM = 1e-05
ZLOSS = 0.001
CLIP = 0.01
BETA_ONE = 0.9
BETA_TWO = 0.95
EPS_ADAM = 1e-08
RATES = (0.03, 0.1, 0.03, 0.015, 0.05, 0.15, 0.7, 0.7)
DECAYS = (0.1, 0.1, 0.1, 0.1, 0.1, 0.0, 0.0, 0.0)
F32 = jnp.float32
BF16 = jnp.bfloat16


def swap(block, axis, mask):
    route = [(i, i ^ mask) for i in range(lax.axis_size(axis))]
    return lax.ppermute(block, axis, route)


def masks_down(size):
    found = []
    mask = size // 2
    while mask >= 1:
        found.append(mask)
        mask //= 2
    return found


def reverse_bits(value, size):
    result = 0
    mask = 1
    while mask < size:
        result = result * 2 + (value & mask) // mask
        mask *= 2
    return result


def spread(block, held=()):
    for step, mask in enumerate(masks_down(lax.axis_size("seq"))):
        received = swap(block, "seq", mask)
        if held:
            received = after(received, *held[step])
        block = jnp.concatenate([block, received], 0)
    return block


def collect(block, steps=0, skip=0, held=None):
    masks = masks_down(lax.axis_size("seq"))[::-1]
    for mask in masks[skip : steps or len(masks)]:
        half = block.shape[0] // 2
        sent = swap(block[half:].astype(BF16), "seq", mask)
        if held is not None:
            sent = after(sent, held)
        block = block[:half].astype(F32) + sent.astype(F32)
    return block


def from_all(block, axis):
    size = lax.axis_size(axis)
    found = jnp.stack([block] + [swap(block, axis, mask) for mask in range(1, size)])
    return jnp.take(found, lax.axis_index(axis) ^ jnp.arange(size), axis=0)


def sum_everywhere(block):
    for axis in ("seq", "pipe", "dp"):
        block = jnp.sum(from_all(block, axis), 0)
    return block


def norm_rows(values, gain, bias):
    center = values - jnp.mean(values, -1, keepdims=True)
    spread_sq = jnp.mean(center * center, -1, keepdims=True)
    return center * lax.rsqrt(spread_sq + EPS_NORM) * gain + bias


def gelu_tanh(values):
    return jax.nn.gelu(values, approximate=True)


def head_pairs(values):
    tile, columns = values.shape
    place = lax.broadcasted_iota(jnp.int32, (tile, columns), 1)
    wide = values.astype(F32)
    return jnp.concatenate(
        [jnp.where(place < HEAD, wide, 0.0), jnp.where(place < HEAD, 0.0, wide)], 0
    )


def join_pair(values):
    columns, double = values.shape
    tile = double // 2
    place = lax.broadcasted_iota(jnp.int32, (columns, tile), 0)
    return jnp.where(place < HEAD, values[:, :tile], values[:, tile:]).T


def pair_allowed(place_row, document_row, place_column, document_column):
    allowed = (place_column[...] <= place_row[...]) & (document_column[...] == document_row[...])
    return jnp.concatenate([allowed, allowed], 1)


def across(left, right):
    return lax.dot_general(left, right, (((1,), (1,)), ((), ())), preferred_element_type=F32)


def attend_kernel(
    packed_ref, place_row, document_row, place_column, document_column, out_ref, log_ref
):
    tile, columns = out_ref.shape
    here = pl.ds(pl.multiple_of(pl.program_id(0) * tile, tile), tile)
    allowed = pair_allowed(place_row, document_row, place_column, document_column)
    for pair in range(columns // 128):
        span = slice(pair * 128, pair * 128 + 128)
        key_span = slice(columns + pair * 128, columns + pair * 128 + 128)
        value_span = slice(2 * columns + pair * 128, 2 * columns + pair * 128 + 128)
        queries = (head_pairs(packed_ref[here, span]) * HEAD ** (-0.5)).astype(BF16)
        scores = jnp.where(allowed, across(packed_ref[:, key_span], queries), -1e30)
        top = jnp.max(scores, 0, keepdims=True)
        exponent = jnp.exp(scores - top)
        total = jnp.sum(exponent, 0, keepdims=True)
        log_ref[pair, 0] = top + jnp.log(total)
        mixed = jnp.dot(
            packed_ref[:, value_span].T, exponent.astype(BF16), preferred_element_type=F32
        )
        out_ref[:, span] = join_pair(mixed / total).astype(out_ref.dtype)


def row_specs(length, tile):
    return [
        pl.BlockSpec((1, tile), lambda t: (0, t)),
        pl.BlockSpec((1, tile), lambda t: (0, t)),
        pl.BlockSpec((length, 1), lambda t: (0, 0)),
        pl.BlockSpec((length, 1), lambda t: (0, 0)),
    ]


def both_ways(rows):
    place, document = rows
    return place[None, :], document[None, :], place[:, None], document[:, None]


def attend_forward(packed, columns, rows):
    length, stored = packed.shape
    pairs = columns // 128
    tile = min(256, length)
    steps = length // tile
    return pl.pallas_call(
        attend_kernel,
        grid=(steps,),
        in_specs=[pl.BlockSpec((length, stored), lambda t: (0, 0))] + row_specs(length, tile),
        out_specs=[
            pl.BlockSpec((tile, columns), lambda t: (t, 0)),
            pl.BlockSpec((pairs, 1, 1, 2 * tile), lambda t: (0, t, 0, 0)),
        ],
        out_shape=[
            jax.ShapeDtypeStruct((length, columns), BF16),
            jax.ShapeDtypeStruct((pairs, steps, 1, 2 * tile), F32),
        ],
        compiler_params=pltpu.CompilerParams(vmem_limit_bytes=48 * 1024 * 1024),
        cost_estimate=pl.CostEstimate(
            flops=4 * length * length * columns,
            bytes_accessed=2 * length * (stored + columns),
            transcendentals=length * length * pairs * 2,
        ),
    )(packed, *both_ways(rows))


def attend_back_kernel(
    packed_ref,
    grad_ref,
    log_ref,
    place_row,
    document_row,
    place_column,
    document_column,
    out_ref,
    key_total,
    value_total,
):
    tile, columns = grad_ref.shape
    step = pl.program_id(0)
    here = pl.ds(pl.multiple_of(step * tile, tile), tile)
    allowed = pair_allowed(place_row, document_row, place_column, document_column)
    factor = HEAD ** (-0.5)

    @pl.when(step == 0)
    def _():
        key_total[...] = jnp.zeros_like(key_total)
        value_total[...] = jnp.zeros_like(value_total)

    for pair in range(columns // 128):
        span = slice(pair * 128, pair * 128 + 128)
        key_span = slice(columns + pair * 128, columns + pair * 128 + 128)
        value_span = slice(2 * columns + pair * 128, 2 * columns + pair * 128 + 128)
        queries = (head_pairs(packed_ref[here, span]) * factor).astype(BF16)
        grads = head_pairs(grad_ref[:, span]).astype(BF16)
        keys = packed_ref[:, key_span]
        scores = jnp.where(allowed, across(keys, queries), -1e30)
        probabilities = jnp.exp(scores - log_ref[pair, 0])
        value_total[:, span] += jnp.dot(
            probabilities.astype(BF16), grads, preferred_element_type=F32
        )
        grad_soft = across(packed_ref[:, value_span], grads)
        mean = jnp.sum(probabilities * grad_soft, 0, keepdims=True)
        grad_scores = (probabilities * (grad_soft - mean)).astype(BF16)
        key_total[:, span] += jnp.dot(grad_scores, queries, preferred_element_type=F32)
        grad_queries = jnp.dot(keys.T, grad_scores, preferred_element_type=F32)
        out_ref[here, span] = (join_pair(grad_queries) * factor).astype(out_ref.dtype)

    @pl.when(step == pl.num_programs(0) - 1)
    def _():
        out_ref[:, columns : 2 * columns] = key_total[...].astype(out_ref.dtype)
        out_ref[:, 2 * columns : 3 * columns] = value_total[...].astype(out_ref.dtype)
        out_ref[:, 3 * columns :] = jnp.zeros(
            (out_ref.shape[0], out_ref.shape[1] - 3 * columns), out_ref.dtype
        )


def attend_backward(packed, log_sums, grad_mixed, rows):
    length, stored = packed.shape
    columns = grad_mixed.shape[1]
    pairs = columns // 128
    tile = min(256, length)
    steps = length // tile
    return pl.pallas_call(
        attend_back_kernel,
        grid=(steps,),
        in_specs=[
            pl.BlockSpec((length, stored), lambda t: (0, 0)),
            pl.BlockSpec((tile, columns), lambda t: (t, 0)),
            pl.BlockSpec((pairs, 1, 1, 2 * tile), lambda t: (0, t, 0, 0)),
        ]
        + row_specs(length, tile),
        out_specs=pl.BlockSpec((length, stored), lambda t: (0, 0)),
        out_shape=jax.ShapeDtypeStruct((length, stored), BF16),
        scratch_shapes=[pltpu.VMEM((length, columns), F32)] * 2,
        compiler_params=pltpu.CompilerParams(vmem_limit_bytes=48 * 1024 * 1024),
        cost_estimate=pl.CostEstimate(
            flops=10 * length * length * columns,
            bytes_accessed=4 * length * stored,
            transcendentals=length * length * pairs * 2,
        ),
    )(packed, grad_mixed, log_sums, *both_ways(rows))


def forward_attention(residual, w_attn, gain_rows, rows):
    columns = w_attn.shape[1] // 4
    normed = norm_rows(residual, gain_rows[0], gain_rows[1])
    first_full = spread(normed.astype(BF16))
    packed = jnp.dot(first_full, w_attn, preferred_element_type=F32).astype(BF16)
    mixed_rows, log_sums = attend_forward(packed, columns, rows)
    branch = jnp.einsum(
        "tc,dc->td", mixed_rows, w_attn[:, 3 * columns :], preferred_element_type=F32
    )
    return residual + collect(branch), (residual, first_full, packed, log_sums, mixed_rows)


def forward_feed(middle, w_fc, w_proj, gain_rows):
    second = norm_rows(middle, gain_rows[2], gain_rows[3])
    second_full = spread(second.astype(BF16))
    hidden = jnp.dot(second_full, w_fc, preferred_element_type=F32)
    active = gelu_tanh(hidden).astype(BF16)
    branch = jnp.einsum("tf,df->td", active, w_proj, preferred_element_type=F32)
    return middle + collect(branch), (middle, second_full, hidden, active)


def backward_feed(grad_out, saved, w_fc, w_proj, gain_rows):
    middle, second_full, hidden, active = saved
    grad_z = spread(grad_out.astype(BF16))
    grad_active = jnp.dot(grad_z, w_proj, preferred_element_type=F32)
    _, gelu_pull = jax.vjp(gelu_tanh, hidden)
    grad_hidden = gelu_pull(grad_active)[0].astype(BF16)
    grad_second = collect(
        jnp.einsum("tf,df->td", grad_hidden, w_fc, preferred_element_type=F32)
    )
    grad_fc = jnp.einsum("td,tf->df", second_full, grad_hidden, preferred_element_type=F32)
    grad_proj = jnp.einsum("td,tf->df", grad_z, active, preferred_element_type=F32)
    _, norm_pull = jax.vjp(norm_rows, middle, gain_rows[2], gain_rows[3])
    grad_middle, grad_gain, grad_bias = norm_pull(grad_second)
    return (
        grad_middle + grad_out,
        (grad_fc.astype(BF16), grad_proj.astype(BF16)),
        jnp.stack([grad_gain, grad_bias]),
    )


def backward_attention(grad_middle, saved, w_attn, gain_rows, rows):
    residual, first_full, packed, log_sums, mixed_rows = saved
    columns = w_attn.shape[1] // 4
    grad_y = spread(grad_middle.astype(BF16))
    grad_mixed = jnp.dot(
        grad_y, w_attn[:, 3 * columns :], preferred_element_type=F32
    ).astype(BF16)
    grad_packed = attend_backward(packed, log_sums, grad_mixed, rows)
    grad_first = collect(
        jnp.einsum("tc,dc->td", grad_packed, w_attn, preferred_element_type=F32)
    )
    grad_out_w = jnp.einsum("td,tc->dc", grad_y, mixed_rows, preferred_element_type=F32)
    grad_qkv = jnp.einsum(
        "td,tc->dc", first_full, grad_packed[:, : 3 * columns], preferred_element_type=F32
    )
    _, norm_pull = jax.vjp(norm_rows, residual, gain_rows[0], gain_rows[1])
    grad_residual, grad_gain, grad_bias = norm_pull(grad_first)
    return (
        grad_residual + grad_middle,
        jnp.concatenate([grad_qkv, grad_out_w], 1).astype(BF16),
        jnp.stack([grad_gain, grad_bias]),
    )


def block(go, step, *operands):
    shapes = jax.eval_shape(step, *operands)

    def idle(*_):
        return jax.tree.map(lambda leaf: jnp.zeros(leaf.shape, leaf.dtype), shapes)

    return lax.cond(go, step, idle, *operands)


def after(value, *others):
    return lax.optimization_barrier((value, *others))[0]


def together(*values):
    return lax.optimization_barrier(values)


def by_rows(matrix):
    return with_layout_constraint(matrix, Layout((0, 1)))


def exchange_blocks(blocks, axis):
    return [blocks[0]] + [swap(blocks[m], axis, m) for m in range(1, len(blocks))]


def place_columns(blocks, index):
    width = blocks[0].shape[1]
    whole = jnp.zeros((blocks[0].shape[0], width * len(blocks)), blocks[0].dtype)
    for m, block in enumerate(blocks):
        whole = lax.dynamic_update_slice_in_dim(whole, block, (index ^ m) * width, 1)
    return whole


def take_columns(whole, index, count):
    width = whole.shape[1] // count
    return [
        lax.dynamic_slice_in_dim(whole, (index ^ m) * width, width, 1) for m in range(count)
    ]


def row_of(column):
    return jnp.broadcast_to(column, (column.shape[0], 128)).T[:1]


def head_kernel(rows_ref, table_ref, bias_ref, low_ref, mixed_ref, top_ref, sum_ref):
    table = table_ref[...]
    logits = lax.dot_general(
        rows_ref[...], table, (((1,), (1,)), ((), ())), preferred_element_type=F32
    )
    logits = logits + bias_ref[...]
    row_top = jnp.max(logits, 1, keepdims=True)
    exponent = jnp.exp(logits - row_top)
    top_ref[...] = row_of(row_top)
    sum_ref[...] = row_of(jnp.sum(exponent, 1, keepdims=True))
    low = exponent.astype(BF16)
    low_ref[...] = low
    mixed_ref[...] = jnp.dot(low, table, preferred_element_type=F32).astype(mixed_ref.dtype)


def head_block(rows, table, bias):
    length, width = rows.shape
    part_rows = table.shape[0]
    tile = min(512, length)
    return pl.pallas_call(
        head_kernel,
        grid=(length // tile,),
        in_specs=[
            pl.BlockSpec((tile, width), lambda t: (t, 0)),
            pl.BlockSpec((part_rows, width), lambda t: (0, 0), pipeline_mode=pl.Buffered(1)),
            pl.BlockSpec((1, part_rows), lambda t: (0, 0), pipeline_mode=pl.Buffered(1)),
        ],
        out_specs=[
            pl.BlockSpec((tile, part_rows), lambda t: (t, 0)),
            pl.BlockSpec((tile, width), lambda t: (t, 0)),
            pl.BlockSpec((1, tile), lambda t: (0, t)),
            pl.BlockSpec((1, tile), lambda t: (0, t)),
        ],
        out_shape=[
            jax.ShapeDtypeStruct((length, part_rows), BF16),
            jax.ShapeDtypeStruct((length, width), F32),
            jax.ShapeDtypeStruct((1, length), F32),
            jax.ShapeDtypeStruct((1, length), F32),
        ],
        compiler_params=pltpu.CompilerParams(vmem_limit_bytes=56 * 1024 * 1024),
        cost_estimate=pl.CostEstimate(
            flops=4 * length * part_rows * width,
            bytes_accessed=2 * part_rows * (width + length) + 6 * length * width,
            transcendentals=length * part_rows,
        ),
    )(rows, table, bias)


def table_kernel(count, *refs):
    low_refs, row_refs, out_ref = refs[:count], refs[count : 2 * count], refs[2 * count]
    total = None
    for low_ref, row_ref in zip(low_refs, row_refs):
        product = lax.dot_general(
            low_ref[...], row_ref[...], (((0,), (0,)), ((), ())), preferred_element_type=F32
        )
        total = product if total is None else total + product
    out_ref[...] = total.astype(out_ref.dtype)


def table_gradient_of(lows, rows, first, count_tiles, tile):
    count = len(lows)
    length, part_rows = lows[0].shape
    width = rows[0].shape[1]
    return pl.pallas_call(
        lambda *refs: table_kernel(count, *refs),
        grid=(count_tiles,),
        in_specs=[pl.BlockSpec((length, tile), lambda v: (0, v + first))] * count
        + [pl.BlockSpec((length, width), lambda v: (0, 0), pipeline_mode=pl.Buffered(1))] * count,
        out_specs=pl.BlockSpec((tile, width), lambda v: (v, 0)),
        out_shape=jax.ShapeDtypeStruct((count_tiles * tile, width), BF16),
        compiler_params=pltpu.CompilerParams(vmem_limit_bytes=60 * 1024 * 1024),
        cost_estimate=pl.CostEstimate(
            flops=2 * count * length * count_tiles * tile * width,
            bytes_accessed=2 * count_tiles * tile * (width + count * length)
            + 2 * count * length * width,
            transcendentals=0,
        ),
    )(*lows, *rows)


def part_place(group, half, part_rows, slice_rows):
    wanted = group * part_rows + half * (part_rows // 2)
    return jnp.minimum(wanted, slice_rows - part_rows // 2), wanted


def scatter_kernel(count_ref, list_ref, near_ref, far_ref, rows_ref, out_ref, square_ref, wide):
    slice_rows = out_ref.shape[0]
    shift = (slice_rows - 1).bit_length()
    replicas, half_rows = near_ref.shape[:2]
    section, replica = lax.axis_index("pipe"), lax.axis_index("dp")
    out_ref[...] = jnp.zeros_like(out_ref)
    for m in range(replicas):
        for half, part in ((section, near_ref), (1 - section, far_ref)):
            start, _ = part_place(replica ^ m, half, 2 * half_rows, slice_rows)
            out_ref[pl.ds(pl.multiple_of(start, 8), half_rows), :] += part[m].astype(F32)
    wide[...] = rows_ref[...].astype(F32)

    def add_one(k):
        coded = list_ref[k]
        here = pl.ds(jnp.bitwise_and(coded, (1 << shift) - 1), 1)
        out_ref[here, :] += wide[pl.ds(lax.shift_right_logical(coded, shift), 1), :]

    def add_some(k, carry):
        for u in range(8):
            add_one(8 * k + u)
        return carry

    def add_last(k, carry):
        add_one(k)
        return carry

    count = count_ref[0]
    groups = lax.shift_right_logical(count, 3)
    lax.fori_loop(0, groups, add_some, 0)
    lax.fori_loop(8 * groups, count, add_last, 0)
    result = out_ref[...]
    square_ref[...] = jnp.sum(result * result, 0, keepdims=True)


def scatter_rows(listing, count, near, far, rows, slice_rows):
    columns = near.shape[2]
    whole = pl.BlockSpec(memory_space=pltpu.VMEM)
    scalars = pl.BlockSpec(memory_space=pltpu.SMEM)
    return pl.pallas_call(
        scatter_kernel,
        in_specs=[scalars, scalars, whole, whole, whole],
        out_specs=[whole, whole],
        out_shape=[
            jax.ShapeDtypeStruct((slice_rows, columns), F32),
            jax.ShapeDtypeStruct((1, columns), F32),
        ],
        scratch_shapes=[pltpu.VMEM(rows.shape, F32)],
        compiler_params=pltpu.CompilerParams(vmem_limit_bytes=60 * 1024 * 1024),
        cost_estimate=pl.CostEstimate(
            flops=4 * slice_rows * columns,
            bytes_accessed=8 * slice_rows * columns + 2 * rows.size,
            transcendentals=0,
        ),
    )(count, listing, near, far, rows)


def scatter_over(part, axes):
    return lax.psum_scatter(part, axes, scatter_dimension=0, tiled=True)


def merge_stats(stats):
    both = jnp.stack(stats)
    for axis, place in (("seq", 2), ("dp", 1)):
        size = lax.axis_size(axis)
        found = [both]
        for mask in range(1, size):
            shift = reverse_bits(mask, size) if axis == "seq" else mask
            order = jnp.array([k ^ shift for k in range(size)])
            found.append(jnp.take(swap(both, axis, mask), order, axis=place))
        top = found[0][0]
        for pair in found[1:]:
            top = jnp.maximum(top, pair[0])
        both = jnp.stack([top, sum(pair[1] * jnp.exp(pair[0] - top) for pair in found)])
    return both[0] + jnp.log(both[1])


def adamw_update(master, first, second, gradient, rate, decay):
    first_new = BETA_ONE * first + (1.0 - BETA_ONE) * gradient
    second_new = BETA_TWO * second + (1.0 - BETA_TWO) * gradient * gradient
    ratio = (
        first_new
        / (1.0 - BETA_ONE**STEP)
        / (jnp.sqrt(second_new / (1.0 - BETA_TWO**STEP)) + EPS_ADAM)
    )
    return (master - rate * (ratio + decay * master), first_new, second_new)


def per_device(
    token_ids,
    segments,
    valid,
    attn_qkv,
    attn_qkv_first,
    attn_qkv_second,
    attn_out,
    attn_out_first,
    attn_out_second,
    mlp_in,
    mlp_in_first,
    mlp_in_second,
    mlp_out,
    mlp_out_first,
    mlp_out_second,
    embed_table,
    embed_table_first,
    embed_table_second,
    position_table,
    position_table_first,
    position_table_second,
    norm_params,
    norm_params_first,
    norm_params_second,
    final_norm,
    final_norm_first,
    final_norm_second,
):
    section, replica, lane = lax.axis_index("pipe"), lax.axis_index("dp"), lax.axis_index("seq")
    sections, replicas, lanes = (lax.axis_size(name) for name in ("pipe", "dp", "seq"))
    length = token_ids.shape[1]
    assert sections == 2 and token_ids.shape[0] == sections and attn_qkv.shape[0] == 1
    shard_rows = length // lanes
    slice_rows, slice_columns = embed_table.shape
    width = slice_columns * replicas
    part_rows = -(-slice_rows // (replicas * 128)) * 128
    half_rows = part_rows // 2
    assert part_rows * (replicas - 1) < slice_rows
    lane_order = [reverse_bits(k, lanes) for k in range(lanes)]
    lane_blocks = lane ^ jnp.array(lane_order)

    norm_mine = jnp.concatenate([norm_params.reshape(-1, norm_params.shape[2]), final_norm], 0)
    norm_columns = norm_mine.shape[1]
    norm_all = norm_mine[None]
    for axis in ("seq", "dp", "pipe"):
        for mask in reversed(masks_down(lax.axis_size(axis))):
            norm_all = jnp.concatenate([norm_all, swap(norm_all, axis, mask)], 0)
    own_place = (section * replicas + replica) * lanes + lane
    norm_all = jnp.take(norm_all, own_place ^ jnp.arange(norm_all.shape[0]), axis=0)
    norm_all = jnp.transpose(norm_all, (1, 0, 2)).reshape(norm_mine.shape[0], width)
    gain_stack = norm_all[:-2].reshape(norm_params.shape[0], 4, width)
    final_rows = norm_all[-2:]

    own_ids = lax.dynamic_index_in_dim(token_ids, section, 0, keepdims=False)
    own_valid = lax.dynamic_index_in_dim(valid, section, 0, keepdims=False)
    row_segments = lax.dynamic_index_in_dim(segments, section, 0, keepdims=False)
    coded = own_ids * 2 + own_valid
    coded_all = jnp.stack([coded] + [swap(coded, "dp", m) for m in range(1, replicas)])
    ids_all = coded_all // 2
    position = jnp.arange(length)
    weight_all = jnp.where(position < length - 1, coded_all % 2, 0).astype(F32)
    targets_all = jnp.roll(ids_all, -1, axis=1)

    def by_lane(values):
        return jnp.take(values.reshape(-1, lanes, shard_rows), lane_blocks, axis=1)

    ids_lane, weight_lane, targets_lane = by_lane(ids_all), by_lane(weight_all), by_lane(targets_all)

    go = lax.optimization_barrier(jnp.int32(1)) > 0
    qkv_columns = attn_qkv.shape[2] * attn_qkv.shape[3]
    attn_columns = qkv_columns + attn_out.shape[1]
    shards = [
        jnp.concatenate([attn_qkv[0].reshape(-1, qkv_columns), attn_out[0].T], 1),
        mlp_in[0],
        mlp_out[0].T,
    ]
    gathered = [
        lax.all_gather(by_rows(shard.astype(BF16)), "dp", axis=0, tiled=True) for shard in shards
    ]

    def two_layers(mine):
        other = swap(mine, "pipe", 1)
        return jnp.where(section == 0, mine, other), jnp.where(section == 0, other, mine)

    w_attn, w_fc = two_layers(gathered[0]), two_layers(gathered[1])

    vocab_start = lane * slice_rows
    wanted = jnp.transpose(ids_lane, (1, 0, 2)).reshape(-1) - vocab_start
    inside = (wanted >= 0) & (wanted < slice_rows)
    picked = jnp.take(embed_table, jnp.clip(wanted, 0, slice_rows - 1), axis=0)
    picked = jnp.where(inside[:, None], picked, 0.0).astype(BF16)
    picked = collect(picked).astype(BF16).reshape(replicas, shard_rows, slice_columns)
    embed_rows = place_columns(exchange_blocks(list(picked), "dp"), replica)
    position_low = position_table.astype(BF16)
    position_rows = place_columns(
        exchange_blocks([position_low] * replicas, "dp"), replica
    )
    start_rows = embed_rows.astype(F32) + position_rows.astype(F32)
    next_first = lax.ppermute(embed_rows[:1], "seq", [(k, k - 1) for k in range(1, lanes)])
    target_rows = jnp.concatenate([embed_rows[1:], next_first], 0).astype(F32)

    coded_other = swap(coded_all, "pipe", 1)
    ids_both = jnp.where(
        section == 0,
        jnp.concatenate([ids_all, coded_other // 2], 0),
        jnp.concatenate([coded_other // 2, ids_all], 0),
    )
    back_wanted = jnp.transpose(by_lane(ids_both), (1, 0, 2)).reshape(-1) - vocab_start
    back_inside = (back_wanted >= 0) & (back_wanted < slice_rows)
    back_number = jnp.arange(back_wanted.shape[0])
    back_coded = back_number * (1 << (slice_rows - 1).bit_length()) + back_wanted
    back_listing = jnp.sort(jnp.where(back_inside, back_coded, 2**31 - 1))
    back_count = jnp.sum(back_inside.astype(jnp.int32))[None]
    start_rows, back_listing, back_count = together(start_rows, back_listing, back_count)

    table_f32 = after(embed_table, start_rows)
    table_parts = [
        lax.dynamic_slice_in_dim(
            table_f32,
            part_place(replica ^ m, section, part_rows, slice_rows)[0],
            half_rows,
            0,
        ).astype(BF16)
        for m in range(replicas)
    ]
    table_blocks = exchange_blocks(table_parts, "dp")
    bias_halves = []
    for half in (section, 1 - section):
        start, wanted = part_place(replica, half, part_rows, slice_rows)
        bias_halves.append(jnp.where(start + jnp.arange(half_rows) >= wanted, 0.0, -1e30))
    table_bias = jnp.concatenate(bias_halves).astype(F32)[None]

    row_place = (lane_blocks[:, None] * shard_rows + jnp.arange(shard_rows)[None, :]).reshape(-1)
    row_document = jnp.take(row_segments.reshape(lanes, shard_rows), lane_blocks, axis=0).reshape(-1)
    places = (row_place, row_document)
    rows = start_rows
    saved = []
    for layer in range(2):
        gains = gain_stack[layer]
        rows, kept_attn = block(go, forward_attention, rows, w_attn[layer], gains, places)
        if layer == 0:
            rows, gathered[2] = together(rows, gathered[2])
            w_proj = two_layers(gathered[2])
        rows, kept_feed = block(go, forward_feed, rows, w_fc[layer], w_proj[layer], gains)
        saved.append((kept_attn, kept_feed))
        if layer == 0:
            rows, *table_blocks = together(rows, *table_blocks)
            table_half = place_columns(table_blocks, replica)
            table_other = swap(table_half, "pipe", 1)
    table = jnp.concatenate([table_half, table_other], 0)
    final_value, final_pull = jax.vjp(norm_rows, rows, final_rows[0], final_rows[1])
    final_low = final_value.astype(BF16)

    full, heads = [], []
    steps = len(masks_down(lanes))
    for m, part in enumerate(exchange_blocks([final_low] * replicas, "dp")):
        held = [[heads[m - back][2]] if m >= back else [] for back in range(steps + 1, 0, -1)]
        full.append(spread(after(part, *held[0]), held[1:]))
        heads.append(block(go, head_block, full[m], table, table_bias))
    stat_shape = (replicas, lanes, shard_rows)
    row_top = jnp.stack([head[2] for head in heads]).reshape(stat_shape)
    row_sum = jnp.stack([head[3] for head in heads]).reshape(stat_shape)
    log_total = merge_stats((row_top, row_sum))
    scale = weight_lane * (1.0 + 2.0 * ZLOSS * log_total) * jnp.exp(row_top - log_total)
    own_weight, own_log = weight_lane[0, 0], log_total[0, 0]
    target_logit = jnp.sum(final_low.astype(F32) * target_rows, 1)
    own_penalty = own_weight * ZLOSS * own_log * own_log
    own_loss = own_weight * (own_log - target_logit) + own_penalty

    scale_flat = scale.reshape(replicas, length)
    weighted_parts = [scale_flat[m][:, None] * heads[m][1] for m in range(replicas)]
    first_sums = [collect(part, 1) for part in weighted_parts]
    tile = max(t for t in range(128, 641, 128) if part_rows % t == 0)
    first_tiles = half_rows // tile
    lows = [head[0] for head in heads]
    scaled = [
        after((scale_flat[m][:, None] * full[m].astype(F32)).astype(BF16), *first_sums)
        for m in range(replicas)
    ]
    late_tiles = part_rows // tile - first_tiles
    late = block(
        go,
        lambda lows, scaled: table_gradient_of(lows, scaled, first_tiles, late_tiles, tile),
        lows,
        scaled,
    )
    head_parts = [collect(part, 0, 1, late).astype(BF16) for part in first_sums]
    half_sent = late[half_rows - first_tiles * tile :]
    half_sent, *head_parts = together(half_sent, *head_parts)
    half_other = swap(half_sent, "pipe", 1)
    received_parts = exchange_blocks(head_parts, "dp")
    scaled[0] = after(scaled[0], *head_parts)
    early = block(
        go,
        lambda lows, scaled: table_gradient_of(lows, scaled, 0, first_tiles, tile),
        lows,
        scaled,
    )
    half_kept = jnp.concatenate([early, late[: half_rows - first_tiles * tile]], 0)
    head_parts = [received_parts[0]] + [after(part, early) for part in received_parts[1:]]
    grad_final_rows = sum(part.astype(F32) for part in head_parts)
    grad_final_rows = grad_final_rows - own_weight[:, None] * target_rows
    gradient, final_gain_part, final_bias_part = final_pull(grad_final_rows)
    grad_final = jnp.stack([final_gain_part, final_bias_part])

    weighted = own_weight[:, None] * final_low.astype(F32)
    before_first = lax.ppermute(
        weighted[-1:].astype(BF16), "seq", [(k, k + 1) for k in range(lanes - 1)]
    )
    target_part = jnp.concatenate([before_first.astype(F32), weighted[:-1]], 0)

    scattered = [[], []]
    grad_gains = [None, None]
    for layer in (1, 0):
        kept_attn, kept_feed = saved[layer]
        gains = gain_stack[layer]
        gradient, feed_parts, gains_feed = block(
            go, backward_feed, gradient, kept_feed, w_fc[layer], w_proj[layer], gains
        )
        if layer == 1:
            gradient, half_other, *feed_parts = together(gradient, half_other, *feed_parts)
            scattered[1].extend(scatter_over(part, ("dp", "pipe")) for part in feed_parts)
            half_sum = (
                half_kept.astype(F32) + half_other.astype(F32)
            ).astype(BF16)
            gradient, *half_parts = together(gradient, *take_columns(half_sum, replica, replicas))
            half_parts = exchange_blocks(half_parts, "dp")
        else:
            gradient, scattered[1][1], feed_parts, half_parts = together(
                gradient, scattered[1][1], feed_parts, half_parts
            )
            scattered[0].extend(scatter_over(part, "dp") for part in feed_parts)
            half_back = jnp.stack(half_parts)
            gradient, half_back = together(gradient, half_back)
            half_far = swap(half_back, "pipe", 1)
        gradient, attn_part, gains_attn = block(
            go, backward_attention, gradient, kept_attn, w_attn[layer], gains, places
        )
        scattered[layer].append(scatter_over(attn_part, "dp"))
        if layer == 1:
            gradient, scattered[1][0] = together(gradient, scattered[1][0])
        else:
            gradient, scattered[1][2] = together(gradient, scattered[1][2])
        grad_gains[layer] = jnp.concatenate([gains_attn, gains_feed], 0)
    sent_rows = jnp.concatenate(
        [(gradient - target_part).astype(BF16), gradient.astype(BF16)], 0
    )
    back = exchange_blocks(take_columns(sent_rows, replica, replicas), "dp")
    position_part = sum(part[shard_rows:].astype(F32) for part in back)
    position_grad = position_part + swap(position_part, "pipe", 1)
    back = jnp.concatenate([part[:shard_rows] for part in back], 0)
    back, half_far, scattered[0][0] = together(back, half_far, scattered[0][0])
    back_other = swap(back, "pipe", 1)
    back_other, scattered[0][1] = together(back_other, scattered[0][1])
    back_both = jnp.where(
        section == 0,
        jnp.concatenate([back, back_other], 0),
        jnp.concatenate([back_other, back], 0),
    )
    back_rows = spread(back_both)
    table_grad, table_square = scatter_rows(
        back_listing, back_count, half_back, half_far, back_rows, slice_rows
    )

    sent = [parts[0] for parts in zip(*scattered)]
    sent[2] = jnp.where(section == 0, scattered[1][2], scattered[0][2])
    feed_halves = [swap(half, "pipe", 1) for half in scattered[1][:2]]
    received = [swap(part, "pipe", 1) for part in sent]
    feed_grads = [
        jnp.where(
            section == 0,
            scattered[0][k].astype(F32) + received[k].astype(F32),
            jnp.concatenate([feed_halves[k], scattered[1][k]], 0).astype(F32),
        )
        for k in range(2)
    ]
    fc_part, proj_part = feed_grads
    attn_part = jnp.where(section == 0, scattered[0][2], scattered[1][2]).astype(
        F32
    ) + received[2].astype(F32)
    qkv_grad = attn_part[:, :qkv_columns].reshape(attn_qkv.shape)
    out_grad = attn_part[:, qkv_columns:].T[None]
    fc_grad = fc_part[None]
    proj_grad = proj_part.T[None]

    norm_grad_all = jnp.concatenate([grad_gains[0], grad_gains[1], grad_final], 0)
    squares = (
        jnp.sum(qkv_grad * qkv_grad)
        + jnp.sum(out_grad * out_grad)
        + jnp.sum(fc_grad * fc_grad)
        + jnp.sum(proj_grad * proj_grad)
        + (jnp.sum(table_square) + jnp.sum(position_grad * position_grad)) / sections
    )
    sums = jnp.stack([squares, jnp.sum(own_loss), jnp.sum(own_penalty), jnp.sum(own_weight)])
    sums = jnp.pad(sums, (0, width - sums.shape[0]))[None]
    summed = sum_everywhere(jnp.concatenate([norm_grad_all, sums], 0))
    norm_grad_all, sums = summed[:-1], summed[-1]
    norm_grad_mine = lax.dynamic_slice_in_dim(
        norm_grad_all, own_place * norm_columns, norm_columns, 1
    )
    gradients = (
        qkv_grad,
        out_grad,
        fc_grad,
        proj_grad,
        table_grad,
        position_grad,
        norm_grad_mine[:-2].reshape(norm_params.shape),
        norm_grad_mine[-2:],
    )
    squares = sums[0] + jnp.sum(norm_grad_all * norm_grad_all)
    loss_sum, penalty_sum, token_count = sums[1], sums[2], sums[3]
    grad_norm = jnp.sqrt(squares) / token_count
    clip_factor = jnp.minimum(1.0, CLIP / (grad_norm + 1e-06))
    step_scale = clip_factor / token_count
    masters = (
        attn_qkv,
        attn_out,
        mlp_in,
        mlp_out,
        embed_table,
        position_table,
        norm_params,
        final_norm,
    )
    moments = (
        (attn_qkv_first, attn_qkv_second),
        (attn_out_first, attn_out_second),
        (mlp_in_first, mlp_in_second),
        (mlp_out_first, mlp_out_second),
        (embed_table_first, embed_table_second),
        (position_table_first, position_table_second),
        (norm_params_first, norm_params_second),
        (final_norm_first, final_norm_second),
    )
    results = []
    for index in range(8):
        results.extend(
            adamw_update(
                masters[index],
                moments[index][0],
                moments[index][1],
                gradients[index] * step_scale,
                RATES[index],
                DECAYS[index],
            )
        )
    loss_parts = jnp.stack([loss_sum, token_count])
    return (loss_parts, penalty_sum, grad_norm, *results)


def solution(mesh):
    row_spec = P("dp", None)
    qkv_spec = P("pipe", "dp", None, "seq")
    into_spec = P("pipe", "dp", "seq")
    out_spec = P("pipe", "seq", "dp")
    table_spec = P("seq", "dp")
    norm_spec = P(None, None, ("pipe", "dp", "seq"))
    final_spec = P(None, ("pipe", "dp", "seq"))
    kinds = (
        qkv_spec,
        out_spec,
        into_spec,
        out_spec,
        table_spec,
        table_spec,
        norm_spec,
        final_spec,
    )
    triples = tuple(spec for spec in kinds for _ in range(3))
    return jax.shard_map(
        per_device,
        mesh=mesh,
        in_specs=(row_spec, row_spec, row_spec) + triples,
        out_specs=(P(), P(), P()) + triples,
        check_vma=False,
    )
```

```python
import jax
import jax.numpy as jnp
from jax import lax
from jax.experimental import pallas as pl
from jax.experimental.layout import Layout, with_layout_constraint
from jax.experimental.pallas import tpu as pltpu
from jax.sharding import PartitionSpec as P

HEAD = 64
STEP = 10


EPS_NORM = 1e-05
ZLOSS = 0.001
CLIP = 0.01
BETA_ONE = 0.9
BETA_TWO = 0.95
EPS_ADAM = 1e-08
RATES = (0.03, 0.1, 0.03, 0.015, 0.05, 0.15, 0.7, 0.7)
DECAYS = (0.1, 0.1, 0.1, 0.1, 0.1, 0.0, 0.0, 0.0)
F32 = jnp.float32
BF16 = jnp.bfloat16


def swap(block, axis, mask):
    route = [(i, i ^ mask) for i in range(lax.axis_size(axis))]
    return lax.ppermute(block, axis, route)


def masks_down(size):
    found = []
    mask = size // 2
    while mask >= 1:
        found.append(mask)
        mask //= 2
    return found


def reverse_bits(value, size):
    result = 0
    mask = 1
    while mask < size:
        result = result * 2 + (value & mask) // mask
        mask *= 2
    return result


def spread(block, steps=None, held=()):
    for mask in masks_down(lax.axis_size("seq"))[:steps]:
        received = swap(block, "seq", mask)
        if held:
            received = after(received, *held)
        block = jnp.concatenate([block, received], 0)
    return block


def collect(block):
    for mask in reversed(masks_down(lax.axis_size("seq"))):
        half = block.shape[0] // 2
        sent = swap(block[half:].astype(BF16), "seq", mask)
        block = block[:half].astype(F32) + sent.astype(F32)
    return block


def collect_scaled(block, scale):
    half = block.shape[0] // 2
    mask = masks_down(lax.axis_size("seq"))[-1]
    sent = swap((block[half:].astype(F32) * scale[half:, None]).astype(BF16), "seq", mask)
    return block[:half].astype(F32) * scale[:half, None] + sent.astype(F32)


def collect_rest(block, held):
    for mask in reversed(masks_down(lax.axis_size("seq"))[:-1]):
        half = block.shape[0] // 2
        sent = after(swap(block[half:].astype(BF16), "seq", mask), held)
        block = block[:half] + sent.astype(F32)
    return block


def from_all(block, axis):
    size = lax.axis_size(axis)
    found = jnp.stack([block] + [swap(block, axis, mask) for mask in range(1, size)])
    return jnp.take(found, lax.axis_index(axis) ^ jnp.arange(size), axis=0)


def sum_everywhere(block):
    for axis in ("seq", "pipe", "dp"):
        block = jnp.sum(from_all(block, axis), 0)
    return block


def norm_rows(values, gain, bias):
    center = values - jnp.mean(values, -1, keepdims=True)
    spread_sq = jnp.mean(center * center, -1, keepdims=True)
    return center * lax.rsqrt(spread_sq + EPS_NORM) * gain + bias


def gelu_tanh(values):
    return jax.nn.gelu(values, approximate=True)


def head_pairs(values):
    tile, columns = values.shape
    place = lax.broadcasted_iota(jnp.int32, (tile, columns), 1)
    wide = values.astype(F32)
    return jnp.concatenate(
        [jnp.where(place < HEAD, wide, 0.0), jnp.where(place < HEAD, 0.0, wide)], 0
    )


def join_pair(values):
    columns, double = values.shape
    tile = double // 2
    place = lax.broadcasted_iota(jnp.int32, (columns, tile), 0)
    return jnp.where(place < HEAD, values[:, :tile], values[:, tile:]).T


def pair_allowed(place_row, document_row, place_column, document_column):
    allowed = (place_column[...] <= place_row[...]) & (document_column[...] == document_row[...])
    return jnp.concatenate([allowed, allowed], 1)


def across(left, right):
    return lax.dot_general(left, right, (((1,), (1,)), ((), ())), preferred_element_type=F32)


def attend_kernel(
    packed_ref, place_row, document_row, place_column, document_column, out_ref, log_ref
):
    tile, columns = out_ref.shape
    here = pl.ds(pl.multiple_of(pl.program_id(0) * tile, tile), tile)
    allowed = pair_allowed(place_row, document_row, place_column, document_column)
    for pair in range(columns // 128):
        span = slice(pair * 128, pair * 128 + 128)
        key_span = slice(columns + pair * 128, columns + pair * 128 + 128)
        value_span = slice(2 * columns + pair * 128, 2 * columns + pair * 128 + 128)
        queries = (head_pairs(packed_ref[here, span]) * HEAD ** (-0.5)).astype(BF16)
        scores = jnp.where(allowed, across(packed_ref[:, key_span], queries), -1e30)
        top = jnp.max(scores, 0, keepdims=True)
        exponent = jnp.exp(scores - top)
        total = jnp.sum(exponent, 0, keepdims=True)
        log_ref[pair, 0] = top + jnp.log(total)
        mixed = jnp.dot(
            packed_ref[:, value_span].T, exponent.astype(BF16), preferred_element_type=F32
        )
        out_ref[:, span] = join_pair(mixed / total).astype(out_ref.dtype)


def row_specs(length, tile):
    return [
        pl.BlockSpec((1, tile), lambda t: (0, t)),
        pl.BlockSpec((1, tile), lambda t: (0, t)),
        pl.BlockSpec((length, 1), lambda t: (0, 0)),
        pl.BlockSpec((length, 1), lambda t: (0, 0)),
    ]


def both_ways(rows):
    place, document = rows
    return place[None, :], document[None, :], place[:, None], document[:, None]


def attend_forward(packed, columns, rows):
    length, stored = packed.shape
    pairs = columns // 128
    tile = min(256, length)
    steps = length // tile
    return pl.pallas_call(
        attend_kernel,
        grid=(steps,),
        in_specs=[pl.BlockSpec((length, stored), lambda t: (0, 0))] + row_specs(length, tile),
        out_specs=[
            pl.BlockSpec((tile, columns), lambda t: (t, 0)),
            pl.BlockSpec((pairs, 1, 1, 2 * tile), lambda t: (0, t, 0, 0)),
        ],
        out_shape=[
            jax.ShapeDtypeStruct((length, columns), BF16),
            jax.ShapeDtypeStruct((pairs, steps, 1, 2 * tile), F32),
        ],
        compiler_params=pltpu.CompilerParams(vmem_limit_bytes=48 * 1024 * 1024),
        cost_estimate=pl.CostEstimate(
            flops=4 * length * length * columns,
            bytes_accessed=2 * length * (stored + columns),
            transcendentals=length * length * pairs * 2,
        ),
    )(packed, *both_ways(rows))


def attend_back_kernel(
    packed_ref,
    grad_ref,
    log_ref,
    place_row,
    document_row,
    place_column,
    document_column,
    out_ref,
    key_total,
    value_total,
):
    tile, columns = grad_ref.shape
    step = pl.program_id(0)
    here = pl.ds(pl.multiple_of(step * tile, tile), tile)
    allowed = pair_allowed(place_row, document_row, place_column, document_column)
    factor = HEAD ** (-0.5)

    @pl.when(step == 0)
    def _():
        key_total[...] = jnp.zeros_like(key_total)
        value_total[...] = jnp.zeros_like(value_total)

    for pair in range(columns // 128):
        span = slice(pair * 128, pair * 128 + 128)
        key_span = slice(columns + pair * 128, columns + pair * 128 + 128)
        value_span = slice(2 * columns + pair * 128, 2 * columns + pair * 128 + 128)
        queries = (head_pairs(packed_ref[here, span]) * factor).astype(BF16)
        grads = head_pairs(grad_ref[:, span]).astype(BF16)
        keys = packed_ref[:, key_span]
        scores = jnp.where(allowed, across(keys, queries), -1e30)
        probabilities = jnp.exp(scores - log_ref[pair, 0])
        value_total[:, span] += jnp.dot(
            probabilities.astype(BF16), grads, preferred_element_type=F32
        )
        grad_soft = across(packed_ref[:, value_span], grads)
        mean = jnp.sum(probabilities * grad_soft, 0, keepdims=True)
        grad_scores = (probabilities * (grad_soft - mean)).astype(BF16)
        key_total[:, span] += jnp.dot(grad_scores, queries, preferred_element_type=F32)
        grad_queries = jnp.dot(keys.T, grad_scores, preferred_element_type=F32)
        out_ref[here, span] = (join_pair(grad_queries) * factor).astype(out_ref.dtype)

    @pl.when(step == pl.num_programs(0) - 1)
    def _():
        out_ref[:, columns : 2 * columns] = key_total[...].astype(out_ref.dtype)
        out_ref[:, 2 * columns : 3 * columns] = value_total[...].astype(out_ref.dtype)
        out_ref[:, 3 * columns :] = jnp.zeros(
            (out_ref.shape[0], out_ref.shape[1] - 3 * columns), out_ref.dtype
        )


def attend_backward(packed, log_sums, grad_mixed, rows):
    length, stored = packed.shape
    columns = grad_mixed.shape[1]
    pairs = columns // 128
    tile = min(256, length)
    steps = length // tile
    return pl.pallas_call(
        attend_back_kernel,
        grid=(steps,),
        in_specs=[
            pl.BlockSpec((length, stored), lambda t: (0, 0)),
            pl.BlockSpec((tile, columns), lambda t: (t, 0)),
            pl.BlockSpec((pairs, 1, 1, 2 * tile), lambda t: (0, t, 0, 0)),
        ]
        + row_specs(length, tile),
        out_specs=pl.BlockSpec((length, stored), lambda t: (0, 0)),
        out_shape=jax.ShapeDtypeStruct((length, stored), BF16),
        scratch_shapes=[pltpu.VMEM((length, columns), F32)] * 2,
        compiler_params=pltpu.CompilerParams(vmem_limit_bytes=48 * 1024 * 1024),
        cost_estimate=pl.CostEstimate(
            flops=10 * length * length * columns,
            bytes_accessed=4 * length * stored,
            transcendentals=length * length * pairs * 2,
        ),
    )(packed, grad_mixed, log_sums, *both_ways(rows))


def forward_attention(residual, w_attn, gain_rows, rows):
    columns = w_attn.shape[1] // 4
    normed = norm_rows(residual, gain_rows[0], gain_rows[1])
    first_full = spread(normed.astype(BF16))
    packed = jnp.dot(first_full, w_attn, preferred_element_type=F32).astype(BF16)
    mixed_rows, log_sums = attend_forward(packed, columns, rows)
    branch = jnp.einsum(
        "tc,dc->td", mixed_rows, w_attn[:, 3 * columns :], preferred_element_type=F32
    )
    return residual + collect(branch), (residual, first_full, packed, log_sums, mixed_rows)


def forward_feed(middle, w_fc, w_proj, gain_rows):
    second = norm_rows(middle, gain_rows[2], gain_rows[3])
    second_full = spread(second.astype(BF16))
    hidden = jnp.dot(second_full, w_fc, preferred_element_type=F32)
    active = gelu_tanh(hidden).astype(BF16)
    branch = jnp.einsum("tf,df->td", active, w_proj, preferred_element_type=F32)
    return middle + collect(branch), (middle, second_full, hidden, active)


def backward_feed(grad_out, saved, w_fc, w_proj, gain_rows):
    middle, second_full, hidden, active = saved
    grad_z = spread(grad_out.astype(BF16))
    grad_active = jnp.dot(grad_z, w_proj, preferred_element_type=F32)
    _, gelu_pull = jax.vjp(gelu_tanh, hidden)
    grad_hidden = gelu_pull(grad_active)[0].astype(BF16)
    grad_second = collect(
        jnp.einsum("tf,df->td", grad_hidden, w_fc, preferred_element_type=F32)
    )
    grad_fc = jnp.einsum("td,tf->df", second_full, grad_hidden, preferred_element_type=F32)
    grad_proj = jnp.einsum("td,tf->df", grad_z, active, preferred_element_type=F32)
    _, norm_pull = jax.vjp(norm_rows, middle, gain_rows[2], gain_rows[3])
    grad_middle, grad_gain, grad_bias = norm_pull(grad_second)
    return (
        grad_middle + grad_out,
        (grad_fc.astype(BF16), grad_proj.astype(BF16)),
        jnp.stack([grad_gain, grad_bias]),
    )


def backward_attention(grad_middle, saved, w_attn, gain_rows, rows):
    residual, first_full, packed, log_sums, mixed_rows = saved
    columns = w_attn.shape[1] // 4
    grad_y = spread(grad_middle.astype(BF16))
    grad_mixed = jnp.dot(
        grad_y, w_attn[:, 3 * columns :], preferred_element_type=F32
    ).astype(BF16)
    grad_packed = attend_backward(packed, log_sums, grad_mixed, rows)
    grad_first = collect(
        jnp.einsum("tc,dc->td", grad_packed, w_attn, preferred_element_type=F32)
    )
    grad_out_w = jnp.einsum("td,tc->dc", grad_y, mixed_rows, preferred_element_type=F32)
    grad_qkv = jnp.einsum(
        "td,tc->dc", first_full, grad_packed[:, : 3 * columns], preferred_element_type=F32
    )
    _, norm_pull = jax.vjp(norm_rows, residual, gain_rows[0], gain_rows[1])
    grad_residual, grad_gain, grad_bias = norm_pull(grad_first)
    return (
        grad_residual + grad_middle,
        jnp.concatenate([grad_qkv, grad_out_w], 1).astype(BF16),
        jnp.stack([grad_gain, grad_bias]),
    )


def block(go, step, *operands):
    shapes = jax.eval_shape(step, *operands)

    def idle(*_):
        return jax.tree.map(lambda leaf: jnp.zeros(leaf.shape, leaf.dtype), shapes)

    return lax.cond(go, step, idle, *operands)


def after(value, *others):
    return lax.optimization_barrier((value, *others))[0]


def together(*values):
    return lax.optimization_barrier(values)


def by_rows(matrix):
    return with_layout_constraint(matrix, Layout((0, 1)))


def exchange_blocks(blocks, axis):
    return [blocks[0]] + [swap(blocks[m], axis, m) for m in range(1, len(blocks))]


def place_columns(blocks, index):
    width = blocks[0].shape[1]
    whole = jnp.zeros((blocks[0].shape[0], width * len(blocks)), blocks[0].dtype)
    for m, block in enumerate(blocks):
        whole = lax.dynamic_update_slice_in_dim(whole, block, (index ^ m) * width, 1)
    return whole


def take_columns(whole, index, count):
    width = whole.shape[1] // count
    return [
        lax.dynamic_slice_in_dim(whole, (index ^ m) * width, width, 1) for m in range(count)
    ]


def row_of(column):
    return jnp.broadcast_to(column, (column.shape[0], 128)).T[:1]


def head_kernel(first_ref, second_ref, table_ref, bias_ref, low_ref, mixed_ref, top_ref, sum_ref):
    table = table_ref[...]
    rows = jnp.where(pl.program_id(0) == 0, first_ref[...], second_ref[...])
    logits = lax.dot_general(
        rows, table, (((1,), (1,)), ((), ())), preferred_element_type=F32
    )
    logits = logits + bias_ref[...]
    row_top = jnp.max(logits, 1, keepdims=True)
    exponent = jnp.exp(logits - row_top)
    top_ref[...] = row_of(row_top)
    sum_ref[...] = row_of(jnp.sum(exponent, 1, keepdims=True))
    low = exponent.astype(BF16)
    low_ref[...] = low
    mixed_ref[...] = jnp.dot(low, table, preferred_element_type=F32).astype(mixed_ref.dtype)


def head_block(first, second, table, bias):
    tile, width = first.shape
    length = 2 * tile
    part_rows = table.shape[0]
    return pl.pallas_call(
        head_kernel,
        grid=(length // tile,),
        in_specs=[
            pl.BlockSpec((tile, width), lambda t: (0, 0), pipeline_mode=pl.Buffered(1)),
            pl.BlockSpec((tile, width), lambda t: (0, 0), pipeline_mode=pl.Buffered(1)),
            pl.BlockSpec((part_rows, width), lambda t: (0, 0), pipeline_mode=pl.Buffered(1)),
            pl.BlockSpec((1, part_rows), lambda t: (0, 0), pipeline_mode=pl.Buffered(1)),
        ],
        out_specs=[
            pl.BlockSpec((tile, part_rows), lambda t: (t, 0)),
            pl.BlockSpec((tile, width), lambda t: (t, 0)),
            pl.BlockSpec((1, tile), lambda t: (0, t)),
            pl.BlockSpec((1, tile), lambda t: (0, t)),
        ],
        out_shape=[
            jax.ShapeDtypeStruct((length, part_rows), BF16),
            jax.ShapeDtypeStruct((length, width), BF16),
            jax.ShapeDtypeStruct((1, length), F32),
            jax.ShapeDtypeStruct((1, length), F32),
        ],
        compiler_params=pltpu.CompilerParams(vmem_limit_bytes=56 * 1024 * 1024),
        cost_estimate=pl.CostEstimate(
            flops=4 * length * part_rows * width,
            bytes_accessed=2 * part_rows * (width + length) + 6 * length * width,
            transcendentals=length * part_rows,
        ),
    )(first, second, table, bias)


def table_kernel(count, *refs):
    low_refs, row_refs, out_ref = refs[:count], refs[count : 3 * count], refs[3 * count]
    half = row_refs[0].shape[0]
    total = None
    for k, row_ref in enumerate(row_refs):
        product = lax.dot_general(
            low_refs[k // 2][k % 2 * half : (k % 2 + 1) * half, :],
            row_ref[...],
            (((0,), (0,)), ((), ())),
            preferred_element_type=F32,
        )
        total = product if total is None else total + product
    out_ref[...] = total.astype(out_ref.dtype)


def table_gradient_of(lows, rows, first, count_tiles, tile):
    count = len(lows)
    length, part_rows = lows[0].shape
    half, width = rows[0].shape
    return pl.pallas_call(
        lambda *refs: table_kernel(count, *refs),
        grid=(count_tiles,),
        in_specs=[pl.BlockSpec((length, tile), lambda v: (0, v + first))] * count
        + [pl.BlockSpec((half, width), lambda v: (0, 0), pipeline_mode=pl.Buffered(1))]
        * (2 * count),
        out_specs=pl.BlockSpec((tile, width), lambda v: (v, 0)),
        out_shape=jax.ShapeDtypeStruct((count_tiles * tile, width), BF16),
        compiler_params=pltpu.CompilerParams(vmem_limit_bytes=60 * 1024 * 1024),
        cost_estimate=pl.CostEstimate(
            flops=2 * count * length * count_tiles * tile * width,
            bytes_accessed=2 * count_tiles * tile * (width + count * length)
            + 2 * count * length * width,
            transcendentals=0,
        ),
    )(*lows, *rows)


def part_place(group, half, part_rows, slice_rows):
    wanted = group * part_rows + half * (part_rows // 2)
    return jnp.minimum(wanted, slice_rows - part_rows // 2), wanted


def scatter_kernel(
    count_ref, list_ref, near_ref, far_ref, own_ref, other_ref, out_ref, square_ref, wide
):
    slice_rows = out_ref.shape[0]
    shift = (slice_rows - 1).bit_length()
    replicas, half_rows = near_ref.shape[:2]
    section, replica = lax.axis_index("pipe"), lax.axis_index("dp")
    out_ref[...] = jnp.zeros_like(out_ref)
    for m in range(replicas):
        for half, part in ((section, near_ref), (1 - section, far_ref)):
            start, _ = part_place(replica ^ m, half, 2 * half_rows, slice_rows)
            out_ref[pl.ds(pl.multiple_of(start, 8), half_rows), :] += part[m].astype(F32)
    count_rows = own_ref.shape[0]
    wide[pl.ds(pl.multiple_of(section * count_rows, 8), count_rows), :] = own_ref[...].astype(F32)
    wide[pl.ds(pl.multiple_of((1 - section) * count_rows, 8), count_rows), :] = other_ref[
        ...
    ].astype(F32)

    def add_one(k):
        coded = list_ref[k]
        here = pl.ds(jnp.bitwise_and(coded, (1 << shift) - 1), 1)
        out_ref[here, :] += wide[pl.ds(lax.shift_right_logical(coded, shift), 1), :]

    def add_some(k, carry):
        for u in range(8):
            add_one(8 * k + u)
        return carry

    def add_last(k, carry):
        add_one(k)
        return carry

    count = count_ref[0]
    groups = lax.shift_right_logical(count, 3)
    lax.fori_loop(0, groups, add_some, 0)
    lax.fori_loop(8 * groups, count, add_last, 0)
    result = out_ref[...]
    square_ref[...] = jnp.sum(result * result, 0, keepdims=True)


def scatter_rows(listing, count, near, far, own, other, slice_rows):
    columns = near.shape[2]
    whole = pl.BlockSpec(memory_space=pltpu.VMEM)
    scalars = pl.BlockSpec(memory_space=pltpu.SMEM)
    return pl.pallas_call(
        scatter_kernel,
        in_specs=[scalars, scalars, whole, whole, whole, whole],
        out_specs=[whole, whole],
        out_shape=[
            jax.ShapeDtypeStruct((slice_rows, columns), F32),
            jax.ShapeDtypeStruct((1, columns), F32),
        ],
        scratch_shapes=[pltpu.VMEM((2 * own.shape[0], columns), F32)],
        compiler_params=pltpu.CompilerParams(vmem_limit_bytes=60 * 1024 * 1024),
        cost_estimate=pl.CostEstimate(
            flops=4 * slice_rows * columns,
            bytes_accessed=8 * slice_rows * columns + 4 * own.size,
            transcendentals=0,
        ),
    )(count, listing, near, far, own, other)


def scatter_over(part, axes):
    return lax.psum_scatter(part, axes, scatter_dimension=0, tiled=True)


def merge_stats(stats):
    both = jnp.stack(stats)
    for axis, place in (("seq", 2), ("dp", 1)):
        size = lax.axis_size(axis)
        found = [both]
        for mask in range(1, size):
            shift = reverse_bits(mask, size) if axis == "seq" else mask
            order = jnp.array([k ^ shift for k in range(size)])
            found.append(jnp.take(swap(both, axis, mask), order, axis=place))
        top = found[0][0]
        for pair in found[1:]:
            top = jnp.maximum(top, pair[0])
        both = jnp.stack([top, sum(pair[1] * jnp.exp(pair[0] - top) for pair in found)])
    return both[0] + jnp.log(both[1])


def adamw_update(master, first, second, gradient, rate, decay):
    first_new = BETA_ONE * first + (1.0 - BETA_ONE) * gradient
    second_new = BETA_TWO * second + (1.0 - BETA_TWO) * gradient * gradient
    ratio = (
        first_new
        / (1.0 - BETA_ONE**STEP)
        / (jnp.sqrt(second_new / (1.0 - BETA_TWO**STEP)) + EPS_ADAM)
    )
    return (master - rate * (ratio + decay * master), first_new, second_new)


def per_device(
    token_ids,
    segments,
    valid,
    attn_qkv,
    attn_qkv_first,
    attn_qkv_second,
    attn_out,
    attn_out_first,
    attn_out_second,
    mlp_in,
    mlp_in_first,
    mlp_in_second,
    mlp_out,
    mlp_out_first,
    mlp_out_second,
    embed_table,
    embed_table_first,
    embed_table_second,
    position_table,
    position_table_first,
    position_table_second,
    norm_params,
    norm_params_first,
    norm_params_second,
    final_norm,
    final_norm_first,
    final_norm_second,
):
    section, replica, lane = lax.axis_index("pipe"), lax.axis_index("dp"), lax.axis_index("seq")
    sections, replicas, lanes = (lax.axis_size(name) for name in ("pipe", "dp", "seq"))
    length = token_ids.shape[1]
    assert sections == 2 and token_ids.shape[0] == sections and attn_qkv.shape[0] == 1
    shard_rows = length // lanes
    slice_rows, slice_columns = embed_table.shape
    width = slice_columns * replicas
    part_rows = -(-slice_rows // (replicas * 128)) * 128
    half_rows = part_rows // 2
    assert part_rows * (replicas - 1) < slice_rows
    lane_order = [reverse_bits(k, lanes) for k in range(lanes)]
    lane_blocks = lane ^ jnp.array(lane_order)

    norm_mine = jnp.concatenate([norm_params.reshape(-1, norm_params.shape[2]), final_norm], 0)
    norm_columns = norm_mine.shape[1]
    norm_all = from_all(from_all(from_all(norm_mine, "pipe"), "dp"), "seq")
    norm_all = jnp.transpose(norm_all, (2, 1, 0, 3, 4)).reshape(-1, *norm_mine.shape)
    own_place = (section * replicas + replica) * lanes + lane
    own_ids = lax.dynamic_index_in_dim(token_ids, section, 0, keepdims=False)
    own_valid = lax.dynamic_index_in_dim(valid, section, 0, keepdims=False)
    row_segments = lax.dynamic_index_in_dim(segments, section, 0, keepdims=False)
    coded = own_ids * 2 + own_valid
    coded_all = jnp.stack([coded] + [swap(coded, "dp", m) for m in range(1, replicas)])
    ids_all = coded_all // 2
    position = jnp.arange(length)
    weight_all = jnp.where(position < length - 1, coded_all % 2, 0).astype(F32)
    targets_all = jnp.roll(ids_all, -1, axis=1)

    def by_lane(values):
        return jnp.take(values.reshape(-1, lanes, shard_rows), lane_blocks, axis=1)

    ids_lane, weight_lane, targets_lane = by_lane(ids_all), by_lane(weight_all), by_lane(targets_all)

    go = lax.optimization_barrier(jnp.int32(1)) > 0
    qkv_columns = attn_qkv.shape[2] * attn_qkv.shape[3]
    attn_columns = qkv_columns + attn_out.shape[1]
    shards = [
        jnp.concatenate([attn_qkv[0].reshape(-1, qkv_columns), attn_out[0].T], 1),
        mlp_in[0],
        mlp_out[0].T,
    ]
    shards = [by_rows(shard.astype(BF16)) for shard in shards]

    def both_layers(mine, other=None):
        if other is None:
            other = swap(mine, "pipe", 1)
        return [jnp.where(section == 0, mine, other), jnp.where(section == 0, other, mine)]

    def over_dp(shard):
        return lax.all_gather(shard, "dp", axis=0, tiled=True)

    attn_mine, fc_mine = over_dp(shards[0]), over_dp(shards[1])
    proj_shards = both_layers(shards[2])

    vocab_start = lane * slice_rows
    wanted = jnp.transpose(ids_lane, (1, 0, 2)).reshape(-1) - vocab_start
    inside = (wanted >= 0) & (wanted < slice_rows)
    picked = jnp.take(embed_table, jnp.clip(wanted, 0, slice_rows - 1), axis=0)
    picked = jnp.where(inside[:, None], picked, 0.0).astype(BF16)
    picked, norm_all, proj_shards, attn_mine = together(
        picked, norm_all, proj_shards, attn_mine
    )
    attn_other = swap(attn_mine, "pipe", 1)
    w_proj = [over_dp(shard) for shard in proj_shards]
    picked = collect(picked).astype(BF16).reshape(replicas, shard_rows, slice_columns)
    norm_all = jnp.transpose(norm_all, (1, 0, 2)).reshape(norm_mine.shape[0], width)
    gain_stack = norm_all[:-2].reshape(norm_params.shape[0], 4, width)
    final_rows = norm_all[-2:]
    embed_blocks, attn_other = together(exchange_blocks(list(picked), "dp"), attn_other)
    w_attn = both_layers(attn_mine, attn_other)
    embed_rows = place_columns(embed_blocks, replica)
    position_low = position_table.astype(BF16)
    position_rows = place_columns(
        exchange_blocks([position_low] * replicas, "dp"), replica
    )
    start_rows = embed_rows.astype(F32) + position_rows.astype(F32)
    next_first = lax.ppermute(embed_rows[:1], "seq", [(k, k - 1) for k in range(1, lanes)])
    target_rows = jnp.concatenate([embed_rows[1:], next_first], 0).astype(F32)

    coded_other = swap(coded_all, "pipe", 1)
    ids_both = jnp.where(
        section == 0,
        jnp.concatenate([ids_all, coded_other // 2], 0),
        jnp.concatenate([coded_other // 2, ids_all], 0),
    )
    back_wanted = by_lane(ids_both).reshape(sections, replicas, lanes, shard_rows)
    back_wanted = jnp.transpose(back_wanted, (0, 2, 1, 3)).reshape(-1) - vocab_start
    back_inside = (back_wanted >= 0) & (back_wanted < slice_rows)
    back_number = jnp.arange(back_wanted.shape[0])
    back_coded = back_number * (1 << (slice_rows - 1).bit_length()) + back_wanted
    back_listing = jnp.sort(jnp.where(back_inside, back_coded, 2**31 - 1))
    back_count = jnp.sum(back_inside.astype(jnp.int32))[None]
    start_rows, back_listing, back_count = together(start_rows, back_listing, back_count)

    start_rows, fc_mine = together(start_rows, fc_mine)
    w_fc = both_layers(fc_mine)

    bias_halves = []
    for half in (section, 1 - section):
        start, wanted = part_place(replica, half, part_rows, slice_rows)
        bias_halves.append(jnp.where(start + jnp.arange(half_rows) >= wanted, 0.0, -1e30))
    table_bias = jnp.concatenate(bias_halves).astype(F32)[None]

    row_place = (lane_blocks[:, None] * shard_rows + jnp.arange(shard_rows)[None, :]).reshape(-1)
    row_document = jnp.take(row_segments.reshape(lanes, shard_rows), lane_blocks, axis=0).reshape(-1)
    places = (row_place, row_document)
    rows = start_rows
    saved = []
    for layer in range(2):
        gains = gain_stack[layer]
        rows, kept_attn = block(go, forward_attention, rows, w_attn[layer], gains, places)
        if layer == 0:
            table_f32 = after(embed_table, rows)
            table_parts = [
                lax.dynamic_slice_in_dim(
                    table_f32,
                    part_place(replica ^ m, section, part_rows, slice_rows)[0],
                    half_rows,
                    0,
                ).astype(BF16)
                for m in range(replicas)
            ]
            rows, *table_parts = together(rows, *table_parts)
            table_blocks = exchange_blocks(table_parts, "dp")
        else:
            rows, w_proj[1] = together(rows, w_proj[1])
            rows, *table_blocks = together(rows, *table_blocks)
            table_half = place_columns(table_blocks, replica)
            table_other = swap(table_half, "pipe", 1)
        rows, kept_feed = block(go, forward_feed, rows, w_fc[layer], w_proj[layer], gains)
        saved.append((kept_attn, kept_feed))
    table = jnp.concatenate([table_half, table_other], 0)
    final_value, final_pull = jax.vjp(norm_rows, rows, final_rows[0], final_rows[1])
    final_low = final_value.astype(BF16)

    parts = exchange_blocks([final_low] * replicas, "dp")
    steps = len(masks_down(lanes)) - 1
    full, heads = [], []
    half = spread(parts[0], steps)

    def head_step(half, table, bias, *coming):
        other = swap(half, "seq", 1)
        outputs = head_block(half, other, table, bias)
        return (half, other), outputs, [spread(part, steps, (outputs[2],)) for part in coming]

    for m in range(replicas):
        rows, head, coming = block(go, head_step, half, table, table_bias, *parts[m + 1 : m + 2])
        full.append(rows)
        heads.append(head)
        half = coming[0] if coming else None
    stat_shape = (replicas, lanes, shard_rows)
    row_top = jnp.stack([head[2] for head in heads]).reshape(stat_shape)
    row_sum = jnp.stack([head[3] for head in heads]).reshape(stat_shape)
    log_total = merge_stats((row_top, row_sum))
    scale = weight_lane * (1.0 + 2.0 * ZLOSS * log_total) * jnp.exp(row_top - log_total)
    own_weight, own_log = weight_lane[0, 0], log_total[0, 0]
    target_logit = jnp.sum(final_low.astype(F32) * target_rows, 1)
    own_penalty = own_weight * ZLOSS * own_log * own_log
    own_loss = own_weight * (own_log - target_logit) + own_penalty

    scale_flat = scale.reshape(replicas, length)
    first_sums = [collect_scaled(heads[m][1], scale_flat[m]) for m in range(replicas)]
    tile = max(t for t in range(128, 641, 128) if part_rows % t == 0)
    first_tiles = half_rows // tile
    lows = [head[0] for head in heads]
    half_length = length // 2
    scaled = [
        after(
            (
                scale_flat[m][k * half_length : (k + 1) * half_length, None]
                * full[m][k].astype(F32)
            ).astype(BF16),
            *first_sums,
        )
        for m in range(replicas)
        for k in range(2)
    ]
    late_tiles = part_rows // tile - first_tiles
    late = block(
        go,
        lambda lows, scaled: table_gradient_of(lows, scaled, first_tiles, late_tiles, tile),
        lows,
        scaled,
    )
    head_parts = [collect_rest(part, late).astype(BF16) for part in first_sums]
    half_sent = late[half_rows - first_tiles * tile :]
    half_sent, *head_parts = together(half_sent, *head_parts)
    half_other = swap(half_sent, "pipe", 1)
    received_parts = exchange_blocks(head_parts, "dp")
    scaled[0] = after(scaled[0], *head_parts)
    early = block(
        go,
        lambda lows, scaled: table_gradient_of(lows, scaled, 0, first_tiles, tile),
        lows,
        scaled,
    )
    half_kept = jnp.concatenate([early, late[: half_rows - first_tiles * tile]], 0)
    head_parts = [received_parts[0]] + [after(part, early) for part in received_parts[1:]]
    grad_final_rows = sum(part.astype(F32) for part in head_parts)
    grad_final_rows = grad_final_rows - own_weight[:, None] * target_rows
    gradient, final_gain_part, final_bias_part = final_pull(grad_final_rows)
    grad_final = jnp.stack([final_gain_part, final_bias_part])

    weighted = own_weight[:, None] * final_low.astype(F32)
    before_first = lax.ppermute(
        weighted[-1:].astype(BF16), "seq", [(k, k + 1) for k in range(lanes - 1)]
    )
    target_part = jnp.concatenate([before_first.astype(F32), weighted[:-1]], 0)

    grad_gains = [None, None]
    moving = [list(range(1, replicas))[: replicas // 2], list(range(1, replicas))[replicas // 2 :]]
    arrived = {}

    def send_some(value, stage):
        value, *sent = together(value, *[half_parts[m] for m in moving[stage]])
        return value, {m: swap(part, "dp", m) for m, part in zip(moving[stage], sent)}

    def column_half(matrix, half):
        columns = matrix.shape[1] // 2
        return lax.dynamic_slice_in_dim(matrix, half * columns, columns, 1)

    def send_halves(value, matrices):
        value, *sent = together(value, *[column_half(part, 1 - section) for part in matrices])
        return value, [swap(part, "pipe", 1) for part in sent]

    def sum_halves(value, matrices, coming):
        sums = [
            (column_half(part, section).astype(F32) + other.astype(F32)).astype(BF16)
            for part, other in zip(matrices, coming)
        ]
        return together(value, *sums)

    gradient, feed_late, gains_feed = block(
        go, backward_feed, gradient, saved[1][1], w_fc[1], w_proj[1], gain_stack[1]
    )
    gradient, half_other, *feed_late = together(gradient, half_other, *feed_late)
    half_sum = (half_kept.astype(F32) + half_other.astype(F32)).astype(BF16)
    half_parts = take_columns(half_sum, replica, replicas)
    gradient, flight = send_some(gradient, 0)
    gradient, coming = send_halves(gradient, feed_late)
    gradient, attn_late, gains_attn = block(
        go, backward_attention, gradient, saved[1][0], w_attn[1], gain_stack[1], places
    )
    grad_gains[1] = jnp.concatenate([gains_attn, gains_feed], 0)
    gradient, flight, coming, attn_late = together(gradient, flight, coming, attn_late)
    arrived.update(flight)
    gradient, flight = send_some(gradient, 1)
    gradient, *sums = sum_halves(gradient, feed_late, coming)
    feed_late = [scatter_over(part, "dp") for part in sums]
    gradient, attn_coming = send_halves(gradient, [attn_late])
    gradient, feed_early, gains_feed = block(
        go, backward_feed, gradient, saved[0][1], w_fc[0], w_proj[0], gain_stack[0]
    )
    gradient, flight, attn_coming, *feed_early = together(
        gradient, flight, attn_coming, *feed_early
    )
    arrived.update(flight)
    half_back = jnp.stack([half_parts[0]] + [arrived[m] for m in range(1, replicas)])
    gradient, half_back = together(gradient, half_back)
    half_far = swap(half_back, "pipe", 1)
    feed_early = [scatter_over(part, "dp") for part in feed_early]
    gradient, attn_late = sum_halves(gradient, [attn_late], attn_coming)
    attn_late = scatter_over(attn_late, "dp")
    gradient, feed_late = together(gradient, feed_late)
    gradient, attn_early, gains_attn = block(
        go, backward_attention, gradient, saved[0][0], w_attn[0], gain_stack[0], places
    )
    grad_gains[0] = jnp.concatenate([gains_attn, gains_feed], 0)
    gradient, attn_coming = send_halves(gradient, [attn_early])
    late_halves = [swap(part, "pipe", 1) for part in feed_late]

    sent_rows = jnp.concatenate(
        [(gradient - target_part).astype(BF16), gradient.astype(BF16)], 0
    )
    back = exchange_blocks(take_columns(sent_rows, replica, replicas), "dp")
    position_part = sum(part[shard_rows:].astype(F32) for part in back)
    position_grad = position_part + swap(position_part, "pipe", 1)
    back = jnp.concatenate([part[:shard_rows] for part in back], 0)
    back, attn_coming, half_far, feed_early[0] = together(
        back, attn_coming, half_far, feed_early[0]
    )
    back, attn_early = sum_halves(back, [attn_early], attn_coming)
    attn_early = scatter_over(attn_early, "dp")
    back_other = swap(back, "pipe", 1)
    own_rows = spread(back)
    back_other, feed_early[1] = together(back_other, feed_early[1])
    other_rows = spread(back_other)
    table_grad, table_square = scatter_rows(
        back_listing, back_count, half_back, half_far, own_rows, other_rows, slice_rows
    )

    feed_coming = [swap(part, "pipe", 1) for part in feed_early]
    attn_late, attn_early, *feed_coming = together(
        attn_late, attn_early, *feed_coming, table_square
    )[:-1]
    attn_coming = swap(jnp.where(section == 0, attn_late, attn_early), "pipe", 1)
    attn_part = jnp.where(
        section == 0,
        jnp.concatenate([attn_early, attn_coming], 1),
        jnp.concatenate([attn_coming, attn_late], 1),
    ).astype(F32)
    fc_part, proj_part = (
        jnp.where(
            section == 0,
            feed_early[k].astype(F32) + feed_coming[k].astype(F32),
            jnp.concatenate([late_halves[k], feed_late[k]], 1).astype(F32),
        )
        for k in range(2)
    )
    qkv_grad = attn_part[:, :qkv_columns].reshape(attn_qkv.shape)
    out_grad = attn_part[:, qkv_columns:].T[None]
    fc_grad = fc_part[None]
    proj_grad = proj_part.T[None]

    norm_grad_all = jnp.concatenate([grad_gains[0], grad_gains[1], grad_final], 0)
    squares = (
        jnp.sum(qkv_grad * qkv_grad)
        + jnp.sum(out_grad * out_grad)
        + jnp.sum(fc_grad * fc_grad)
        + jnp.sum(proj_grad * proj_grad)
        + (jnp.sum(table_square) + jnp.sum(position_grad * position_grad)) / sections
    )
    sums = jnp.stack([squares, jnp.sum(own_loss), jnp.sum(own_penalty), jnp.sum(own_weight)])
    sums = jnp.pad(sums, (0, width - sums.shape[0]))[None]
    summed = sum_everywhere(jnp.concatenate([norm_grad_all, sums], 0))
    norm_grad_all, sums = summed[:-1], summed[-1]
    norm_grad_mine = lax.dynamic_slice_in_dim(
        norm_grad_all, own_place * norm_columns, norm_columns, 1
    )
    gradients = (
        qkv_grad,
        out_grad,
        fc_grad,
        proj_grad,
        table_grad,
        position_grad,
        norm_grad_mine[:-2].reshape(norm_params.shape),
        norm_grad_mine[-2:],
    )
    squares = sums[0] + jnp.sum(norm_grad_all * norm_grad_all)
    loss_sum, penalty_sum, token_count = sums[1], sums[2], sums[3]
    grad_norm = jnp.sqrt(squares) / token_count
    clip_factor = jnp.minimum(1.0, CLIP / (grad_norm + 1e-06))
    step_scale = clip_factor / token_count
    masters = (
        attn_qkv,
        attn_out,
        mlp_in,
        mlp_out,
        embed_table,
        position_table,
        norm_params,
        final_norm,
    )
    moments = (
        (attn_qkv_first, attn_qkv_second),
        (attn_out_first, attn_out_second),
        (mlp_in_first, mlp_in_second),
        (mlp_out_first, mlp_out_second),
        (embed_table_first, embed_table_second),
        (position_table_first, position_table_second),
        (norm_params_first, norm_params_second),
        (final_norm_first, final_norm_second),
    )
    results = []
    for index in range(8):
        results.extend(
            adamw_update(
                masters[index],
                moments[index][0],
                moments[index][1],
                gradients[index] * step_scale,
                RATES[index],
                DECAYS[index],
            )
        )
    loss_parts = jnp.stack([loss_sum, token_count])
    return (loss_parts, penalty_sum, grad_norm, *results)


def solution(mesh):
    row_spec = P("dp", None)
    qkv_spec = P("pipe", "dp", None, "seq")
    into_spec = P("pipe", "dp", "seq")
    out_spec = P("pipe", "seq", "dp")
    table_spec = P("seq", "dp")
    norm_spec = P(None, None, ("pipe", "dp", "seq"))
    final_spec = P(None, ("pipe", "dp", "seq"))
    kinds = (
        qkv_spec,
        out_spec,
        into_spec,
        out_spec,
        table_spec,
        table_spec,
        norm_spec,
        final_spec,
    )
    triples = tuple(spec for spec in kinds for _ in range(3))
    return jax.shard_map(
        per_device,
        mesh=mesh,
        in_specs=(row_spec, row_spec, row_spec) + triples,
        out_specs=(P(), P(), P()) + triples,
        check_vma=False,
    )
```

```python
import jax
import jax.numpy as jnp
from jax import lax
from jax.experimental import pallas as pl
from jax.experimental.layout import Layout, with_layout_constraint
from jax.experimental.pallas import tpu as pltpu
from jax.sharding import PartitionSpec as P

HEAD = 64
STEP = 10


EPS_NORM = 1e-05
ZLOSS = 0.001
CLIP = 0.01
BETA_ONE = 0.9
BETA_TWO = 0.95
EPS_ADAM = 1e-08
RATES = (0.03, 0.1, 0.03, 0.015, 0.05, 0.15, 0.7, 0.7)
DECAYS = (0.1, 0.1, 0.1, 0.1, 0.1, 0.0, 0.0, 0.0)
F32 = jnp.float32
BF16 = jnp.bfloat16


def swap(block, axis, mask):
    route = [(i, i ^ mask) for i in range(lax.axis_size(axis))]
    return lax.ppermute(block, axis, route)


def masks_down(size):
    found = []
    mask = size // 2
    while mask >= 1:
        found.append(mask)
        mask //= 2
    return found


def reverse_bits(value, size):
    result = 0
    mask = 1
    while mask < size:
        result = result * 2 + (value & mask) // mask
        mask *= 2
    return result


def spread(block, steps=None, held=()):
    for mask in masks_down(lax.axis_size("seq"))[:steps]:
        received = swap(block, "seq", mask)
        if held:
            received = after(received, *held)
        block = jnp.concatenate([block, received], 0)
    return block


def collect(block):
    for mask in reversed(masks_down(lax.axis_size("seq"))):
        half = block.shape[0] // 2
        sent = swap(block[half:].astype(BF16), "seq", mask)
        block = block[:half].astype(F32) + sent.astype(F32)
    return block


def collect_scaled(block, scale):
    half = block.shape[0] // 2
    mask = masks_down(lax.axis_size("seq"))[-1]
    sent = swap((block[half:].astype(F32) * scale[half:, None]).astype(BF16), "seq", mask)
    return block[:half].astype(F32) * scale[:half, None] + sent.astype(F32)


def collect_rest(block, held):
    for mask in reversed(masks_down(lax.axis_size("seq"))[:-1]):
        half = block.shape[0] // 2
        sent = after(swap(block[half:].astype(BF16), "seq", mask), held)
        block = block[:half] + sent.astype(F32)
    return block


def from_all(block, axis):
    names = axis if isinstance(axis, tuple) else (axis,)
    size = 1
    for name in names:
        size *= lax.axis_size(name)
    routes = [[(i, i ^ mask) for i in range(size)] for mask in range(1, size)]
    found = jnp.stack([block] + [lax.ppermute(block, axis, route) for route in routes])
    return jnp.take(found, lax.axis_index(axis) ^ jnp.arange(size), axis=0)


def sum_everywhere(block):
    for axis in ("seq", ("pipe", "dp")):
        block = jnp.sum(from_all(block, axis), 0)
    return block


def norm_rows(values, gain, bias):
    center = values - jnp.mean(values, -1, keepdims=True)
    spread_sq = jnp.mean(center * center, -1, keepdims=True)
    return center * lax.rsqrt(spread_sq + EPS_NORM) * gain + bias


def gelu_tanh(values):
    return jax.nn.gelu(values, approximate=True)


def head_pairs(values):
    tile, columns = values.shape
    place = lax.broadcasted_iota(jnp.int32, (tile, columns), 1)
    wide = values.astype(F32)
    return jnp.concatenate(
        [jnp.where(place < HEAD, wide, 0.0), jnp.where(place < HEAD, 0.0, wide)], 0
    )


def join_pair(values):
    columns, double = values.shape
    tile = double // 2
    place = lax.broadcasted_iota(jnp.int32, (columns, tile), 0)
    return jnp.where(place < HEAD, values[:, :tile], values[:, tile:]).T


def pair_allowed(place_row, document_row, place_column, document_column):
    allowed = (place_column[...] <= place_row[...]) & (document_column[...] == document_row[...])
    return jnp.concatenate([allowed, allowed], 1)


def across(left, right):
    return lax.dot_general(left, right, (((1,), (1,)), ((), ())), preferred_element_type=F32)


def attend_kernel(
    packed_ref, place_row, document_row, place_column, document_column, out_ref, log_ref
):
    tile, columns = out_ref.shape
    here = pl.ds(pl.multiple_of(pl.program_id(0) * tile, tile), tile)
    allowed = pair_allowed(place_row, document_row, place_column, document_column)
    for pair in range(columns // 128):
        span = slice(pair * 128, pair * 128 + 128)
        key_span = slice(columns + pair * 128, columns + pair * 128 + 128)
        value_span = slice(2 * columns + pair * 128, 2 * columns + pair * 128 + 128)
        queries = (head_pairs(packed_ref[here, span]) * HEAD ** (-0.5)).astype(BF16)
        scores = jnp.where(allowed, across(packed_ref[:, key_span], queries), -1e30)
        top = jnp.max(scores, 0, keepdims=True)
        exponent = jnp.exp(scores - top)
        total = jnp.sum(exponent, 0, keepdims=True)
        log_ref[pair, 0] = top + jnp.log(total)
        mixed = jnp.dot(
            packed_ref[:, value_span].T, exponent.astype(BF16), preferred_element_type=F32
        )
        out_ref[:, span] = join_pair(mixed / total).astype(out_ref.dtype)


def row_specs(length, tile):
    return [
        pl.BlockSpec((1, tile), lambda t: (0, t)),
        pl.BlockSpec((1, tile), lambda t: (0, t)),
        pl.BlockSpec((length, 1), lambda t: (0, 0)),
        pl.BlockSpec((length, 1), lambda t: (0, 0)),
    ]


def both_ways(rows):
    place, document = rows
    return place[None, :], document[None, :], place[:, None], document[:, None]


def attend_forward(packed, columns, rows):
    length, stored = packed.shape
    pairs = columns // 128
    tile = min(256, length)
    steps = length // tile
    return pl.pallas_call(
        attend_kernel,
        grid=(steps,),
        in_specs=[pl.BlockSpec((length, stored), lambda t: (0, 0))] + row_specs(length, tile),
        out_specs=[
            pl.BlockSpec((tile, columns), lambda t: (t, 0)),
            pl.BlockSpec((pairs, 1, 1, 2 * tile), lambda t: (0, t, 0, 0)),
        ],
        out_shape=[
            jax.ShapeDtypeStruct((length, columns), BF16),
            jax.ShapeDtypeStruct((pairs, steps, 1, 2 * tile), F32),
        ],
        compiler_params=pltpu.CompilerParams(vmem_limit_bytes=48 * 1024 * 1024),
        cost_estimate=pl.CostEstimate(
            flops=4 * length * length * columns,
            bytes_accessed=2 * length * (stored + columns),
            transcendentals=length * length * pairs * 2,
        ),
    )(packed, *both_ways(rows))


def attend_back_kernel(
    packed_ref,
    grad_ref,
    log_ref,
    place_row,
    document_row,
    place_column,
    document_column,
    out_ref,
    key_total,
    value_total,
):
    tile, columns = grad_ref.shape
    step = pl.program_id(0)
    here = pl.ds(pl.multiple_of(step * tile, tile), tile)
    allowed = pair_allowed(place_row, document_row, place_column, document_column)
    factor = HEAD ** (-0.5)

    @pl.when(step == 0)
    def _():
        key_total[...] = jnp.zeros_like(key_total)
        value_total[...] = jnp.zeros_like(value_total)

    for pair in range(columns // 128):
        span = slice(pair * 128, pair * 128 + 128)
        key_span = slice(columns + pair * 128, columns + pair * 128 + 128)
        value_span = slice(2 * columns + pair * 128, 2 * columns + pair * 128 + 128)
        queries = (head_pairs(packed_ref[here, span]) * factor).astype(BF16)
        grads = head_pairs(grad_ref[:, span]).astype(BF16)
        keys = packed_ref[:, key_span]
        scores = jnp.where(allowed, across(keys, queries), -1e30)
        probabilities = jnp.exp(scores - log_ref[pair, 0])
        value_total[:, span] += jnp.dot(
            probabilities.astype(BF16), grads, preferred_element_type=F32
        )
        grad_soft = across(packed_ref[:, value_span], grads)
        mean = jnp.sum(probabilities * grad_soft, 0, keepdims=True)
        grad_scores = (probabilities * (grad_soft - mean)).astype(BF16)
        key_total[:, span] += jnp.dot(grad_scores, queries, preferred_element_type=F32)
        grad_queries = jnp.dot(keys.T, grad_scores, preferred_element_type=F32)
        out_ref[here, span] = (join_pair(grad_queries) * factor).astype(out_ref.dtype)

    @pl.when(step == pl.num_programs(0) - 1)
    def _():
        out_ref[:, columns : 2 * columns] = key_total[...].astype(out_ref.dtype)
        out_ref[:, 2 * columns : 3 * columns] = value_total[...].astype(out_ref.dtype)
        out_ref[:, 3 * columns :] = jnp.zeros(
            (out_ref.shape[0], out_ref.shape[1] - 3 * columns), out_ref.dtype
        )


def attend_backward(packed, log_sums, grad_mixed, rows):
    length, stored = packed.shape
    columns = grad_mixed.shape[1]
    pairs = columns // 128
    tile = min(256, length)
    steps = length // tile
    return pl.pallas_call(
        attend_back_kernel,
        grid=(steps,),
        in_specs=[
            pl.BlockSpec((length, stored), lambda t: (0, 0)),
            pl.BlockSpec((tile, columns), lambda t: (t, 0)),
            pl.BlockSpec((pairs, 1, 1, 2 * tile), lambda t: (0, t, 0, 0)),
        ]
        + row_specs(length, tile),
        out_specs=pl.BlockSpec((length, stored), lambda t: (0, 0)),
        out_shape=jax.ShapeDtypeStruct((length, stored), BF16),
        scratch_shapes=[pltpu.VMEM((length, columns), F32)] * 2,
        compiler_params=pltpu.CompilerParams(vmem_limit_bytes=48 * 1024 * 1024),
        cost_estimate=pl.CostEstimate(
            flops=10 * length * length * columns,
            bytes_accessed=4 * length * stored,
            transcendentals=length * length * pairs * 2,
        ),
    )(packed, grad_mixed, log_sums, *both_ways(rows))


def forward_attention(residual, w_attn, gain_rows, rows):
    columns = w_attn.shape[1] // 4
    normed = norm_rows(residual, gain_rows[0], gain_rows[1])
    first_full = spread(normed.astype(BF16))
    packed = jnp.dot(first_full, w_attn, preferred_element_type=F32).astype(BF16)
    mixed_rows, log_sums = attend_forward(packed, columns, rows)
    branch = jnp.einsum(
        "tc,dc->td", mixed_rows, w_attn[:, 3 * columns :], preferred_element_type=F32
    )
    return residual + collect(branch), (residual, first_full, packed, log_sums, mixed_rows)


def forward_feed(middle, w_fc, w_proj, gain_rows):
    second = norm_rows(middle, gain_rows[2], gain_rows[3])
    second_full = spread(second.astype(BF16))
    hidden = jnp.dot(second_full, w_fc, preferred_element_type=F32)
    active = gelu_tanh(hidden).astype(BF16)
    branch = jnp.einsum("tf,df->td", active, w_proj, preferred_element_type=F32)
    return middle + collect(branch), (middle, second_full, hidden, active)


def backward_feed(grad_out, saved, w_fc, w_proj, gain_rows):
    middle, second_full, hidden, active = saved
    grad_z = spread(grad_out.astype(BF16))
    grad_active = jnp.dot(grad_z, w_proj, preferred_element_type=F32)
    _, gelu_pull = jax.vjp(gelu_tanh, hidden)
    grad_hidden = gelu_pull(grad_active)[0].astype(BF16)
    grad_second = collect(
        jnp.einsum("tf,df->td", grad_hidden, w_fc, preferred_element_type=F32)
    )
    grad_fc = jnp.einsum("td,tf->df", second_full, grad_hidden, preferred_element_type=F32)
    grad_proj = jnp.einsum("td,tf->df", grad_z, active, preferred_element_type=F32)
    _, norm_pull = jax.vjp(norm_rows, middle, gain_rows[2], gain_rows[3])
    grad_middle, grad_gain, grad_bias = norm_pull(grad_second)
    return (
        grad_middle + grad_out,
        (grad_fc.astype(BF16), grad_proj.astype(BF16)),
        jnp.stack([grad_gain, grad_bias]),
    )


def backward_attention(grad_middle, saved, w_attn, gain_rows, rows):
    residual, first_full, packed, log_sums, mixed_rows = saved
    columns = w_attn.shape[1] // 4
    grad_y = spread(grad_middle.astype(BF16))
    grad_mixed = jnp.dot(
        grad_y, w_attn[:, 3 * columns :], preferred_element_type=F32
    ).astype(BF16)
    grad_packed = attend_backward(packed, log_sums, grad_mixed, rows)
    grad_first = collect(
        jnp.einsum("tc,dc->td", grad_packed, w_attn, preferred_element_type=F32)
    )
    grad_out_w = jnp.einsum("td,tc->dc", grad_y, mixed_rows, preferred_element_type=F32)
    grad_qkv = jnp.einsum(
        "td,tc->dc", first_full, grad_packed[:, : 3 * columns], preferred_element_type=F32
    )
    _, norm_pull = jax.vjp(norm_rows, residual, gain_rows[0], gain_rows[1])
    grad_residual, grad_gain, grad_bias = norm_pull(grad_first)
    return (
        grad_residual + grad_middle,
        jnp.concatenate([grad_qkv, grad_out_w], 1).astype(BF16),
        jnp.stack([grad_gain, grad_bias]),
    )


def block(go, step, *operands):
    shapes = jax.eval_shape(step, *operands)

    def idle(*_):
        return jax.tree.map(lambda leaf: jnp.zeros(leaf.shape, leaf.dtype), shapes)

    return lax.cond(go, step, idle, *operands)


def after(value, *others):
    return lax.optimization_barrier((value, *others))[0]


def together(*values):
    return lax.optimization_barrier(values)


def by_rows(matrix):
    return with_layout_constraint(matrix, Layout((0, 1)))


def exchange_blocks(blocks, axis):
    return [blocks[0]] + [swap(blocks[m], axis, m) for m in range(1, len(blocks))]


def place_columns(blocks, index):
    width = blocks[0].shape[1]
    whole = jnp.zeros((blocks[0].shape[0], width * len(blocks)), blocks[0].dtype)
    for m, block in enumerate(blocks):
        whole = lax.dynamic_update_slice_in_dim(whole, block, (index ^ m) * width, 1)
    return whole


def take_columns(whole, index, count):
    width = whole.shape[1] // count
    return [
        lax.dynamic_slice_in_dim(whole, (index ^ m) * width, width, 1) for m in range(count)
    ]


def row_of(column):
    return jnp.broadcast_to(column, (column.shape[0], 128)).T[:1]


def head_kernel(first_ref, second_ref, table_ref, bias_ref, low_ref, mixed_ref, top_ref, sum_ref):
    table = table_ref[...]
    rows = jnp.where(pl.program_id(0) == 0, first_ref[...], second_ref[...])
    logits = lax.dot_general(
        rows, table, (((1,), (1,)), ((), ())), preferred_element_type=F32
    )
    logits = logits + bias_ref[...]
    row_top = jnp.max(logits, 1, keepdims=True)
    exponent = jnp.exp(logits - row_top)
    top_ref[...] = row_of(row_top)
    sum_ref[...] = row_of(jnp.sum(exponent, 1, keepdims=True))
    low = exponent.astype(BF16)
    low_ref[...] = low
    mixed_ref[...] = jnp.dot(low, table, preferred_element_type=F32).astype(mixed_ref.dtype)


def head_block(first, second, table, bias):
    tile, width = first.shape
    length = 2 * tile
    part_rows = table.shape[0]
    return pl.pallas_call(
        head_kernel,
        grid=(length // tile,),
        in_specs=[
            pl.BlockSpec((tile, width), lambda t: (0, 0), pipeline_mode=pl.Buffered(1)),
            pl.BlockSpec((tile, width), lambda t: (0, 0), pipeline_mode=pl.Buffered(1)),
            pl.BlockSpec((part_rows, width), lambda t: (0, 0), pipeline_mode=pl.Buffered(1)),
            pl.BlockSpec((1, part_rows), lambda t: (0, 0), pipeline_mode=pl.Buffered(1)),
        ],
        out_specs=[
            pl.BlockSpec((tile, part_rows), lambda t: (t, 0)),
            pl.BlockSpec((tile, width), lambda t: (t, 0)),
            pl.BlockSpec((1, tile), lambda t: (0, t)),
            pl.BlockSpec((1, tile), lambda t: (0, t)),
        ],
        out_shape=[
            jax.ShapeDtypeStruct((length, part_rows), BF16),
            jax.ShapeDtypeStruct((length, width), BF16),
            jax.ShapeDtypeStruct((1, length), F32),
            jax.ShapeDtypeStruct((1, length), F32),
        ],
        compiler_params=pltpu.CompilerParams(vmem_limit_bytes=56 * 1024 * 1024),
        cost_estimate=pl.CostEstimate(
            flops=4 * length * part_rows * width,
            bytes_accessed=2 * part_rows * (width + length) + 6 * length * width,
            transcendentals=length * part_rows,
        ),
    )(first, second, table, bias)


def table_kernel(count, *refs):
    low_refs, row_refs, out_ref = refs[:count], refs[count : 3 * count], refs[3 * count]
    half = row_refs[0].shape[0]
    total = None
    for k, row_ref in enumerate(row_refs):
        product = lax.dot_general(
            low_refs[k // 2][k % 2 * half : (k % 2 + 1) * half, :],
            row_ref[...],
            (((0,), (0,)), ((), ())),
            preferred_element_type=F32,
        )
        total = product if total is None else total + product
    out_ref[...] = total.astype(out_ref.dtype)


def table_gradient_of(lows, rows, first, count_tiles, tile):
    count = len(lows)
    length, part_rows = lows[0].shape
    half, width = rows[0].shape
    return pl.pallas_call(
        lambda *refs: table_kernel(count, *refs),
        grid=(count_tiles,),
        in_specs=[pl.BlockSpec((length, tile), lambda v: (0, v + first))] * count
        + [pl.BlockSpec((half, width), lambda v: (0, 0), pipeline_mode=pl.Buffered(1))]
        * (2 * count),
        out_specs=pl.BlockSpec((tile, width), lambda v: (v, 0)),
        out_shape=jax.ShapeDtypeStruct((count_tiles * tile, width), BF16),
        compiler_params=pltpu.CompilerParams(vmem_limit_bytes=60 * 1024 * 1024),
        cost_estimate=pl.CostEstimate(
            flops=2 * count * length * count_tiles * tile * width,
            bytes_accessed=2 * count_tiles * tile * (width + count * length)
            + 2 * count * length * width,
            transcendentals=0,
        ),
    )(*lows, *rows)


def part_place(group, half, part_rows, slice_rows):
    wanted = group * part_rows + half * (part_rows // 2)
    return jnp.minimum(wanted, slice_rows - part_rows // 2), wanted


def scatter_kernel(
    count_ref, list_ref, near_ref, far_ref, own_ref, other_ref, out_ref, square_ref, wide
):
    slice_rows = out_ref.shape[0]
    shift = (slice_rows - 1).bit_length()
    replicas, half_rows = near_ref.shape[:2]
    section, replica = lax.axis_index("pipe"), lax.axis_index("dp")
    out_ref[...] = jnp.zeros_like(out_ref)
    for m in range(replicas):
        for half, part in ((section, near_ref), (1 - section, far_ref)):
            start, _ = part_place(replica ^ m, half, 2 * half_rows, slice_rows)
            out_ref[pl.ds(pl.multiple_of(start, 8), half_rows), :] += part[m].astype(F32)
    count_rows = own_ref.shape[0]
    wide[pl.ds(pl.multiple_of(section * count_rows, 8), count_rows), :] = own_ref[...].astype(F32)
    wide[pl.ds(pl.multiple_of((1 - section) * count_rows, 8), count_rows), :] = other_ref[
        ...
    ].astype(F32)

    def add_one(k):
        coded = list_ref[k]
        here = pl.ds(jnp.bitwise_and(coded, (1 << shift) - 1), 1)
        out_ref[here, :] += wide[pl.ds(lax.shift_right_logical(coded, shift), 1), :]

    def add_some(k, carry):
        for u in range(8):
            add_one(8 * k + u)
        return carry

    def add_last(k, carry):
        add_one(k)
        return carry

    count = count_ref[0]
    groups = lax.shift_right_logical(count, 3)
    lax.fori_loop(0, groups, add_some, 0)
    lax.fori_loop(8 * groups, count, add_last, 0)
    result = out_ref[...]
    square_ref[...] = jnp.sum(result * result, 0, keepdims=True)


def scatter_rows(listing, count, near, far, own, other, slice_rows):
    columns = near.shape[2]
    whole = pl.BlockSpec(memory_space=pltpu.VMEM)
    scalars = pl.BlockSpec(memory_space=pltpu.SMEM)
    return pl.pallas_call(
        scatter_kernel,
        in_specs=[scalars, scalars, whole, whole, whole, whole],
        out_specs=[whole, whole],
        out_shape=[
            jax.ShapeDtypeStruct((slice_rows, columns), F32),
            jax.ShapeDtypeStruct((1, columns), F32),
        ],
        scratch_shapes=[pltpu.VMEM((2 * own.shape[0], columns), F32)],
        compiler_params=pltpu.CompilerParams(vmem_limit_bytes=60 * 1024 * 1024),
        cost_estimate=pl.CostEstimate(
            flops=4 * slice_rows * columns,
            bytes_accessed=8 * slice_rows * columns + 4 * own.size,
            transcendentals=0,
        ),
    )(count, listing, near, far, own, other)


def scatter_over(part, axes):
    return lax.psum_scatter(part, axes, scatter_dimension=0, tiled=True)


def merge_stats(stats):
    both = jnp.stack(stats)
    for axis, place in (("seq", 2), ("dp", 1)):
        size = lax.axis_size(axis)
        found = [both]
        for mask in range(1, size):
            shift = reverse_bits(mask, size) if axis == "seq" else mask
            order = jnp.array([k ^ shift for k in range(size)])
            found.append(jnp.take(swap(both, axis, mask), order, axis=place))
        top = found[0][0]
        for pair in found[1:]:
            top = jnp.maximum(top, pair[0])
        both = jnp.stack([top, sum(pair[1] * jnp.exp(pair[0] - top) for pair in found)])
    return both[0] + jnp.log(both[1])


def adamw_update(master, first, second, gradient, rate, decay):
    first_new = BETA_ONE * first + (1.0 - BETA_ONE) * gradient
    second_new = BETA_TWO * second + (1.0 - BETA_TWO) * gradient * gradient
    ratio = (
        first_new
        / (1.0 - BETA_ONE**STEP)
        / (jnp.sqrt(second_new / (1.0 - BETA_TWO**STEP)) + EPS_ADAM)
    )
    return (master - rate * (ratio + decay * master), first_new, second_new)


def per_device(
    token_ids,
    segments,
    valid,
    attn_qkv,
    attn_qkv_first,
    attn_qkv_second,
    attn_out,
    attn_out_first,
    attn_out_second,
    mlp_in,
    mlp_in_first,
    mlp_in_second,
    mlp_out,
    mlp_out_first,
    mlp_out_second,
    embed_table,
    embed_table_first,
    embed_table_second,
    position_table,
    position_table_first,
    position_table_second,
    norm_params,
    norm_params_first,
    norm_params_second,
    final_norm,
    final_norm_first,
    final_norm_second,
):
    section, replica, lane = lax.axis_index("pipe"), lax.axis_index("dp"), lax.axis_index("seq")
    sections, replicas, lanes = (lax.axis_size(name) for name in ("pipe", "dp", "seq"))
    length = token_ids.shape[1]
    assert sections == 2 and token_ids.shape[0] == sections and attn_qkv.shape[0] == 1
    shard_rows = length // lanes
    slice_rows, slice_columns = embed_table.shape
    width = slice_columns * replicas
    part_rows = -(-slice_rows // (replicas * 128)) * 128
    half_rows = part_rows // 2
    assert part_rows * (replicas - 1) < slice_rows
    lane_order = [reverse_bits(k, lanes) for k in range(lanes)]
    lane_blocks = lane ^ jnp.array(lane_order)

    norm_mine = jnp.concatenate([norm_params.reshape(-1, norm_params.shape[2]), final_norm], 0)
    norm_columns = norm_mine.shape[1]
    norm_all = from_all(from_all(from_all(norm_mine, "pipe"), "dp"), "seq")
    norm_all = jnp.transpose(norm_all, (2, 1, 0, 3, 4)).reshape(-1, *norm_mine.shape)
    own_place = (section * replicas + replica) * lanes + lane
    own_ids = lax.dynamic_index_in_dim(token_ids, section, 0, keepdims=False)
    own_valid = lax.dynamic_index_in_dim(valid, section, 0, keepdims=False)
    row_segments = lax.dynamic_index_in_dim(segments, section, 0, keepdims=False)
    coded = own_ids * 2 + own_valid
    coded_all = jnp.stack([coded] + [swap(coded, "dp", m) for m in range(1, replicas)])
    ids_all = coded_all // 2
    position = jnp.arange(length)
    weight_all = jnp.where(position < length - 1, coded_all % 2, 0).astype(F32)
    targets_all = jnp.roll(ids_all, -1, axis=1)

    def by_lane(values):
        return jnp.take(values.reshape(-1, lanes, shard_rows), lane_blocks, axis=1)

    ids_lane, weight_lane, targets_lane = by_lane(ids_all), by_lane(weight_all), by_lane(targets_all)

    go = lax.optimization_barrier(jnp.int32(1)) > 0
    qkv_columns = attn_qkv.shape[2] * attn_qkv.shape[3]
    attn_columns = qkv_columns + attn_out.shape[1]
    shards = [
        jnp.concatenate([attn_qkv[0].reshape(-1, qkv_columns), attn_out[0].T], 1),
        mlp_in[0],
        mlp_out[0].T,
    ]
    shards = [by_rows(shard.astype(BF16)) for shard in shards]

    def both_layers(mine, other=None):
        if other is None:
            other = swap(mine, "pipe", 1)
        return [jnp.where(section == 0, mine, other), jnp.where(section == 0, other, mine)]

    def over_dp(shard):
        return lax.all_gather(shard, "dp", axis=0, tiled=True)

    attn_mine, fc_mine = over_dp(shards[0]), over_dp(shards[1])
    proj_shards = both_layers(shards[2])

    vocab_start = lane * slice_rows
    wanted = jnp.transpose(ids_lane, (1, 0, 2)).reshape(-1) - vocab_start
    inside = (wanted >= 0) & (wanted < slice_rows)
    picked = jnp.take(embed_table, jnp.clip(wanted, 0, slice_rows - 1), axis=0)
    picked = jnp.where(inside[:, None], picked, 0.0).astype(BF16)
    picked, norm_all, proj_shards, attn_mine = together(
        picked, norm_all, proj_shards, attn_mine
    )
    attn_other = swap(attn_mine, "pipe", 1)
    w_proj = [over_dp(shard) for shard in proj_shards]
    picked = collect(picked).astype(BF16).reshape(replicas, shard_rows, slice_columns)
    norm_all = jnp.transpose(norm_all, (1, 0, 2)).reshape(norm_mine.shape[0], width)
    gain_stack = norm_all[:-2].reshape(norm_params.shape[0], 4, width)
    final_rows = norm_all[-2:]
    embed_blocks, attn_other = together(exchange_blocks(list(picked), "dp"), attn_other)
    w_attn = both_layers(attn_mine, attn_other)
    embed_rows = place_columns(embed_blocks, replica)
    position_low = position_table.astype(BF16)
    position_rows = place_columns(
        exchange_blocks([position_low] * replicas, "dp"), replica
    )
    start_rows = embed_rows.astype(F32) + position_rows.astype(F32)
    next_first = lax.ppermute(embed_rows[:1], "seq", [(k, k - 1) for k in range(1, lanes)])
    target_rows = jnp.concatenate([embed_rows[1:], next_first], 0).astype(F32)

    coded_other = swap(coded_all, "pipe", 1)
    ids_both = jnp.where(
        section == 0,
        jnp.concatenate([ids_all, coded_other // 2], 0),
        jnp.concatenate([coded_other // 2, ids_all], 0),
    )
    back_wanted = by_lane(ids_both).reshape(sections, replicas, lanes, shard_rows)
    back_wanted = jnp.transpose(back_wanted, (0, 2, 1, 3)).reshape(-1) - vocab_start
    back_inside = (back_wanted >= 0) & (back_wanted < slice_rows)
    back_number = jnp.arange(back_wanted.shape[0])
    back_coded = back_number * (1 << (slice_rows - 1).bit_length()) + back_wanted
    back_listing = jnp.sort(jnp.where(back_inside, back_coded, 2**31 - 1))
    back_count = jnp.sum(back_inside.astype(jnp.int32))[None]
    start_rows, back_listing, back_count = together(start_rows, back_listing, back_count)

    start_rows, fc_mine = together(start_rows, fc_mine)
    w_fc = both_layers(fc_mine)

    bias_halves = []
    for half in (section, 1 - section):
        start, wanted = part_place(replica, half, part_rows, slice_rows)
        bias_halves.append(jnp.where(start + jnp.arange(half_rows) >= wanted, 0.0, -1e30))
    table_bias = jnp.concatenate(bias_halves).astype(F32)[None]

    row_place = (lane_blocks[:, None] * shard_rows + jnp.arange(shard_rows)[None, :]).reshape(-1)
    row_document = jnp.take(row_segments.reshape(lanes, shard_rows), lane_blocks, axis=0).reshape(-1)
    places = (row_place, row_document)
    rows = start_rows
    saved = []
    for layer in range(2):
        gains = gain_stack[layer]
        rows, kept_attn = block(go, forward_attention, rows, w_attn[layer], gains, places)
        if layer == 0:
            table_f32 = after(embed_table, rows)
            table_parts = [
                lax.dynamic_slice_in_dim(
                    table_f32,
                    part_place(replica ^ m, section, part_rows, slice_rows)[0],
                    half_rows,
                    0,
                ).astype(BF16)
                for m in range(replicas)
            ]
            rows, *table_parts = together(rows, *table_parts)
            table_blocks = exchange_blocks(table_parts, "dp")
        else:
            rows, w_proj[1] = together(rows, w_proj[1])
            rows, *table_blocks = together(rows, *table_blocks)
            table_half = place_columns(table_blocks, replica)
            table_other = swap(table_half, "pipe", 1)
        rows, kept_feed = block(go, forward_feed, rows, w_fc[layer], w_proj[layer], gains)
        saved.append((kept_attn, kept_feed))
    table = jnp.concatenate([table_half, table_other], 0)
    final_value, final_pull = jax.vjp(norm_rows, rows, final_rows[0], final_rows[1])
    final_low = final_value.astype(BF16)

    parts = exchange_blocks([final_low] * replicas, "dp")
    steps = len(masks_down(lanes)) - 1
    full, heads = [], []
    half = spread(parts[0], steps)

    def head_step(half, table, bias, *coming):
        other = swap(half, "seq", 1)
        outputs = head_block(half, other, table, bias)
        return (half, other), outputs, [spread(part, steps, (outputs[2],)) for part in coming]

    for m in range(replicas):
        rows, head, coming = block(go, head_step, half, table, table_bias, *parts[m + 1 : m + 2])
        full.append(rows)
        heads.append(head)
        half = coming[0] if coming else None
    stat_shape = (replicas, lanes, shard_rows)
    row_top = jnp.stack([head[2] for head in heads]).reshape(stat_shape)
    row_sum = jnp.stack([head[3] for head in heads]).reshape(stat_shape)
    log_total = merge_stats((row_top, row_sum))
    scale = weight_lane * (1.0 + 2.0 * ZLOSS * log_total) * jnp.exp(row_top - log_total)
    own_weight, own_log = weight_lane[0, 0], log_total[0, 0]
    target_logit = jnp.sum(final_low.astype(F32) * target_rows, 1)
    own_penalty = own_weight * ZLOSS * own_log * own_log
    own_loss = own_weight * (own_log - target_logit) + own_penalty

    scale_flat = scale.reshape(replicas, length)
    first_sums = [collect_scaled(heads[m][1], scale_flat[m]) for m in range(replicas)]
    tile = max(t for t in range(128, 641, 128) if part_rows % t == 0)
    first_tiles = half_rows // tile
    lows = [head[0] for head in heads]
    half_length = length // 2
    scaled = [
        after(
            (
                scale_flat[m][k * half_length : (k + 1) * half_length, None]
                * full[m][k].astype(F32)
            ).astype(BF16),
            *first_sums,
        )
        for m in range(replicas)
        for k in range(2)
    ]
    late_tiles = part_rows // tile - first_tiles
    late = block(
        go,
        lambda lows, scaled: table_gradient_of(lows, scaled, first_tiles, late_tiles, tile),
        lows,
        scaled,
    )
    head_parts = [collect_rest(part, late).astype(BF16) for part in first_sums]
    half_sent = late[half_rows - first_tiles * tile :]
    half_sent, *head_parts = together(half_sent, *head_parts)
    half_other = swap(half_sent, "pipe", 1)
    received_parts = exchange_blocks(head_parts, "dp")
    scaled[0] = after(scaled[0], *head_parts)
    early = block(
        go,
        lambda lows, scaled: table_gradient_of(lows, scaled, 0, first_tiles, tile),
        lows,
        scaled,
    )
    half_kept = jnp.concatenate([early, late[: half_rows - first_tiles * tile]], 0)
    head_parts = [received_parts[0]] + [after(part, early) for part in received_parts[1:]]
    grad_final_rows = sum(part.astype(F32) for part in head_parts)
    grad_final_rows = grad_final_rows - own_weight[:, None] * target_rows
    gradient, final_gain_part, final_bias_part = final_pull(grad_final_rows)
    grad_final = jnp.stack([final_gain_part, final_bias_part])

    weighted = own_weight[:, None] * final_low.astype(F32)
    before_first = lax.ppermute(
        weighted[-1:].astype(BF16), "seq", [(k, k + 1) for k in range(lanes - 1)]
    )
    target_part = jnp.concatenate([before_first.astype(F32), weighted[:-1]], 0)

    grad_gains = [None, None]
    moving = [list(range(1, replicas))[: replicas // 2], list(range(1, replicas))[replicas // 2 :]]
    arrived = {}

    def send_some(value, stage):
        value, *sent = together(value, *[half_parts[m] for m in moving[stage]])
        return value, {m: swap(part, "dp", m) for m, part in zip(moving[stage], sent)}

    def column_half(matrix, half):
        columns = matrix.shape[1] // 2
        return lax.dynamic_slice_in_dim(matrix, half * columns, columns, 1)

    def send_halves(value, matrices):
        value, *sent = together(value, *[column_half(part, 1 - section) for part in matrices])
        return value, [swap(part, "pipe", 1) for part in sent]

    def sum_halves(value, matrices, coming):
        sums = [
            (column_half(part, section).astype(F32) + other.astype(F32)).astype(BF16)
            for part, other in zip(matrices, coming)
        ]
        return together(value, *sums)

    gradient, feed_late, gains_feed = block(
        go, backward_feed, gradient, saved[1][1], w_fc[1], w_proj[1], gain_stack[1]
    )
    gradient, half_other, *feed_late = together(gradient, half_other, *feed_late)
    half_sum = (half_kept.astype(F32) + half_other.astype(F32)).astype(BF16)
    half_parts = take_columns(half_sum, replica, replicas)
    gradient, flight = send_some(gradient, 0)
    gradient, coming = send_halves(gradient, feed_late)
    gradient, attn_late, gains_attn = block(
        go, backward_attention, gradient, saved[1][0], w_attn[1], gain_stack[1], places
    )
    grad_gains[1] = jnp.concatenate([gains_attn, gains_feed], 0)
    gradient, flight, coming, attn_late = together(gradient, flight, coming, attn_late)
    arrived.update(flight)
    gradient, flight = send_some(gradient, 1)
    gradient, *sums = sum_halves(gradient, feed_late, coming)
    feed_late = [scatter_over(part, "dp") for part in sums]
    gradient, attn_coming = send_halves(gradient, [attn_late])
    gradient, feed_early, gains_feed = block(
        go, backward_feed, gradient, saved[0][1], w_fc[0], w_proj[0], gain_stack[0]
    )
    gradient, flight, attn_coming, *feed_early = together(
        gradient, flight, attn_coming, *feed_early
    )
    arrived.update(flight)
    half_back = jnp.stack([half_parts[0]] + [arrived[m] for m in range(1, replicas)])
    gradient, half_back = together(gradient, half_back)
    half_far = swap(half_back, "pipe", 1)
    feed_early = [scatter_over(part, "dp") for part in feed_early]
    gradient, attn_late = sum_halves(gradient, [attn_late], attn_coming)
    attn_late = scatter_over(attn_late, "dp")
    gradient, feed_late = together(gradient, feed_late)
    gradient, attn_early, gains_attn = block(
        go, backward_attention, gradient, saved[0][0], w_attn[0], gain_stack[0], places
    )
    grad_gains[0] = jnp.concatenate([gains_attn, gains_feed], 0)
    gradient, attn_coming = send_halves(gradient, [attn_early])
    late_halves = [swap(part, "pipe", 1) for part in feed_late]

    back = exchange_blocks(
        take_columns((gradient - target_part).astype(BF16), replica, replicas), "dp"
    )
    back = jnp.concatenate(back, 0)
    position_sent = gradient.astype(BF16)
    back, attn_coming, half_far, feed_early[0] = together(
        back, attn_coming, half_far, feed_early[0]
    )
    back, attn_early = sum_halves(back, [attn_early], attn_coming)
    attn_early = scatter_over(attn_early, "dp")
    back_other = swap(back, "pipe", 1)
    own_rows = spread(back)
    back_other, feed_early[1], position_sent = together(
        back_other, feed_early[1], position_sent
    )
    position_part = sum(
        part.astype(F32)
        for part in exchange_blocks(take_columns(position_sent, replica, replicas), "dp")
    )
    position_grad = position_part + swap(position_part, "pipe", 1)
    other_rows = spread(back_other)
    table_grad, table_square = scatter_rows(
        back_listing, back_count, half_back, half_far, own_rows, other_rows, slice_rows
    )

    feed_coming = [swap(part, "pipe", 1) for part in feed_early]
    attn_late, attn_early, *feed_coming = together(
        attn_late, attn_early, *feed_coming, table_square
    )[:-1]
    attn_coming = swap(jnp.where(section == 0, attn_late, attn_early), "pipe", 1)
    attn_part = jnp.where(
        section == 0,
        jnp.concatenate([attn_early, attn_coming], 1),
        jnp.concatenate([attn_coming, attn_late], 1),
    ).astype(F32)
    fc_part, proj_part = (
        jnp.where(
            section == 0,
            feed_early[k].astype(F32) + feed_coming[k].astype(F32),
            jnp.concatenate([late_halves[k], feed_late[k]], 1).astype(F32),
        )
        for k in range(2)
    )
    qkv_grad = attn_part[:, :qkv_columns].reshape(attn_qkv.shape)
    out_grad = by_rows(attn_part[:, qkv_columns:].T)[None]
    fc_grad = by_rows(fc_part)[None]
    proj_grad = by_rows(proj_part.T)[None]

    norm_grad_all = jnp.concatenate([grad_gains[0], grad_gains[1], grad_final], 0)
    squares = (
        jnp.sum(qkv_grad * qkv_grad)
        + jnp.sum(out_grad * out_grad)
        + jnp.sum(fc_grad * fc_grad)
        + jnp.sum(proj_grad * proj_grad)
        + (jnp.sum(table_square) + jnp.sum(position_grad * position_grad)) / sections
    )
    sums = jnp.stack([squares, jnp.sum(own_loss), jnp.sum(own_penalty), jnp.sum(own_weight)])
    sums = jnp.pad(sums, (0, width - sums.shape[0]))[None]
    summed = sum_everywhere(jnp.concatenate([norm_grad_all, sums], 0))
    norm_grad_all, sums = summed[:-1], summed[-1]
    norm_grad_mine = lax.dynamic_slice_in_dim(
        norm_grad_all, own_place * norm_columns, norm_columns, 1
    )
    gradients = (
        qkv_grad,
        out_grad,
        fc_grad,
        proj_grad,
        table_grad,
        position_grad,
        norm_grad_mine[:-2].reshape(norm_params.shape),
        norm_grad_mine[-2:],
    )
    squares = sums[0] + jnp.sum(norm_grad_all * norm_grad_all)
    loss_sum, penalty_sum, token_count = sums[1], sums[2], sums[3]
    grad_norm = jnp.sqrt(squares) / token_count
    clip_factor = jnp.minimum(1.0, CLIP / (grad_norm + 1e-06))
    step_scale = clip_factor / token_count
    masters = (
        attn_qkv,
        attn_out,
        mlp_in,
        mlp_out,
        embed_table,
        position_table,
        norm_params,
        final_norm,
    )
    moments = (
        (attn_qkv_first, attn_qkv_second),
        (attn_out_first, attn_out_second),
        (mlp_in_first, mlp_in_second),
        (mlp_out_first, mlp_out_second),
        (embed_table_first, embed_table_second),
        (position_table_first, position_table_second),
        (norm_params_first, norm_params_second),
        (final_norm_first, final_norm_second),
    )
    results = []
    for index in range(8):
        results.extend(
            adamw_update(
                masters[index],
                moments[index][0],
                moments[index][1],
                gradients[index] * step_scale,
                RATES[index],
                DECAYS[index],
            )
        )
    loss_parts = jnp.stack([loss_sum, token_count])
    return (loss_parts, penalty_sum, grad_norm, *results)


def solution(mesh):
    row_spec = P("dp", None)
    qkv_spec = P("pipe", "dp", None, "seq")
    into_spec = P("pipe", "dp", "seq")
    out_spec = P("pipe", "seq", "dp")
    table_spec = P("seq", "dp")
    norm_spec = P(None, None, ("pipe", "dp", "seq"))
    final_spec = P(None, ("pipe", "dp", "seq"))
    kinds = (
        qkv_spec,
        out_spec,
        into_spec,
        out_spec,
        table_spec,
        table_spec,
        norm_spec,
        final_spec,
    )
    triples = tuple(spec for spec in kinds for _ in range(3))
    return jax.shard_map(
        per_device,
        mesh=mesh,
        in_specs=(row_spec, row_spec, row_spec) + triples,
        out_specs=(P(), P(), P()) + triples,
        check_vma=False,
    )
```

```python
import jax
import jax.numpy as jnp
from jax import lax
from jax.experimental import pallas as pl
from jax.experimental.layout import Layout, with_layout_constraint
from jax.experimental.pallas import tpu as pltpu
from jax.sharding import PartitionSpec as P

HEAD = 64
STEP = 10


EPS_NORM = 1e-05
ZLOSS = 0.001
CLIP = 0.01
BETA_ONE = 0.9
BETA_TWO = 0.95
EPS_ADAM = 1e-08
RATES = (0.03, 0.1, 0.03, 0.015, 0.05, 0.15, 0.7, 0.7)
DECAYS = (0.1, 0.1, 0.1, 0.1, 0.1, 0.0, 0.0, 0.0)
F32 = jnp.float32
BF16 = jnp.bfloat16


def swap(block, axis, mask):
    route = [(i, i ^ mask) for i in range(lax.axis_size(axis))]
    return lax.ppermute(block, axis, route)


def masks_down(size):
    found = []
    mask = size // 2
    while mask >= 1:
        found.append(mask)
        mask //= 2
    return found


def reverse_bits(value, size):
    result = 0
    mask = 1
    while mask < size:
        result = result * 2 + (value & mask) // mask
        mask *= 2
    return result


def spread(block, steps=None, held=()):
    for mask in masks_down(lax.axis_size("seq"))[:steps]:
        received = swap(block, "seq", mask)
        if held:
            received = after(received, *held)
        block = jnp.concatenate([block, received], 0)
    return block


def collect(block):
    for mask in reversed(masks_down(lax.axis_size("seq"))):
        half = block.shape[0] // 2
        sent = swap(block[half:].astype(BF16), "seq", mask)
        block = block[:half].astype(F32) + sent.astype(F32)
    return block


def collect_scaled(block, scale):
    half = block.shape[0] // 2
    mask = masks_down(lax.axis_size("seq"))[-1]
    sent = swap((block[half:].astype(F32) * scale[half:, None]).astype(BF16), "seq", mask)
    return block[:half].astype(F32) * scale[:half, None] + sent.astype(F32)


def collect_rest(block, held):
    for mask in reversed(masks_down(lax.axis_size("seq"))[:-1]):
        half = block.shape[0] // 2
        sent = after(swap(block[half:].astype(BF16), "seq", mask), held)
        block = block[:half] + sent.astype(F32)
    return block


def from_all(block, axis):
    names = axis if isinstance(axis, tuple) else (axis,)
    size = 1
    for name in names:
        size *= lax.axis_size(name)
    routes = [[(i, i ^ mask) for i in range(size)] for mask in range(1, size)]
    found = jnp.stack([block] + [lax.ppermute(block, axis, route) for route in routes])
    return jnp.take(found, lax.axis_index(axis) ^ jnp.arange(size), axis=0)


def sum_everywhere(block):
    for axis in ("seq", ("pipe", "dp")):
        block = jnp.sum(from_all(block, axis), 0)
    return block


def norm_rows(values, gain, bias):
    center = values - jnp.mean(values, -1, keepdims=True)
    spread_sq = jnp.mean(center * center, -1, keepdims=True)
    return center * lax.rsqrt(spread_sq + EPS_NORM) * gain + bias


def gelu_tanh(values):
    return jax.nn.gelu(values, approximate=True)


def head_pairs(values):
    tile, columns = values.shape
    place = lax.broadcasted_iota(jnp.int32, (tile, columns), 1)
    wide = values.astype(F32)
    return jnp.concatenate(
        [jnp.where(place < HEAD, wide, 0.0), jnp.where(place < HEAD, 0.0, wide)], 0
    )


def join_pair(values):
    columns, double = values.shape
    tile = double // 2
    place = lax.broadcasted_iota(jnp.int32, (columns, tile), 0)
    return jnp.where(place < HEAD, values[:, :tile], values[:, tile:]).T


def pair_allowed(place_row, document_row, place_column, document_column):
    allowed = (place_column[...] <= place_row[...]) & (document_column[...] == document_row[...])
    return jnp.concatenate([allowed, allowed], 1)


def across(left, right):
    return lax.dot_general(left, right, (((1,), (1,)), ((), ())), preferred_element_type=F32)


def attend_kernel(
    packed_ref, place_row, document_row, place_column, document_column, out_ref, log_ref
):
    tile, columns = out_ref.shape
    here = pl.ds(pl.multiple_of(pl.program_id(0) * tile, tile), tile)
    allowed = pair_allowed(place_row, document_row, place_column, document_column)
    for pair in range(columns // 128):
        span = slice(pair * 128, pair * 128 + 128)
        key_span = slice(columns + pair * 128, columns + pair * 128 + 128)
        value_span = slice(2 * columns + pair * 128, 2 * columns + pair * 128 + 128)
        queries = (head_pairs(packed_ref[here, span]) * HEAD ** (-0.5)).astype(BF16)
        scores = jnp.where(allowed, across(packed_ref[:, key_span], queries), -1e30)
        top = jnp.max(scores, 0, keepdims=True)
        exponent = jnp.exp(scores - top)
        total = jnp.sum(exponent, 0, keepdims=True)
        log_ref[pair, 0] = top + jnp.log(total)
        mixed = jnp.dot(
            packed_ref[:, value_span].T, exponent.astype(BF16), preferred_element_type=F32
        )
        out_ref[:, span] = join_pair(mixed / total).astype(out_ref.dtype)


def row_specs(length, tile):
    return [
        pl.BlockSpec((1, tile), lambda t: (0, t)),
        pl.BlockSpec((1, tile), lambda t: (0, t)),
        pl.BlockSpec((length, 1), lambda t: (0, 0)),
        pl.BlockSpec((length, 1), lambda t: (0, 0)),
    ]


def both_ways(rows):
    place, document = rows
    return place[None, :], document[None, :], place[:, None], document[:, None]


def attend_forward(packed, columns, rows):
    length, stored = packed.shape
    pairs = columns // 128
    tile = min(256, length)
    steps = length // tile
    return pl.pallas_call(
        attend_kernel,
        grid=(steps,),
        in_specs=[pl.BlockSpec((length, stored), lambda t: (0, 0))] + row_specs(length, tile),
        out_specs=[
            pl.BlockSpec((tile, columns), lambda t: (t, 0)),
            pl.BlockSpec((pairs, 1, 1, 2 * tile), lambda t: (0, t, 0, 0)),
        ],
        out_shape=[
            jax.ShapeDtypeStruct((length, columns), BF16),
            jax.ShapeDtypeStruct((pairs, steps, 1, 2 * tile), F32),
        ],
        compiler_params=pltpu.CompilerParams(vmem_limit_bytes=48 * 1024 * 1024),
        cost_estimate=pl.CostEstimate(
            flops=4 * length * length * columns,
            bytes_accessed=2 * length * (stored + columns),
            transcendentals=length * length * pairs * 2,
        ),
    )(packed, *both_ways(rows))


def attend_back_kernel(
    packed_ref,
    grad_ref,
    log_ref,
    place_row,
    document_row,
    place_column,
    document_column,
    out_ref,
    key_total,
    value_total,
):
    tile, columns = grad_ref.shape
    step = pl.program_id(0)
    here = pl.ds(pl.multiple_of(step * tile, tile), tile)
    allowed = pair_allowed(place_row, document_row, place_column, document_column)
    factor = HEAD ** (-0.5)

    @pl.when(step == 0)
    def _():
        key_total[...] = jnp.zeros_like(key_total)
        value_total[...] = jnp.zeros_like(value_total)

    for pair in range(columns // 128):
        span = slice(pair * 128, pair * 128 + 128)
        key_span = slice(columns + pair * 128, columns + pair * 128 + 128)
        value_span = slice(2 * columns + pair * 128, 2 * columns + pair * 128 + 128)
        queries = (head_pairs(packed_ref[here, span]) * factor).astype(BF16)
        grads = head_pairs(grad_ref[:, span]).astype(BF16)
        keys = packed_ref[:, key_span]
        scores = jnp.where(allowed, across(keys, queries), -1e30)
        probabilities = jnp.exp(scores - log_ref[pair, 0])
        value_total[:, span] += jnp.dot(
            probabilities.astype(BF16), grads, preferred_element_type=F32
        )
        grad_soft = across(packed_ref[:, value_span], grads)
        mean = jnp.sum(probabilities * grad_soft, 0, keepdims=True)
        grad_scores = (probabilities * (grad_soft - mean)).astype(BF16)
        key_total[:, span] += jnp.dot(grad_scores, queries, preferred_element_type=F32)
        grad_queries = jnp.dot(keys.T, grad_scores, preferred_element_type=F32)
        out_ref[here, span] = (join_pair(grad_queries) * factor).astype(out_ref.dtype)

    @pl.when(step == pl.num_programs(0) - 1)
    def _():
        out_ref[:, columns : 2 * columns] = key_total[...].astype(out_ref.dtype)
        out_ref[:, 2 * columns : 3 * columns] = value_total[...].astype(out_ref.dtype)
        out_ref[:, 3 * columns :] = jnp.zeros(
            (out_ref.shape[0], out_ref.shape[1] - 3 * columns), out_ref.dtype
        )


def attend_backward(packed, log_sums, grad_mixed, rows):
    length, stored = packed.shape
    columns = grad_mixed.shape[1]
    pairs = columns // 128
    tile = min(256, length)
    steps = length // tile
    return pl.pallas_call(
        attend_back_kernel,
        grid=(steps,),
        in_specs=[
            pl.BlockSpec((length, stored), lambda t: (0, 0)),
            pl.BlockSpec((tile, columns), lambda t: (t, 0)),
            pl.BlockSpec((pairs, 1, 1, 2 * tile), lambda t: (0, t, 0, 0)),
        ]
        + row_specs(length, tile),
        out_specs=pl.BlockSpec((length, stored), lambda t: (0, 0)),
        out_shape=jax.ShapeDtypeStruct((length, stored), BF16),
        scratch_shapes=[pltpu.VMEM((length, columns), F32)] * 2,
        compiler_params=pltpu.CompilerParams(vmem_limit_bytes=48 * 1024 * 1024),
        cost_estimate=pl.CostEstimate(
            flops=10 * length * length * columns,
            bytes_accessed=4 * length * stored,
            transcendentals=length * length * pairs * 2,
        ),
    )(packed, grad_mixed, log_sums, *both_ways(rows))


def forward_attention(residual, w_attn, gain_rows, rows):
    columns = w_attn.shape[1] // 4
    normed = norm_rows(residual, gain_rows[0], gain_rows[1])
    first_full = spread(normed.astype(BF16))
    packed = jnp.dot(first_full, w_attn, preferred_element_type=F32).astype(BF16)
    mixed_rows, log_sums = attend_forward(packed, columns, rows)
    branch = jnp.einsum(
        "tc,dc->td", mixed_rows, w_attn[:, 3 * columns :], preferred_element_type=F32
    )
    return residual + collect(branch), (residual, first_full, packed, log_sums, mixed_rows)


def forward_feed(middle, w_fc, w_proj, gain_rows):
    second = norm_rows(middle, gain_rows[2], gain_rows[3])
    second_full = spread(second.astype(BF16))
    hidden = jnp.dot(second_full, w_fc, preferred_element_type=F32)
    active = gelu_tanh(hidden).astype(BF16)
    branch = jnp.einsum("tf,df->td", active, w_proj, preferred_element_type=F32)
    return middle + collect(branch), (middle, second_full, hidden, active)


def backward_feed(grad_out, saved, w_fc, w_proj, gain_rows):
    middle, second_full, hidden, active = saved
    grad_z = spread(grad_out.astype(BF16))
    grad_active = jnp.dot(grad_z, w_proj, preferred_element_type=F32)
    _, gelu_pull = jax.vjp(gelu_tanh, hidden)
    grad_hidden = gelu_pull(grad_active)[0].astype(BF16)
    grad_second = collect(
        jnp.einsum("tf,df->td", grad_hidden, w_fc, preferred_element_type=F32)
    )
    grad_fc = jnp.einsum("td,tf->df", second_full, grad_hidden, preferred_element_type=F32)
    grad_proj = jnp.einsum("td,tf->df", grad_z, active, preferred_element_type=F32)
    _, norm_pull = jax.vjp(norm_rows, middle, gain_rows[2], gain_rows[3])
    grad_middle, grad_gain, grad_bias = norm_pull(grad_second)
    return (
        grad_middle + grad_out,
        (grad_fc.astype(BF16), grad_proj.astype(BF16)),
        jnp.stack([grad_gain, grad_bias]),
    )


def backward_attention(grad_middle, saved, w_attn, gain_rows, rows):
    residual, first_full, packed, log_sums, mixed_rows = saved
    columns = w_attn.shape[1] // 4
    grad_y = spread(grad_middle.astype(BF16))
    grad_mixed = jnp.dot(
        grad_y, w_attn[:, 3 * columns :], preferred_element_type=F32
    ).astype(BF16)
    grad_packed = attend_backward(packed, log_sums, grad_mixed, rows)
    grad_first = collect(
        jnp.einsum("tc,dc->td", grad_packed, w_attn, preferred_element_type=F32)
    )
    grad_out_w = jnp.einsum("td,tc->dc", grad_y, mixed_rows, preferred_element_type=F32)
    grad_qkv = jnp.einsum(
        "td,tc->dc", first_full, grad_packed[:, : 3 * columns], preferred_element_type=F32
    )
    _, norm_pull = jax.vjp(norm_rows, residual, gain_rows[0], gain_rows[1])
    grad_residual, grad_gain, grad_bias = norm_pull(grad_first)
    return (
        grad_residual + grad_middle,
        jnp.concatenate([grad_qkv, grad_out_w], 1).astype(BF16),
        jnp.stack([grad_gain, grad_bias]),
    )


def block(go, step, *operands):
    shapes = jax.eval_shape(step, *operands)

    def idle(*_):
        return jax.tree.map(lambda leaf: jnp.zeros(leaf.shape, leaf.dtype), shapes)

    return lax.cond(go, step, idle, *operands)


def after(value, *others):
    return lax.optimization_barrier((value, *others))[0]


def together(*values):
    return lax.optimization_barrier(values)


def by_rows(matrix):
    return with_layout_constraint(matrix, Layout((0, 1)))


def exchange_blocks(blocks, axis):
    return [blocks[0]] + [swap(blocks[m], axis, m) for m in range(1, len(blocks))]


def place_columns(blocks, index):
    width = blocks[0].shape[1]
    whole = jnp.zeros((blocks[0].shape[0], width * len(blocks)), blocks[0].dtype)
    for m, block in enumerate(blocks):
        whole = lax.dynamic_update_slice_in_dim(whole, block, (index ^ m) * width, 1)
    return whole


def take_columns(whole, index, count):
    width = whole.shape[1] // count
    return [
        lax.dynamic_slice_in_dim(whole, (index ^ m) * width, width, 1) for m in range(count)
    ]


def row_of(column):
    return jnp.broadcast_to(column, (column.shape[0], 128)).T[:1]


def head_kernel(first_ref, second_ref, table_ref, bias_ref, low_ref, mixed_ref, top_ref, sum_ref):
    table = table_ref[...]
    rows = jnp.where(pl.program_id(0) == 0, first_ref[...], second_ref[...])
    logits = lax.dot_general(
        rows, table, (((1,), (1,)), ((), ())), preferred_element_type=F32
    )
    logits = logits + bias_ref[...]
    row_top = jnp.max(logits, 1, keepdims=True)
    exponent = jnp.exp(logits - row_top)
    top_ref[...] = row_of(row_top)
    sum_ref[...] = row_of(jnp.sum(exponent, 1, keepdims=True))
    low = exponent.astype(BF16)
    low_ref[...] = low
    mixed_ref[...] = jnp.dot(low, table, preferred_element_type=F32).astype(mixed_ref.dtype)


def head_block(first, second, table, bias):
    tile, width = first.shape
    length = 2 * tile
    part_rows = table.shape[0]
    return pl.pallas_call(
        head_kernel,
        grid=(length // tile,),
        in_specs=[
            pl.BlockSpec((tile, width), lambda t: (0, 0), pipeline_mode=pl.Buffered(1)),
            pl.BlockSpec((tile, width), lambda t: (0, 0), pipeline_mode=pl.Buffered(1)),
            pl.BlockSpec((part_rows, width), lambda t: (0, 0), pipeline_mode=pl.Buffered(1)),
            pl.BlockSpec((1, part_rows), lambda t: (0, 0), pipeline_mode=pl.Buffered(1)),
        ],
        out_specs=[
            pl.BlockSpec((tile, part_rows), lambda t: (t, 0)),
            pl.BlockSpec((tile, width), lambda t: (t, 0)),
            pl.BlockSpec((1, tile), lambda t: (0, t)),
            pl.BlockSpec((1, tile), lambda t: (0, t)),
        ],
        out_shape=[
            jax.ShapeDtypeStruct((length, part_rows), BF16),
            jax.ShapeDtypeStruct((length, width), BF16),
            jax.ShapeDtypeStruct((1, length), F32),
            jax.ShapeDtypeStruct((1, length), F32),
        ],
        compiler_params=pltpu.CompilerParams(vmem_limit_bytes=56 * 1024 * 1024),
        cost_estimate=pl.CostEstimate(
            flops=4 * length * part_rows * width,
            bytes_accessed=2 * part_rows * (width + length) + 6 * length * width,
            transcendentals=length * part_rows,
        ),
    )(first, second, table, bias)


def table_kernel(count, *refs):
    low_refs, row_refs, out_ref = refs[:count], refs[count : 3 * count], refs[3 * count]
    half = row_refs[0].shape[0]
    total = None
    for k, row_ref in enumerate(row_refs):
        product = lax.dot_general(
            low_refs[k // 2][k % 2 * half : (k % 2 + 1) * half, :],
            row_ref[...],
            (((0,), (0,)), ((), ())),
            preferred_element_type=F32,
        )
        total = product if total is None else total + product
    out_ref[...] = total.astype(out_ref.dtype)


def table_gradient_of(lows, rows, first, count_tiles, tile):
    count = len(lows)
    length, part_rows = lows[0].shape
    half, width = rows[0].shape
    return pl.pallas_call(
        lambda *refs: table_kernel(count, *refs),
        grid=(count_tiles,),
        in_specs=[pl.BlockSpec((length, tile), lambda v: (0, v + first))] * count
        + [pl.BlockSpec((half, width), lambda v: (0, 0), pipeline_mode=pl.Buffered(1))]
        * (2 * count),
        out_specs=pl.BlockSpec((tile, width), lambda v: (v, 0)),
        out_shape=jax.ShapeDtypeStruct((count_tiles * tile, width), BF16),
        compiler_params=pltpu.CompilerParams(vmem_limit_bytes=60 * 1024 * 1024),
        cost_estimate=pl.CostEstimate(
            flops=2 * count * length * count_tiles * tile * width,
            bytes_accessed=2 * count_tiles * tile * (width + count * length)
            + 2 * count * length * width,
            transcendentals=0,
        ),
    )(*lows, *rows)


def part_place(group, half, part_rows, slice_rows):
    wanted = group * part_rows + half * (part_rows // 2)
    return jnp.minimum(wanted, slice_rows - part_rows // 2), wanted


def scatter_kernel(
    count_ref, list_ref, near_ref, far_ref, own_ref, other_ref, out_ref, square_ref, wide
):
    slice_rows = out_ref.shape[0]
    shift = (slice_rows - 1).bit_length()
    replicas, half_rows = near_ref.shape[:2]
    section, replica = lax.axis_index("pipe"), lax.axis_index("dp")
    out_ref[...] = jnp.zeros_like(out_ref)
    for m in range(replicas):
        for half, part in ((section, near_ref), (1 - section, far_ref)):
            start, _ = part_place(replica ^ m, half, 2 * half_rows, slice_rows)
            out_ref[pl.ds(pl.multiple_of(start, 8), half_rows), :] += part[m].astype(F32)
    count_rows = own_ref.shape[0]
    wide[pl.ds(pl.multiple_of(section * count_rows, 8), count_rows), :] = own_ref[...].astype(F32)
    wide[pl.ds(pl.multiple_of((1 - section) * count_rows, 8), count_rows), :] = other_ref[
        ...
    ].astype(F32)

    def add_one(k):
        coded = list_ref[k]
        here = pl.ds(jnp.bitwise_and(coded, (1 << shift) - 1), 1)
        out_ref[here, :] += wide[pl.ds(lax.shift_right_logical(coded, shift), 1), :]

    def add_some(k, carry):
        for u in range(8):
            add_one(8 * k + u)
        return carry

    def add_last(k, carry):
        add_one(k)
        return carry

    count = count_ref[0]
    groups = lax.shift_right_logical(count, 3)
    lax.fori_loop(0, groups, add_some, 0)
    lax.fori_loop(8 * groups, count, add_last, 0)
    result = out_ref[...]
    square_ref[...] = jnp.sum(result * result, 0, keepdims=True)


def scatter_rows(listing, count, near, far, own, other, slice_rows):
    columns = near.shape[2]
    whole = pl.BlockSpec(memory_space=pltpu.VMEM)
    scalars = pl.BlockSpec(memory_space=pltpu.SMEM)
    return pl.pallas_call(
        scatter_kernel,
        in_specs=[scalars, scalars, whole, whole, whole, whole],
        out_specs=[whole, whole],
        out_shape=[
            jax.ShapeDtypeStruct((slice_rows, columns), F32),
            jax.ShapeDtypeStruct((1, columns), F32),
        ],
        scratch_shapes=[pltpu.VMEM((2 * own.shape[0], columns), F32)],
        compiler_params=pltpu.CompilerParams(vmem_limit_bytes=60 * 1024 * 1024),
        cost_estimate=pl.CostEstimate(
            flops=4 * slice_rows * columns,
            bytes_accessed=8 * slice_rows * columns + 4 * own.size,
            transcendentals=0,
        ),
    )(count, listing, near, far, own, other)


def scatter_over(part, axes):
    return lax.psum_scatter(part, axes, scatter_dimension=0, tiled=True)


def merge_stats(stats):
    both = jnp.stack(stats)
    for axis, place in (("seq", 2), ("dp", 1)):
        size = lax.axis_size(axis)
        found = [both]
        for mask in range(1, size):
            shift = reverse_bits(mask, size) if axis == "seq" else mask
            order = jnp.array([k ^ shift for k in range(size)])
            found.append(jnp.take(swap(both, axis, mask), order, axis=place))
        top = found[0][0]
        for pair in found[1:]:
            top = jnp.maximum(top, pair[0])
        both = jnp.stack([top, sum(pair[1] * jnp.exp(pair[0] - top) for pair in found)])
    return both[0] + jnp.log(both[1])


def adamw_update(master, first, second, gradient, rate, decay):
    first_new = BETA_ONE * first + (1.0 - BETA_ONE) * gradient
    second_new = BETA_TWO * second + (1.0 - BETA_TWO) * gradient * gradient
    ratio = (
        first_new
        / (1.0 - BETA_ONE**STEP)
        / (jnp.sqrt(second_new / (1.0 - BETA_TWO**STEP)) + EPS_ADAM)
    )
    return (master - rate * (ratio + decay * master), first_new, second_new)


def per_device(
    token_ids,
    segments,
    valid,
    attn_qkv,
    attn_qkv_first,
    attn_qkv_second,
    attn_out,
    attn_out_first,
    attn_out_second,
    mlp_in,
    mlp_in_first,
    mlp_in_second,
    mlp_out,
    mlp_out_first,
    mlp_out_second,
    embed_table,
    embed_table_first,
    embed_table_second,
    position_table,
    position_table_first,
    position_table_second,
    norm_params,
    norm_params_first,
    norm_params_second,
    final_norm,
    final_norm_first,
    final_norm_second,
):
    section, replica, lane = lax.axis_index("pipe"), lax.axis_index("dp"), lax.axis_index("seq")
    sections, replicas, lanes = (lax.axis_size(name) for name in ("pipe", "dp", "seq"))
    length = token_ids.shape[1]
    assert sections == 2 and token_ids.shape[0] == sections and attn_qkv.shape[0] == 1
    shard_rows = length // lanes
    slice_rows, slice_columns = embed_table.shape
    width = slice_columns * replicas
    part_rows = -(-slice_rows // (replicas * 128)) * 128
    half_rows = part_rows // 2
    assert part_rows * (replicas - 1) < slice_rows
    lane_order = [reverse_bits(k, lanes) for k in range(lanes)]
    lane_blocks = lane ^ jnp.array(lane_order)

    norm_mine = jnp.concatenate([norm_params.reshape(-1, norm_params.shape[2]), final_norm], 0)
    norm_columns = norm_mine.shape[1]
    norm_all = from_all(from_all(from_all(norm_mine, "pipe"), "dp"), "seq")
    norm_all = jnp.transpose(norm_all, (2, 1, 0, 3, 4)).reshape(-1, *norm_mine.shape)
    own_place = (section * replicas + replica) * lanes + lane
    own_ids = lax.dynamic_index_in_dim(token_ids, section, 0, keepdims=False)
    own_valid = lax.dynamic_index_in_dim(valid, section, 0, keepdims=False)
    row_segments = lax.dynamic_index_in_dim(segments, section, 0, keepdims=False)
    coded = own_ids * 2 + own_valid
    coded_all = jnp.stack([coded] + [swap(coded, "dp", m) for m in range(1, replicas)])
    ids_all = coded_all // 2
    position = jnp.arange(length)
    weight_all = jnp.where(position < length - 1, coded_all % 2, 0).astype(F32)
    targets_all = jnp.roll(ids_all, -1, axis=1)

    def by_lane(values):
        return jnp.take(values.reshape(-1, lanes, shard_rows), lane_blocks, axis=1)

    ids_lane, weight_lane, targets_lane = by_lane(ids_all), by_lane(weight_all), by_lane(targets_all)

    go = lax.optimization_barrier(jnp.int32(1)) > 0
    qkv_columns = attn_qkv.shape[2] * attn_qkv.shape[3]
    attn_columns = qkv_columns + attn_out.shape[1]
    shards = [
        jnp.concatenate([attn_qkv[0].reshape(-1, qkv_columns), attn_out[0].T], 1),
        mlp_in[0],
        mlp_out[0].T,
    ]
    shards = [by_rows(shard.astype(BF16)) for shard in shards]

    def both_layers(mine, other=None):
        if other is None:
            other = swap(mine, "pipe", 1)
        return [jnp.where(section == 0, mine, other), jnp.where(section == 0, other, mine)]

    def over_dp(shard):
        return lax.all_gather(shard, "dp", axis=0, tiled=True)

    attn_mine, fc_mine = over_dp(shards[0]), over_dp(shards[1])
    proj_shards = both_layers(shards[2])

    vocab_start = lane * slice_rows
    wanted = jnp.transpose(ids_lane, (1, 0, 2)).reshape(-1) - vocab_start
    inside = (wanted >= 0) & (wanted < slice_rows)
    picked = jnp.take(embed_table, jnp.clip(wanted, 0, slice_rows - 1), axis=0)
    picked = jnp.where(inside[:, None], picked, 0.0).astype(BF16)
    picked, norm_all, proj_shards, attn_mine = together(
        picked, norm_all, proj_shards, attn_mine
    )
    attn_other = swap(attn_mine, "pipe", 1)
    w_proj = [over_dp(shard) for shard in proj_shards]
    picked = collect(picked).astype(BF16).reshape(replicas, shard_rows, slice_columns)
    norm_all = jnp.transpose(norm_all, (1, 0, 2)).reshape(norm_mine.shape[0], width)
    gain_stack = norm_all[:-2].reshape(norm_params.shape[0], 4, width)
    final_rows = norm_all[-2:]
    embed_blocks, attn_other = together(exchange_blocks(list(picked), "dp"), attn_other)
    w_attn = both_layers(attn_mine, attn_other)
    embed_rows = place_columns(embed_blocks, replica)
    position_low = position_table.astype(BF16)
    position_rows = place_columns(
        exchange_blocks([position_low] * replicas, "dp"), replica
    )
    start_rows = embed_rows.astype(F32) + position_rows.astype(F32)
    next_first = lax.ppermute(embed_rows[:1], "seq", [(k, k - 1) for k in range(1, lanes)])
    target_rows = jnp.concatenate([embed_rows[1:], next_first], 0).astype(F32)

    coded_other = swap(coded_all, "pipe", 1)
    ids_both = jnp.where(
        section == 0,
        jnp.concatenate([ids_all, coded_other // 2], 0),
        jnp.concatenate([coded_other // 2, ids_all], 0),
    )
    back_wanted = by_lane(ids_both).reshape(sections, replicas, lanes, shard_rows)
    back_wanted = jnp.transpose(back_wanted, (0, 2, 1, 3)).reshape(-1) - vocab_start
    back_inside = (back_wanted >= 0) & (back_wanted < slice_rows)
    back_number = jnp.arange(back_wanted.shape[0])
    back_coded = back_number * (1 << (slice_rows - 1).bit_length()) + back_wanted
    back_listing = jnp.sort(jnp.where(back_inside, back_coded, 2**31 - 1))
    back_count = jnp.sum(back_inside.astype(jnp.int32))[None]
    start_rows, back_listing, back_count = together(start_rows, back_listing, back_count)

    start_rows, fc_mine = together(start_rows, fc_mine)
    w_fc = both_layers(fc_mine)

    bias_halves = []
    for half in (section, 1 - section):
        start, wanted = part_place(replica, half, part_rows, slice_rows)
        bias_halves.append(jnp.where(start + jnp.arange(half_rows) >= wanted, 0.0, -1e30))
    table_bias = jnp.concatenate(bias_halves).astype(F32)[None]

    row_place = (lane_blocks[:, None] * shard_rows + jnp.arange(shard_rows)[None, :]).reshape(-1)
    row_document = jnp.take(row_segments.reshape(lanes, shard_rows), lane_blocks, axis=0).reshape(-1)
    places = (row_place, row_document)
    rows = start_rows
    saved = []
    for layer in range(2):
        gains = gain_stack[layer]
        rows, kept_attn = block(go, forward_attention, rows, w_attn[layer], gains, places)
        if layer == 0:
            table_f32 = after(embed_table, rows)
            table_parts = [
                lax.dynamic_slice_in_dim(
                    table_f32,
                    part_place(replica ^ m, section, part_rows, slice_rows)[0],
                    half_rows,
                    0,
                ).astype(BF16)
                for m in range(replicas)
            ]
            rows, *table_parts = together(rows, *table_parts)
            table_blocks = exchange_blocks(table_parts, "dp")
        else:
            rows, w_proj[1] = together(rows, w_proj[1])
            rows, *table_blocks = together(rows, *table_blocks)
            table_half = place_columns(table_blocks, replica)
            table_other = swap(table_half, "pipe", 1)
        rows, kept_feed = block(go, forward_feed, rows, w_fc[layer], w_proj[layer], gains)
        saved.append((kept_attn, kept_feed))
    table = jnp.concatenate([table_half, table_other], 0)
    final_value, final_pull = jax.vjp(norm_rows, rows, final_rows[0], final_rows[1])
    final_low = final_value.astype(BF16)

    parts = exchange_blocks([final_low] * replicas, "dp")
    steps = len(masks_down(lanes)) - 1
    full, heads = [], []
    half = spread(parts[0], steps)

    def head_step(half, table, bias, *coming):
        other = swap(half, "seq", 1)
        outputs = head_block(half, other, table, bias)
        return (half, other), outputs, [spread(part, steps, (outputs[2],)) for part in coming]

    for m in range(replicas):
        rows, head, coming = block(go, head_step, half, table, table_bias, *parts[m + 1 : m + 2])
        full.append(rows)
        heads.append(head)
        half = coming[0] if coming else None
    stat_shape = (replicas, lanes, shard_rows)
    row_top = jnp.stack([head[2] for head in heads]).reshape(stat_shape)
    row_sum = jnp.stack([head[3] for head in heads]).reshape(stat_shape)
    log_total = merge_stats((row_top, row_sum))
    scale = weight_lane * (1.0 + 2.0 * ZLOSS * log_total) * jnp.exp(row_top - log_total)
    own_weight, own_log = weight_lane[0, 0], log_total[0, 0]
    target_logit = jnp.sum(final_low.astype(F32) * target_rows, 1)
    own_penalty = own_weight * ZLOSS * own_log * own_log
    own_loss = own_weight * (own_log - target_logit) + own_penalty

    scale_flat = scale.reshape(replicas, length)
    first_sums = [collect_scaled(heads[m][1], scale_flat[m]) for m in range(replicas)]
    tile = max(t for t in range(128, 641, 128) if part_rows % t == 0)
    first_tiles = half_rows // tile
    lows = [head[0] for head in heads]
    half_length = length // 2
    scaled = [
        after(
            (
                scale_flat[m][k * half_length : (k + 1) * half_length, None]
                * full[m][k].astype(F32)
            ).astype(BF16),
            *first_sums,
        )
        for m in range(replicas)
        for k in range(2)
    ]
    late_tiles = part_rows // tile - first_tiles
    late = block(
        go,
        lambda lows, scaled: table_gradient_of(lows, scaled, first_tiles, late_tiles, tile),
        lows,
        scaled,
    )
    head_parts = [collect_rest(part, late).astype(BF16) for part in first_sums]
    half_sent = late[half_rows - first_tiles * tile :]
    half_sent, *head_parts = together(half_sent, *head_parts)
    half_other = swap(half_sent, "pipe", 1)
    received_parts = exchange_blocks(head_parts, "dp")
    scaled[0] = after(scaled[0], *head_parts)
    early = block(
        go,
        lambda lows, scaled: table_gradient_of(lows, scaled, 0, first_tiles, tile),
        lows,
        scaled,
    )
    half_kept = jnp.concatenate([early, late[: half_rows - first_tiles * tile]], 0)
    head_parts = [received_parts[0]] + [after(part, early) for part in received_parts[1:]]
    grad_final_rows = sum(part.astype(F32) for part in head_parts)
    grad_final_rows = grad_final_rows - own_weight[:, None] * target_rows
    gradient, final_gain_part, final_bias_part = final_pull(grad_final_rows)
    grad_final = jnp.stack([final_gain_part, final_bias_part])

    weighted = own_weight[:, None] * final_low.astype(F32)
    before_first = lax.ppermute(
        weighted[-1:].astype(BF16), "seq", [(k, k + 1) for k in range(lanes - 1)]
    )
    target_part = jnp.concatenate([before_first.astype(F32), weighted[:-1]], 0)

    grad_gains = [None, None]
    moving = [list(range(1, replicas))[: replicas // 2], list(range(1, replicas))[replicas // 2 :]]
    arrived = {}

    def send_some(value, stage):
        value, *sent = together(value, *[half_parts[m] for m in moving[stage]])
        return value, {m: swap(part, "dp", m) for m, part in zip(moving[stage], sent)}

    def column_half(matrix, half):
        columns = matrix.shape[1] // 2
        return lax.dynamic_slice_in_dim(matrix, half * columns, columns, 1)

    def send_halves(value, matrices):
        value, *sent = together(value, *[column_half(part, 1 - section) for part in matrices])
        return value, [swap(part, "pipe", 1) for part in sent]

    def sum_halves(value, matrices, coming):
        sums = [
            (column_half(part, section).astype(F32) + other.astype(F32)).astype(BF16)
            for part, other in zip(matrices, coming)
        ]
        return together(value, *sums)

    gradient, feed_late, gains_feed = block(
        go, backward_feed, gradient, saved[1][1], w_fc[1], w_proj[1], gain_stack[1]
    )
    gradient, half_other, *feed_late = together(gradient, half_other, *feed_late)
    half_sum = (half_kept.astype(F32) + half_other.astype(F32)).astype(BF16)
    half_parts = take_columns(half_sum, replica, replicas)
    gradient, flight = send_some(gradient, 0)
    gradient, coming = send_halves(gradient, feed_late)
    gradient, attn_late, gains_attn = block(
        go, backward_attention, gradient, saved[1][0], w_attn[1], gain_stack[1], places
    )
    grad_gains[1] = jnp.concatenate([gains_attn, gains_feed], 0)
    gradient, flight, coming, attn_late = together(gradient, flight, coming, attn_late)
    arrived.update(flight)
    gradient, flight = send_some(gradient, 1)
    gradient, *sums = sum_halves(gradient, feed_late, coming)
    feed_late = [scatter_over(part, "dp") for part in sums]
    gradient, attn_coming = send_halves(gradient, [attn_late])
    gradient, feed_early, gains_feed = block(
        go, backward_feed, gradient, saved[0][1], w_fc[0], w_proj[0], gain_stack[0]
    )
    gradient, flight, attn_coming, *feed_early = together(
        gradient, flight, attn_coming, *feed_early
    )
    arrived.update(flight)
    half_back = jnp.stack([half_parts[0]] + [arrived[m] for m in range(1, replicas)])
    gradient, half_back = together(gradient, half_back)
    half_far = swap(half_back, "pipe", 1)
    feed_early = [scatter_over(part, "dp") for part in feed_early]
    gradient, attn_late = sum_halves(gradient, [attn_late], attn_coming)
    attn_late = scatter_over(attn_late, "dp")
    gradient, feed_late = together(gradient, feed_late)
    gradient, attn_early, gains_attn = block(
        go, backward_attention, gradient, saved[0][0], w_attn[0], gain_stack[0], places
    )
    grad_gains[0] = jnp.concatenate([gains_attn, gains_feed], 0)
    gradient, attn_coming = send_halves(gradient, [attn_early])
    late_halves = [swap(part, "pipe", 1) for part in feed_late]

    back = exchange_blocks(
        take_columns((gradient - target_part).astype(BF16), replica, replicas), "dp"
    )
    back = jnp.concatenate(back, 0)
    position_sent = gradient.astype(BF16)
    back, attn_coming, half_far, feed_early[0] = together(
        back, attn_coming, half_far, feed_early[0]
    )
    back, attn_early = sum_halves(back, [attn_early], attn_coming)
    attn_early = scatter_over(attn_early, "dp")
    back_other = swap(back, "pipe", 1)
    own_rows = spread(back)
    back_other, feed_early[1] = together(back_other, feed_early[1])
    other_rows = spread(back_other)
    position_sent = after(position_sent, other_rows)
    position_parts = exchange_blocks(take_columns(position_sent, replica, replicas), "dp")
    table_grad, table_square = scatter_rows(
        back_listing, back_count, half_back, half_far, own_rows, other_rows, slice_rows
    )

    position_part = sum(
        after(part, table_square).astype(F32) for part in position_parts
    )
    position_grad = position_part + swap(position_part, "pipe", 1)

    feed_coming = [swap(part, "pipe", 1) for part in feed_early]
    attn_late, attn_early, *feed_coming = together(
        attn_late, attn_early, *feed_coming, table_square
    )[:-1]
    attn_coming = swap(jnp.where(section == 0, attn_late, attn_early), "pipe", 1)
    attn_part = jnp.where(
        section == 0,
        jnp.concatenate([attn_early, attn_coming], 1),
        jnp.concatenate([attn_coming, attn_late], 1),
    ).astype(F32)
    fc_part, proj_part = (
        jnp.where(
            section == 0,
            feed_early[k].astype(F32) + feed_coming[k].astype(F32),
            jnp.concatenate([late_halves[k], feed_late[k]], 1).astype(F32),
        )
        for k in range(2)
    )
    qkv_grad = attn_part[:, :qkv_columns].reshape(attn_qkv.shape)
    out_grad = by_rows(attn_part[:, qkv_columns:].T)[None]
    fc_grad = by_rows(fc_part)[None]
    proj_grad = by_rows(proj_part.T)[None]

    norm_grad_all = jnp.concatenate([grad_gains[0], grad_gains[1], grad_final], 0)
    squares = (
        jnp.sum(qkv_grad * qkv_grad)
        + jnp.sum(out_grad * out_grad)
        + jnp.sum(fc_grad * fc_grad)
        + jnp.sum(proj_grad * proj_grad)
        + (jnp.sum(table_square) + jnp.sum(position_grad * position_grad)) / sections
    )
    sums = jnp.stack([squares, jnp.sum(own_loss), jnp.sum(own_penalty), jnp.sum(own_weight)])
    sums = jnp.pad(sums, (0, width - sums.shape[0]))[None]
    summed = sum_everywhere(jnp.concatenate([norm_grad_all, sums], 0))
    norm_grad_all, sums = summed[:-1], summed[-1]
    norm_grad_mine = lax.dynamic_slice_in_dim(
        norm_grad_all, own_place * norm_columns, norm_columns, 1
    )
    gradients = (
        qkv_grad,
        out_grad,
        fc_grad,
        proj_grad,
        table_grad,
        position_grad,
        norm_grad_mine[:-2].reshape(norm_params.shape),
        norm_grad_mine[-2:],
    )
    squares = sums[0] + jnp.sum(norm_grad_all * norm_grad_all)
    loss_sum, penalty_sum, token_count = sums[1], sums[2], sums[3]
    grad_norm = jnp.sqrt(squares) / token_count
    clip_factor = jnp.minimum(1.0, CLIP / (grad_norm + 1e-06))
    step_scale = clip_factor / token_count
    masters = (
        attn_qkv,
        attn_out,
        mlp_in,
        mlp_out,
        embed_table,
        position_table,
        norm_params,
        final_norm,
    )
    moments = (
        (attn_qkv_first, attn_qkv_second),
        (attn_out_first, attn_out_second),
        (mlp_in_first, mlp_in_second),
        (mlp_out_first, mlp_out_second),
        (embed_table_first, embed_table_second),
        (position_table_first, position_table_second),
        (norm_params_first, norm_params_second),
        (final_norm_first, final_norm_second),
    )
    results = []
    for index in range(8):
        results.extend(
            adamw_update(
                masters[index],
                moments[index][0],
                moments[index][1],
                gradients[index] * step_scale,
                RATES[index],
                DECAYS[index],
            )
        )
    loss_parts = jnp.stack([loss_sum, token_count])
    return (loss_parts, penalty_sum, grad_norm, *results)


def solution(mesh):
    row_spec = P("dp", None)
    qkv_spec = P("pipe", "dp", None, "seq")
    into_spec = P("pipe", "dp", "seq")
    out_spec = P("pipe", "seq", "dp")
    table_spec = P("seq", "dp")
    norm_spec = P(None, None, ("pipe", "dp", "seq"))
    final_spec = P(None, ("pipe", "dp", "seq"))
    kinds = (
        qkv_spec,
        out_spec,
        into_spec,
        out_spec,
        table_spec,
        table_spec,
        norm_spec,
        final_spec,
    )
    triples = tuple(spec for spec in kinds for _ in range(3))
    return jax.shard_map(
        per_device,
        mesh=mesh,
        in_specs=(row_spec, row_spec, row_spec) + triples,
        out_specs=(P(), P(), P()) + triples,
        check_vma=False,
    )
```
